128 devices in a mesh: scene: 4 (over x), view: 16 (over y, z), row: 2 (over core).
Axes of the slice: x: 4, y: 4, z: 4, core: 2. Of those that a mesh axis runs over, the one named last changes fastest.
Arguments:
- latents: bfloat16 [4, 64, 2, 32, 1536], P('scene', 'view', 'row'), may hold values from -6 to 6
- norm_gain: float32 [1536], replicated, may hold values from 0.5 to 4
- w_query: bfloat16 [1536, 768], replicated, may hold values from -0.15625 to 0.15625
- w_key: bfloat16 [1536, 768], replicated, may hold values from -0.15625 to 0.15625
- w_value: bfloat16 [1536, 768], replicated, may hold values from -0.15625 to 0.15625
- w_out: bfloat16 [768, 1536], replicated, may hold values from -0.21875 to 0.21875
- kernel: bfloat16 [9, 1536], replicated, may hold values from -4 to 4
- partners: int32 [4, 64, 8], P('scene', 'view'), may hold values from -1 to 63, as said below
- counts: int32 [4, 64], P('scene', 'view'), may hold values from 2 to 8, as said below
- cotangent: bfloat16 [4, 64, 2, 32, 1536], P('scene', 'view', 'row'), may hold values from -1.5 to 1.5
Outputs:
- grad_query: float32 [1536, 768], P(('scene', 'view', 'row'))
- grad_key: float32 [1536, 768], P(('scene', 'view', 'row'))
- grad_value: float32 [1536, 768], P(('scene', 'view', 'row'))
- grad_out: float32 [768, 1536], P(('scene', 'view', 'row'))
The draws below stay inside these ranges and needn't reach their ends.
Inputs may be any that keep to these rules, and one draw needn't show every extreme that they name: Entries j < counts of a view are distinct views held by other groups of 4 views (views 4 * i to 4 * i + 3 form group i); all partners that the views of one group take from another group are one and the same view; entries from counts on are -1. `counts`: the first view of every group has 8 partners.
All inputs are finite; a program needn't handle non-finite values.
Results may differ from the reference program's by a relative error of at most 0.0049.
The reference program's roundings to bfloat16 on the way count: a program that leaves them out, or rounds other values in their place, can miss the bound.
Values may be sent and summed in bfloat16 or wider, within the bound.
A program may use at most 192 MiB of HBM per device.

```python
import jax
import jax.numpy as jnp
from jax import lax

D = 1536
HEADS = 12
HEAD_DIM = 64
W = 32
VIEW_DEV = 4
ROWS_DEV = 1
SCENES = 4
VIEWS = 64
H = 2
MAXP = 8
INNER = 768
N_ROW = 2


def pair_tables(key):
    group_count = VIEWS // VIEW_DEV
    key_local, key_order, key_count = jax.random.split(key, 3)
    chosen = jax.random.randint(key_local, (SCENES, group_count, group_count), 0, VIEW_DEV)
    order_keys = jax.random.split(key_order, SCENES * VIEWS)
    orders = jax.vmap(lambda order_key: jax.random.permutation(order_key, group_count - 1))(order_keys)
    orders = orders.reshape(SCENES, VIEWS, group_count - 1)[:, :, :MAXP]
    home = jnp.arange(VIEWS, dtype=jnp.int32) // VIEW_DEV
    source = (home[None, :, None] + 1 + orders) % group_count
    chosen_rows = jnp.take(chosen, home, axis=1)
    local_view = jnp.take_along_axis(chosen_rows, source, axis=2)
    partner_ids = source * VIEW_DEV + local_view
    drawn = jax.random.randint(key_count, (SCENES, VIEWS), 2, MAXP + 1)
    count_rows = jnp.where((jnp.arange(VIEWS) % VIEW_DEV == 0)[None, :], MAXP, drawn)
    partner_ids = jnp.where(jnp.arange(MAXP)[None, None, :] < count_rows[:, :, None], partner_ids, -1)
    return (partner_ids.astype(jnp.int32), count_rows.astype(jnp.int32))


def draw_partners(key, part):
    return pair_tables(key)[0]


def draw_counts(key, part):
    return pair_tables(key)[1]


def draw_norm_gain(key, part):
    key = jax.random.fold_in(key, 5)
    return jax.random.uniform(key, (D,), jnp.float32, 0.5, 1.5)


def block_levels(own_key, dims, pieces, low, top_value):
    gain, own = 1.0, jax.random.fold_in(own_key, 6)
    for position, parts in pieces:
        steps = jnp.exp(jax.random.uniform(jax.random.fold_in(own, position), (parts,), jnp.float32, low / len(pieces), top_value / len(pieces)))
        gain = gain * jnp.repeat(steps, dims[position] // parts).reshape([-1 if axis == position else 1 for axis in range(len(dims))])
    return gain


def normal_values(rng, dims, scale, most, pieces=(), kind=jnp.bfloat16):
    gain = block_levels(rng, dims, pieces, -0.22, 0.18) if pieces else 1.0
    entries = jax.random.normal(rng, dims, jnp.float32) * scale * gain
    return jnp.minimum(jnp.maximum(entries, -most), most).astype(kind)


def setup_inputs(seed: int = 0) -> dict:
    seeds = jax.random.split(jax.random.key(seed), 11)
    return {
        "latents": normal_values(seeds[0], (SCENES, VIEWS, H, W, D), 1.0, 6.0, ((0, 4), (1, 16), (2, 2))),
        "norm_gain": draw_norm_gain(jax.random.fold_in(seeds[10], 71), 0),
        "w_query": normal_values(seeds[2], (D, INNER), D ** -0.5, 0.15625),
        "w_key": normal_values(seeds[3], (D, INNER), D ** -0.5, 0.15625),
        "w_value": normal_values(seeds[4], (D, INNER), D ** -0.5, 0.15625),
        "w_out": normal_values(seeds[5], (INNER, D), INNER ** -0.5, 0.21875),
        "kernel": normal_values(seeds[6], (9, D), 0.3, 4.0),
        "partners": draw_partners(jax.random.fold_in(seeds[10], 71), 0),
        "counts": draw_counts(jax.random.fold_in(seeds[10], 71), 0),
        "cotangent": normal_values(seeds[9], (SCENES, VIEWS, H, W, D), 0.1, 1.5, ((0, 4), (1, 16), (2, 2))),
    }


epsilon = 1e-06

def rim_conv(padded, kernel, rows, columns):
    result = padded[:, 1:1 + rows, 1:1 + columns].astype(jnp.float32)
    for row_step in range(3):
        for col_step in range(3):
            result = result + kernel[3 * row_step + col_step].astype(jnp.float32) * padded[:, 2 - row_step:2 - row_step + rows, 2 - col_step:2 - col_step + columns].astype(jnp.float32)
    return result.astype(jnp.bfloat16)

def rounded(values):
    return lax.optimization_barrier(values.astype(jnp.bfloat16)).astype(jnp.float32)

def reference(latents, norm_gain, w_query, w_key, w_value, w_out, kernel, partners, counts, cotangent):
    inner_width = HEADS * HEAD_DIM
    scale = HEAD_DIM ** (-0.5)
    view_tokens = H * W
    strip_tokens = ROWS_DEV * W
    block_count = 1 + MAXP
    group_count = VIEWS // VIEW_DEV
    pair_weight = jnp.concatenate((w_key, w_value), axis=1)

    def one_scene(carry, inputs):
        scene_lat, scene_partners, scene_counts, scene_grad = inputs
        lat_f = scene_lat.astype(jnp.float32)
        normed = (lat_f * lax.rsqrt(lax.optimization_barrier(jnp.mean(lat_f * lat_f, -1, keepdims=True)) + epsilon) * norm_gain).astype(jnp.bfloat16)
        flat_rows = normed.reshape(VIEWS * view_tokens, D)
        queries = jnp.dot(flat_rows, w_query, preferred_element_type=jnp.float32).astype(jnp.bfloat16)
        queries = queries.reshape(VIEWS, N_ROW, strip_tokens, HEADS, HEAD_DIM)
        key_value = jnp.dot(flat_rows, pair_weight, preferred_element_type=jnp.float32).astype(jnp.bfloat16)
        key_value = key_value.reshape(VIEWS, view_tokens, 2 * inner_width)
        padded = jnp.pad(scene_grad, ((0, 0), (1, 1), (1, 1), (0, 0)))
        upstream = rim_conv(padded, kernel, H, W)
        up_flat = upstream.reshape(VIEWS * view_tokens, D)
        out_grad = jnp.dot(up_flat, w_out.T, preferred_element_type=jnp.float32).astype(jnp.bfloat16)
        out_grad = out_grad.reshape(VIEWS, N_ROW, strip_tokens, HEADS, HEAD_DIM)

        def view_terms(view_index):
            partner_row = scene_partners[view_index]
            alive_slots = jnp.arange(MAXP, dtype=jnp.int32) < scene_counts[view_index]
            safe_ids = jnp.where(alive_slots, partner_row, 0).astype(jnp.int32)
            block_ids = jnp.concatenate((view_index[None].astype(jnp.int32), safe_ids))
            blocks = key_value[block_ids].reshape(block_count * view_tokens, 2, HEADS, HEAD_DIM).astype(jnp.float32)
            key_rows = blocks[:, 0]
            value_rows = blocks[:, 1]
            key_alive = jnp.repeat(jnp.concatenate((jnp.ones((1,), bool), alive_slots)), view_tokens)
            query_rows = queries[view_index].astype(jnp.float32)
            scores = jnp.einsum('rqhd,khd->rhqk', query_rows, key_rows) * scale
            scores = jnp.where(key_alive, scores, -1e+30)
            highest = lax.optimization_barrier(jnp.max(scores, -1, keepdims=True))
            expo = jnp.exp(scores - highest)
            attention = expo / lax.optimization_barrier(jnp.sum(expo, -1, keepdims=True))
            attention_b = rounded(attention)
            mixed = jnp.einsum('rhqk,khd->rqhd', attention_b, value_rows).astype(jnp.bfloat16).reshape(view_tokens, inner_width)
            grad_rows = out_grad[view_index].astype(jnp.float32)
            dprob = jnp.einsum('rqhd,khd->rhqk', grad_rows, value_rows)
            row_delta = lax.optimization_barrier(jnp.sum(attention * dprob, -1, keepdims=True))
            dscore = rounded(attention * (dprob - row_delta) * scale)
            dquery = jnp.einsum('rhqk,khd->rqhd', dscore, key_rows).astype(jnp.bfloat16).reshape(view_tokens, inner_width)
            dkey = jnp.einsum('rhqk,rqhd->rkhd', dscore, query_rows).reshape(N_ROW, block_count, view_tokens, inner_width)
            dvalue = jnp.einsum('rhqk,rqhd->rkhd', attention_b, grad_rows).reshape(N_ROW, block_count, view_tokens, inner_width)
            return (mixed, dquery, jnp.concatenate((dkey, dvalue), -1), block_ids)

        def group(totals, group_index):
            members = group_index * VIEW_DEV + jnp.arange(VIEW_DEV, dtype=jnp.int32)
            mixed, dquery, dpair, block_ids = jax.vmap(view_terms)(members)
            spread = jnp.moveaxis(dpair, 1, 0).reshape(N_ROW, VIEW_DEV * block_count, view_tokens, 2 * inner_width)
            partial_sum = jnp.zeros((N_ROW, VIEWS, view_tokens, 2 * inner_width), jnp.float32)
            partial_sum = partial_sum.at[:, block_ids.reshape(-1)].add(spread)
            totals = totals + lax.optimization_barrier(jnp.sum(rounded(partial_sum), axis=0))
            return (totals, (mixed, dquery))
        start = jnp.zeros((VIEWS, view_tokens, 2 * inner_width), jnp.float32)
        totals, (mixed, dquery) = lax.scan(group, start, jnp.arange(group_count, dtype=jnp.int32))
        mixed = mixed.reshape(VIEWS * view_tokens, inner_width)
        dquery = dquery.reshape(VIEWS * view_tokens, inner_width)
        dpair = totals.reshape(VIEWS * view_tokens, 2 * inner_width)
        rows_f = flat_rows.astype(jnp.float32)
        grad_query = jnp.dot(flat_rows.T, dquery, preferred_element_type=jnp.float32)
        grad_key = jnp.dot(rows_f.T, dpair[:, :inner_width], precision=lax.Precision.HIGHEST)
        grad_value = jnp.dot(rows_f.T, dpair[:, inner_width:], precision=lax.Precision.HIGHEST)
        grad_out = jnp.dot(mixed.T, up_flat, preferred_element_type=jnp.float32)
        return ((carry[0] + grad_query, carry[1] + grad_key, carry[2] + grad_value, carry[3] + grad_out), None)
    zero_in = jnp.zeros((D, inner_width), jnp.float32)
    zero_out = jnp.zeros((inner_width, D), jnp.float32)
    grads, _ = lax.scan(one_scene, (zero_in, zero_in, zero_in, zero_out), (latents, partners, counts, cotangent))
    return (grads[0], grads[1], grads[2], grads[3])
```

```python
import functools

import jax
import jax.numpy as jnp
from jax import lax
from jax.experimental import pallas as pl
from jax.experimental.pallas import tpu as pltpu
from jax.sharding import PartitionSpec as P

HEAD_DIM = 64
LANES = 128
EPSILON = 1e-06
MESH = pl.DeviceIdType.MESH
VMEM_LIMIT = 60 * 1024 * 1024
NT = (((1,), (1,)), ((), ()))
NN = (((1,), (0,)), ((), ()))


def matmul(a, b, dims=NN):
    return lax.dot_general(a, b, dims, preferred_element_type=jnp.float32)


def vmem(count):
    return [pl.BlockSpec(memory_space=pltpu.VMEM)] * count


def exchange_kernel(
    groups, norm, cot, request, x, cot_all, grant, outbuf,
    req_send, req_recv, out_send, out_recv, fwd_send, fwd_recv, own_send, own_recv,
):
    scene, me, row = lax.axis_index("scene"), lax.axis_index("view"), lax.axis_index("row")
    views = norm.shape[0]
    sibling = (scene, me, 1 - row)
    barrier = pltpu.get_barrier_semaphore()

    def peer(step):
        return lax.rem(me + step, groups)

    for step in range(1, groups):
        pl.semaphore_signal(barrier, inc=1, device_id=(scene, peer(step), row), device_id_type=MESH)
    pl.semaphore_signal(barrier, inc=1, device_id=sibling, device_id_type=MESH)
    pl.semaphore_wait(barrier, groups)

    def remote(src, dst, send, recv, device):
        return pltpu.make_async_remote_copy(
            src_ref=src, dst_ref=dst, send_sem=send, recv_sem=recv, device_id=device, device_id_type=MESH
        )

    asks = [
        remote(request.at[peer(s)], grant.at[me], req_send.at[s], req_recv.at[s], (scene, peer(s), row))
        for s in range(1, groups)
    ]
    for copy in asks:
        copy.start()
    own = [
        remote(norm.at[0], x.at[row, me], own_send.at[0], own_recv.at[0], sibling),
        remote(
            norm.at[pl.ds(1, views - 1)], x.at[row, pl.ds(groups, views - 1)],
            own_send.at[1], own_recv.at[1], sibling,
        ),
        remote(cot, cot_all.at[row], own_send.at[2], own_recv.at[2], sibling),
    ]
    for copy in own:
        copy.start()
    x[row, me] = norm[0]
    x[row, pl.ds(groups, views - 1)] = norm[1:]
    cot_all[row] = cot[...]

    blocks = []
    for s in range(1, groups):
        back = groups - s
        asks[back - 1].wait_recv()
        want = grant[peer(s)][0:1, 0:1]
        block = norm[0]
        for v in range(1, views):
            block = jnp.where(want == v, norm[v], block)
        outbuf[s - 1] = block
        blocks.append(
            remote(outbuf.at[s - 1], x.at[row, me], out_send.at[s], out_recv.at[s], (scene, peer(s), row))
        )
        blocks[-1].start()
    forwards = []
    for s in range(1, groups):
        blocks[s - 1].wait_recv()
        source = lax.rem(me + groups - s, groups)
        forwards.append(
            remote(x.at[row, source], x.at[row, source], fwd_send.at[s], fwd_recv.at[s], sibling)
        )
        forwards[-1].start()
    for copy in own + forwards:
        copy.wait()
    for copy in asks + blocks:
        copy.wait_send()


def exchange(norm, cot, request, groups):
    views, columns, width = norm.shape
    slots = groups + views - 1
    dma = pltpu.SemaphoreType.DMA
    return pl.pallas_call(
        functools.partial(exchange_kernel, groups),
        out_shape=(
            jax.ShapeDtypeStruct((2, slots, columns, width), jnp.bfloat16),
            jax.ShapeDtypeStruct((2, views, columns, width), jnp.bfloat16),
        ),
        in_specs=vmem(3),
        out_specs=tuple(vmem(2)),
        scratch_shapes=[
            pltpu.VMEM((groups, 8, LANES), jnp.int32),
            pltpu.VMEM((groups - 1, columns, width), jnp.bfloat16),
            dma((groups,)), dma((groups,)), dma((groups,)), dma((groups,)),
            dma((groups,)), dma((groups,)), dma((3,)), dma((3,)),
        ],
        compiler_params=pltpu.CompilerParams(
            collective_id=0, has_side_effects=True, vmem_limit_bytes=VMEM_LIMIT
        ),
    )(norm, cot, request)


def local_kernel(
    groups, x, cot, taps, bias, wq_hbm, wk_hbm, wv_hbm, wo_hbm, ga, mt, up,
    wq, wkv, wo, xo, xt, xot, keys, values, qm, om, s_buf, dp_buf, p_buf, ds_buf, dkv, sems,
):
    me, core = lax.axis_index("view"), lax.axis_index("row")
    width = x.shape[-1]
    half = wq.shape[1]
    pairs = half // LANES
    key_rows, queries = s_buf.shape
    columns, views = cot.shape[2], cot.shape[1]
    slots = key_rows // (2 * columns)
    scale = HEAD_DIM ** (-0.5)
    cols = pl.ds(pl.multiple_of(core * half, LANES), half)
    loads = [
        pltpu.make_async_copy(wq_hbm.at[:, cols], wq, sems.at[0]),
        pltpu.make_async_copy(wk_hbm.at[:, cols], wkv.at[:, pl.ds(0, half)], sems.at[1]),
        pltpu.make_async_copy(wv_hbm.at[:, cols], wkv.at[:, pl.ds(half, half)], sems.at[2]),
        pltpu.make_async_copy(wo_hbm.at[cols, :], wo, sems.at[3]),
    ]
    for copy in loads:
        copy.start()

    for strip in range(2):
        base = strip * slots * columns
        top = strip * views * columns
        xo[pl.ds(top, columns)] = x[pl.ds(pl.multiple_of(base + me * columns, columns), columns)]
        rest = (views - 1) * columns
        xo[pl.ds(top + columns, rest)] = x[pl.ds(base + groups * columns, rest)]

    chunk = 4 * LANES
    place = lax.broadcasted_iota(jnp.int32, (columns, chunk), 0)

    def conv_view(view, carry):
        for part in range(width // chunk):
            lanes = pl.ds(part * chunk, chunk)
            kern = taps[:, lanes].astype(jnp.float32)
            shifted = []
            for strip in range(2):
                mid = cot[strip, view, :, lanes].astype(jnp.float32)
                after = jnp.where(place == columns - 1, 0.0, pltpu.roll(mid, columns - 1, 0))
                before = jnp.where(place == 0, 0.0, pltpu.roll(mid, 1, 0))
                shifted.append((after, mid, before))
            for strip in range(2):
                total = shifted[strip][1]
                for a, source in ((1, strip), (2 * strip, 1 - strip)):
                    for b in range(3):
                        total = total + kern[3 * a + b : 3 * a + b + 1] * shifted[source][b]
                where = (part * chunk) // (width // 2)
                offset = part * chunk - where * (width // 2)
                size = min(chunk, width // 2 - offset)
                rows = pl.ds(pl.multiple_of((strip * views + view) * columns, columns), columns)
                rounded = total.astype(jnp.bfloat16)
                up[where, rows, pl.ds(offset, size)] = rounded[:, :size]
                if size < chunk:
                    up[where + 1, rows, pl.ds(0, chunk - size)] = rounded[:, size:]
        return carry

    lax.fori_loop(0, views, conv_view, 0)

    for copy in loads:
        copy.wait()

    lane = lax.broadcasted_iota(jnp.int32, (queries, LANES), 1)

    def split_heads(out, rows_f):
        rounded = rows_f.astype(jnp.bfloat16).astype(jnp.float32)
        for pair in range(pairs):
            block = rounded[:, pair * LANES : (pair + 1) * LANES]
            out[pair, pl.ds(0, queries)] = jnp.where(lane < HEAD_DIM, block, 0.0).astype(jnp.bfloat16)
            out[pair, pl.ds(queries, queries)] = jnp.where(lane < HEAD_DIM, 0.0, block).astype(jnp.bfloat16)

    split_heads(qm, matmul(xo[...], wq[...]))
    og = matmul(up[0], wo[:, pl.ds(0, width // 2)], NT) + matmul(up[1], wo[:, pl.ds(width // 2, width // 2)], NT)
    split_heads(om, og)

    block_rows = key_rows // 4

    def project(i, carry):
        rows = pl.ds(pl.multiple_of(i * block_rows, 16), block_rows)
        out = matmul(x[rows], wkv[...]).astype(jnp.bfloat16)
        for pair in range(pairs):
            keys[pair, rows] = out[:, pair * LANES : (pair + 1) * LANES]
            values[pair, rows] = out[:, half + pair * LANES : half + (pair + 1) * LANES]
        return carry

    lax.fori_loop(0, 4, project, 0)

    eye = (
        lax.broadcasted_iota(jnp.int32, (LANES, LANES), 0) == lax.broadcasted_iota(jnp.int32, (LANES, LANES), 1)
    ).astype(jnp.float32).astype(jnp.bfloat16)

    def turn(j, carry):
        lanes = pl.ds(pl.multiple_of(j * LANES, LANES), LANES)
        xt[lanes] = matmul(eye, x[:, lanes], NT).astype(jnp.bfloat16)
        xot[lanes] = matmul(eye, xo[:, lanes], NT).astype(jnp.bfloat16)
        return carry

    lax.fori_loop(0, width // LANES, turn, 0)

    step = 64
    steps = key_rows // step

    def fold(v, op):
        return op(v.reshape(step // 8, 8, queries), axis=0)

    def one_pair(pair, carry):
        for head in range(2):
            mine = pl.ds(head * queries, queries)
            s_buf[...] = matmul(keys[pair], qm[pair, mine], NT)
            dp_buf[...] = matmul(values[pair], om[pair, mine], NT)

            def high(i, top):
                rows = pl.ds(pl.multiple_of(i * step, step), step)
                v = s_buf[rows] * scale + bias[rows]
                s_buf[rows] = v
                return jnp.maximum(top, fold(v, jnp.max))

            top = lax.fori_loop(0, steps, high, jnp.full((8, queries), -3e38, jnp.float32))
            top = jnp.max(top, axis=0, keepdims=True)

            def weigh(i, sums):
                rows = pl.ds(pl.multiple_of(i * step, step), step)
                e = jnp.exp(s_buf[rows] - top)
                s_buf[rows] = e
                return sums[0] + fold(e, jnp.sum), sums[1] + fold(e * dp_buf[rows], jnp.sum)

            zero = jnp.zeros((8, queries), jnp.float32)
            total, delta = lax.fori_loop(0, steps, weigh, (zero, zero))
            inverse = 1.0 / jnp.sum(total, axis=0, keepdims=True)
            delta = jnp.sum(delta, axis=0, keepdims=True) * inverse

            def finish(i, carry):
                rows = pl.ds(pl.multiple_of(i * step, step), step)
                p = s_buf[rows] * inverse
                p_buf[rows, mine] = p.astype(jnp.bfloat16)
                ds_buf[rows, mine] = (p * (dp_buf[rows] - delta) * scale).astype(jnp.bfloat16)
                return carry

            lax.fori_loop(0, steps, finish, 0)

        dkv[:, pl.ds(0, LANES)] = matmul(ds_buf[...], qm[pair]).astype(jnp.bfloat16)
        dkv[:, pl.ds(LANES, LANES)] = matmul(p_buf[...], om[pair]).astype(jnp.bfloat16)
        vt = matmul(eye, values[pair], NT).astype(jnp.bfloat16)
        kt = matmul(eye, keys[pair], NT).astype(jnp.bfloat16)
        mixed = matmul(vt, p_buf[...]).astype(jnp.bfloat16)
        dq = matmul(kt, ds_buf[...])
        row_of = pl.multiple_of(pair * LANES, LANES)
        mt[pl.ds(row_of, HEAD_DIM)] = mixed[:HEAD_DIM, :queries]
        mt[pl.ds(row_of + HEAD_DIM, HEAD_DIM)] = mixed[HEAD_DIM:, queries:]
        dqt = jnp.concatenate((dq[:HEAD_DIM, :queries], dq[HEAD_DIM:, queries:]), axis=0).astype(jnp.bfloat16)

        def grads(i, carry):
            rows = pl.ds(pl.multiple_of(i * (width // 4), width // 4), width // 4)
            blocks = pl.ds(i * 4, 4)
            gq = matmul(xot[rows], dqt, NT).astype(jnp.bfloat16)
            gkv = matmul(xt[rows], dkv[...]).astype(jnp.bfloat16)
            ga[pair, blocks, :, pl.ds(0, LANES)] = gq.reshape(4, width // 16, LANES)
            ga[pair, blocks, :, pl.ds(LANES, 2 * LANES)] = gkv.reshape(4, width // 16, 2 * LANES)
            return carry

        lax.fori_loop(0, 4, grads, 0)
        return carry

    lax.fori_loop(0, pairs, one_pair, 0)


def local_part(x, cot, taps, bias, wq, wk, wv, wo, groups):
    key_rows, width = x.shape
    queries = bias.shape[1]
    half = wq.shape[1] // 2
    pairs = half // LANES
    bf = jnp.bfloat16
    return pl.pallas_call(
        functools.partial(local_kernel, groups),
        out_shape=(
            jax.ShapeDtypeStruct((pairs, 16, width // 16, 3 * LANES), bf),
            jax.ShapeDtypeStruct((half, queries), bf),
            jax.ShapeDtypeStruct((2, queries, width // 2), bf),
        ),
        in_specs=vmem(4) + [pl.BlockSpec(memory_space=pl.ANY)] * 4,
        out_specs=tuple(vmem(3)),
        scratch_shapes=[
            pltpu.VMEM((width, half), bf),
            pltpu.VMEM((width, 2 * half), bf),
            pltpu.VMEM((half, width), bf),
            pltpu.VMEM((queries, width), bf),
            pltpu.VMEM((width, key_rows), bf),
            pltpu.VMEM((width, queries), bf),
            pltpu.VMEM((pairs, key_rows, LANES), bf),
            pltpu.VMEM((pairs, key_rows, LANES), bf),
            pltpu.VMEM((pairs, 2 * queries, LANES), bf),
            pltpu.VMEM((pairs, 2 * queries, LANES), bf),
            pltpu.VMEM((key_rows, queries), jnp.float32),
            pltpu.VMEM((key_rows, queries), jnp.float32),
            pltpu.VMEM((key_rows, 2 * queries), bf),
            pltpu.VMEM((key_rows, 2 * queries), bf),
            pltpu.VMEM((key_rows, 2 * LANES), bf),
            pltpu.SemaphoreType.DMA((4,)),
        ],
        compiler_params=pltpu.CompilerParams(vmem_limit_bytes=VMEM_LIMIT),
    )(x, cot, taps, bias, wq, wk, wv, wo)


def sums_kernel(
    ga, mt, up, out_a, out_o,
    mixed, o1, r1a, r1b, r1o, p2a, p2b, p2o, r2a, r2b, r2o, p3, p3o, r3, r3o, f_own, f_sib, fo_own, fo_sib,
    m_send, m_recv, s1, d1, s2, d2, s3, d3, s4, d4,
):
    xx, vv, core = lax.axis_index("scene"), lax.axis_index("view"), lax.axis_index("row")
    yy, zz = vv // 4, lax.rem(vv, 4)
    sibling = (xx, vv, 1 - core)

    def along(axis, step):
        if axis == 0:
            at = lax.rem(xx + step, 4)
            return at, (at, vv, core)
        if axis == 1:
            at = lax.rem(yy + step, 4)
            return at, (xx, at * 4 + zz, core)
        at = lax.rem(zz + step, 4)
        return at, (xx, yy * 4 + at, core)

    barrier = pltpu.get_barrier_semaphore()
    for axis in range(3):
        for step in range(1, 4):
            pl.semaphore_signal(barrier, inc=1, device_id=along(axis, step)[1], device_id_type=MESH)
    pl.semaphore_signal(barrier, inc=1, device_id=sibling, device_id_type=MESH)
    pl.semaphore_wait(barrier, 10)

    def remote(src, dst, send, recv, device):
        copy = pltpu.make_async_remote_copy(
            src_ref=src, dst_ref=dst, send_sem=send, recv_sem=recv, device_id=device, device_id_type=MESH
        )
        copy.start()
        return copy

    everything = []

    def send_three(axis, source, target, send, recv, base):
        copies = []
        for step in range(1, 4):
            at, device = along(axis, step)
            copies.append(
                remote(source(at), target.at[step - 1], send.at[base + step - 1], recv.at[base + step - 1], device)
            )
        everything.extend(copies)
        return copies

    swap = remote(mt, mixed.at[core], m_send, m_recv, sibling)
    first_a = send_three(0, lambda at: ga.at[0, at], r1a, s1, d1, 0)
    first_b = [
        send_three(1, lambda at, t=t: ga.at[t, :, at], r1b.at[t - 1], s1, d1, 3 * t) for t in (1, 2)
    ]
    mixed[core] = mt[...]
    swap.wait()
    channels = 2 * mt.shape[0]
    mixed_all = mixed[...].reshape(channels, mt.shape[1])
    half_up = up[core]
    for i in range(4):
        rows = channels // 4
        part = matmul(mixed_all[i * rows : (i + 1) * rows], half_up).astype(jnp.bfloat16)
        o1[i] = part.reshape(4, rows // 4, half_up.shape[1])
    first_o = send_three(0, lambda at: o1.at[at], r1o, s1, d1, 9)

    f32 = jnp.float32

    def collect(copies):
        for copy in copies:
            copy.wait_recv()

    collect(first_a)
    for j in range(4):
        p2a[j] = (
            ga[0, xx, j].astype(f32) + r1a[0, j].astype(f32) + r1a[1, j].astype(f32) + r1a[2, j].astype(f32)
        )
    second = [send_three(1, lambda at: p2a.at[at], r2a, s2, d2, 0)]
    for t in (0, 1):
        collect(first_b[t])
        for j in range(4):
            p2b[t, j] = (
                ga[t + 1, j, yy].astype(f32) + r1b[t, 0, j].astype(f32) + r1b[t, 1, j].astype(f32)
                + r1b[t, 2, j].astype(f32)
            )
        second.append(send_three(0, lambda at, t=t: p2b.at[t, at], r2b.at[t], s2, d2, 3 + 3 * t))
    collect(first_o)
    for j in range(4):
        p2o[j] = (
            o1[xx, j].astype(f32) + r1o[0, j].astype(f32) + r1o[1, j].astype(f32) + r1o[2, j].astype(f32)
        )
    second_o = send_three(1, lambda at: p2o.at[at], r2o, s2, d2, 9)

    third = []
    for t in range(3):
        collect(second[t])
        own, got = (p2a.at[yy], r2a) if t == 0 else (p2b.at[t - 1, xx], r2b.at[t - 1])
        whole = own[...] + got[0] + got[1] + got[2]
        rows = whole.shape[0] // 4
        for j in range(4):
            p3[t, j] = whole[j * rows : (j + 1) * rows]
        third.append(send_three(2, lambda at, t=t: p3.at[t, at], r3.at[t], s3, d3, 3 * t))
    collect(second_o)
    whole = p2o[yy] + r2o[0] + r2o[1] + r2o[2]
    rows = whole.shape[0] // 4
    for j in range(4):
        p3o[j] = whole[j * rows : (j + 1) * rows]
    third_o = send_three(2, lambda at: p3o.at[at], r3o, s3, d3, 9)

    for t in range(3):
        collect(third[t])
        whole = p3[t, zz] + r3[t, 0] + r3[t, 1] + r3[t, 2]
        rows = whole.shape[0] // 2
        for j in range(2):
            f_own[j, t] = whole[j * rows : (j + 1) * rows]
    last_a = remote(f_own.at[1 - core], f_sib, s4.at[0], d4.at[0], sibling)
    collect(third_o)
    whole = p3o[zz] + r3o[0] + r3o[1] + r3o[2]
    rows = whole.shape[0] // 2
    for j in range(2):
        fo_own[j] = whole[j * rows : (j + 1) * rows]
    last_o = remote(fo_own.at[1 - core], fo_sib, s4.at[1], d4.at[1], sibling)
    out_a[core] = f_own[core]
    out_o[core] = fo_own[core]
    last_a.wait()
    last_o.wait()
    out_a[1 - core] = f_sib[...]
    out_o[1 - core] = fo_sib[...]
    for copy in everything:
        copy.wait_send()


def chip_sums(ga, mt, up):
    pairs = ga.shape[0]
    rows, cols = ga.shape[2:]
    half, queries = mt.shape
    wide = up.shape[2]
    orows = 2 * half // 16
    bf, f32 = jnp.bfloat16, jnp.float32
    dma = pltpu.SemaphoreType.DMA
    ga = ga.reshape(pairs, 4, 4, rows, cols)
    return pl.pallas_call(
        sums_kernel,
        out_shape=(
            jax.ShapeDtypeStruct((2, pairs, rows // 8, cols), f32),
            jax.ShapeDtypeStruct((2, orows // 8, wide), f32),
        ),
        in_specs=vmem(3),
        out_specs=tuple(vmem(2)),
        scratch_shapes=[
            pltpu.VMEM((2, half, queries), bf),
            pltpu.VMEM((4, 4, orows, wide), bf),
            pltpu.VMEM((3, 4, rows, cols), bf),
            pltpu.VMEM((2, 3, 4, rows, cols), bf),
            pltpu.VMEM((3, 4, orows, wide), bf),
            pltpu.VMEM((4, rows, cols), f32),
            pltpu.VMEM((2, 4, rows, cols), f32),
            pltpu.VMEM((4, orows, wide), f32),
            pltpu.VMEM((3, rows, cols), f32),
            pltpu.VMEM((2, 3, rows, cols), f32),
            pltpu.VMEM((3, orows, wide), f32),
            pltpu.VMEM((3, 4, rows // 4, cols), f32),
            pltpu.VMEM((4, orows // 4, wide), f32),
            pltpu.VMEM((3, 3, rows // 4, cols), f32),
            pltpu.VMEM((3, orows // 4, wide), f32),
            pltpu.VMEM((2, 3, rows // 8, cols), f32),
            pltpu.VMEM((3, rows // 8, cols), f32),
            pltpu.VMEM((2, orows // 8, wide), f32),
            pltpu.VMEM((orows // 8, wide), f32),
            dma, dma, dma((12,)), dma((12,)), dma((12,)), dma((12,)), dma((12,)), dma((12,)), dma((2,)), dma((2,)),
        ],
        compiler_params=pltpu.CompilerParams(
            collective_id=1, has_side_effects=True, vmem_limit_bytes=VMEM_LIMIT
        ),
    )(ga, mt, up)


def shards(latents, norm_gain, w_query, w_key, w_value, w_out, kernel, partners, counts, cotangent):
    views, _, columns, width = latents.shape[1:]
    groups = lax.axis_size("view")
    me = lax.axis_index("view")
    lat_f = latents[0, :, 0].astype(jnp.float32)
    norm = (
        lat_f * lax.rsqrt(jnp.mean(lat_f * lat_f, -1, keepdims=True) + EPSILON) * norm_gain
    ).astype(jnp.bfloat16)

    partner_ids = partners[0]
    most = partner_ids.shape[1]
    alive = jnp.arange(most, dtype=jnp.int32)[None, :] < counts[0][:, None]
    source = jnp.where(alive, partner_ids // views, -1)
    matches = source[:, :, None] == jnp.arange(groups, dtype=jnp.int32)[None, None, :]
    wanted = jnp.max(jnp.where(matches, (partner_ids % views)[:, :, None], 0), axis=(0, 1))
    request = jnp.broadcast_to(wanted[:, None, None], (groups, 8, LANES))

    x, cot = exchange(norm, cotangent[0, :, 0], request, groups)

    slots = groups + views - 1
    view_of = jnp.arange(views, dtype=jnp.int32)
    slot_of = jnp.arange(slots, dtype=jnp.int32)
    home = jnp.where(view_of == 0, me, groups - 1 + view_of)
    seen = jnp.concatenate((jnp.any(matches, axis=1), jnp.zeros((views, views - 1), bool)), axis=1)
    seen = seen | (slot_of[None, :] == home[:, None])
    bias = jnp.where(seen.T, 0.0, -1e30).astype(jnp.float32)
    bias = jnp.broadcast_to(
        bias[None, :, None, None, :, None], (2, slots, columns, 2, views, columns)
    ).reshape(2 * slots * columns, 2 * views * columns)

    ga, mt, up = local_part(
        x.reshape(2 * slots * columns, width), cot, kernel, bias, w_query, w_key, w_value, w_out, groups
    )
    out_a, out_o = chip_sums(ga, mt, up)
    pairs, rows = out_a.shape[1:3]
    out_a = out_a.reshape(2, pairs, rows, 3, LANES).transpose(3, 2, 0, 1, 4).reshape(3, rows, 2 * pairs * LANES)
    out_o = out_o.transpose(1, 0, 2).reshape(out_o.shape[1], width)
    return out_a[0], out_a[1], out_a[2], out_o


def solution(mesh):
    strips = P("scene", "view", "row", None, None)
    return jax.shard_map(
        shards,
        mesh=mesh,
        in_specs=(
            strips, P(), P(), P(), P(), P(), P(),
            P("scene", "view", None), P("scene", "view"), strips,
        ),
        out_specs=(P(("scene", "view", "row"), None),) * 4,
        check_vma=False,
    )
```

```python
import functools

import jax
import jax.numpy as jnp
from jax import lax
from jax.experimental import pallas as pl
from jax.experimental.pallas import tpu as pltpu
from jax.sharding import PartitionSpec as P

HEAD_DIM = 64
LANES = 128
EPSILON = 1e-06
SIDE = 4
MESH = pl.DeviceIdType.MESH
VMEM_LIMIT = 62 * 1024 * 1024
NT = (((1,), (1,)), ((), ()))
NN = (((1,), (0,)), ((), ()))
BF = jnp.bfloat16
F32 = jnp.float32


def matmul(a, b, dims=NN):
    return lax.dot_general(a, b, dims, preferred_element_type=F32)


def kernel_body(
    lat, gain, cot, taps, partners, wq_hbm, wk_hbm, wv_hbm, wo_hbm,
    out_q, out_k, out_v, out_o,
    x, cot_all, ask, grant, outbuf, bias,
    wq, wkv, wo, xt, keys, values, qm, om, up, s_all, dp_all, tops, p_buf, ds_buf, dkv, mixed,
    gq, gk, gv, r1, p2, r2, p3, r3, f_own, f_sib,
    og, go_tmp, o1, po2, o2, po3, o3, fo_own, fo_sib,
    load_sem, own_send, own_recv, ask_send, ask_recv, out_send, out_recv, fwd_send, fwd_recv,
    mix_send, mix_recv, s1, d1, s2, d2, s3, d3, s4, d4,
):
    xx, me, core = lax.axis_index("scene"), lax.axis_index("view"), lax.axis_index("row")
    yy, zz = me // SIDE, lax.rem(me, SIDE)
    groups = SIDE * SIDE
    views, columns, width = lat.shape
    half = wq.shape[1]
    pairs = half // LANES
    slots = x.shape[0]
    slot_rows = 2 * columns
    key_rows = slots * slot_rows
    queries = views * slot_rows
    scale = HEAD_DIM ** (-0.5)
    sibling = (xx, me, 1 - core)

    def peer(step):
        return lax.rem(me + step, groups)

    def along(axis, step):
        if axis == 0:
            at = lax.rem(xx + step, SIDE)
            return at, (at, me, core)
        if axis == 1:
            at = lax.rem(yy + step, SIDE)
            return at, (xx, at * SIDE + zz, core)
        at = lax.rem(zz + step, SIDE)
        return at, (xx, yy * SIDE + at, core)

    barrier = pltpu.get_barrier_semaphore()
    for step in range(1, groups):
        pl.semaphore_signal(barrier, inc=1, device_id=(xx, peer(step), core), device_id_type=MESH)
    for step in range(1, SIDE):
        pl.semaphore_signal(barrier, inc=1, device_id=along(0, step)[1], device_id_type=MESH)
    pl.semaphore_signal(barrier, inc=1, device_id=sibling, device_id_type=MESH)

    cols = pl.ds(pl.multiple_of(core * half, LANES), half)
    loads = [
        pltpu.make_async_copy(wq_hbm.at[:, cols], wq, load_sem.at[0]),
        pltpu.make_async_copy(wk_hbm.at[:, cols], wkv.at[:, pl.ds(0, half)], load_sem.at[1]),
        pltpu.make_async_copy(wv_hbm.at[:, cols], wkv.at[:, pl.ds(half, half)], load_sem.at[2]),
        pltpu.make_async_copy(wo_hbm.at[cols, :], wo, load_sem.at[3]),
    ]
    for copy in loads:
        copy.start()

    steps_of = lax.broadcasted_iota(jnp.int32, (groups, LANES), 0)
    first_of = lax.rem(me + steps_of, groups) * views
    wanted = jnp.zeros((groups, LANES), jnp.int32)
    slot_of = lax.broadcasted_iota(jnp.int32, bias.shape, 0)
    view_of = lax.broadcasted_iota(jnp.int32, bias.shape, 1) // slot_rows
    slot_first = jnp.where(slot_of < views, -2 * views, lax.rem(me + groups + views - 1 - slot_of, groups) * views)
    seen = jnp.where(slot_of == view_of, 1, 0)
    for v in range(views):
        for j in range(partners.shape[1]):
            number = partners[v, j]
            local = number - first_of
            wanted = jnp.maximum(wanted, jnp.where((local >= 0) & (local < views), local, 0))
            local = number - slot_first
            hit = (local >= 0) & (local < views) & (view_of == v) & (number >= 0)
            seen = jnp.where(hit, 1, seen)
    bias[...] = jnp.where(seen > 0, 0.0, -1e30)
    for step in range(1, groups):
        ask[step] = jnp.broadcast_to(wanted[step : step + 1], ask.shape[1:])

    for v in range(views):
        rows = lat[v].astype(F32)
        mean = jnp.mean(rows * rows, -1, keepdims=True)
        x[v, core] = (rows * lax.rsqrt(mean + EPSILON) * gain[...]).astype(BF)
    cot_all[core] = cot[...]

    pl.semaphore_wait(barrier, groups + SIDE - 1)

    def remote(src, dst, send, recv, device):
        copy = pltpu.make_async_remote_copy(
            src_ref=src, dst_ref=dst, send_sem=send, recv_sem=recv, device_id=device, device_id_type=MESH
        )
        copy.start()
        return copy

    sent = []
    asks = [
        remote(ask.at[s], grant.at[s], ask_send.at[s], ask_recv.at[s], (xx, peer(s), core))
        for s in range(1, groups)
    ]
    mine = x.at[pl.ds(0, views), core]
    own_x = remote(mine, mine, own_send.at[0], own_recv.at[0], sibling)
    own_cot = remote(cot, cot_all.at[core], own_send.at[1], own_recv.at[1], sibling)

    blocks = []
    for s in range(1, groups):
        asks[groups - s - 1].wait_recv()
        want = grant[groups - s][0:1, 0:1]
        block = x[0, core]
        for v in range(1, views):
            block = jnp.where(want == v, x[v, core], block)
        outbuf[s - 1] = block
        blocks.append(
            remote(
                outbuf.at[s - 1], x.at[views - 1 + s, core], out_send.at[s], out_recv.at[s], (xx, peer(s), core)
            )
        )
    sent += asks + [own_x, own_cot] + blocks

    own_cot.wait_recv()
    chunk = 2 * LANES
    place = lax.broadcasted_iota(jnp.int32, (columns, chunk), 0)

    def conv_view(view, carry):
        for part in range(width // chunk):
            lanes = pl.ds(part * chunk, chunk)
            kern = taps[:, lanes].astype(F32)
            shifted = []
            for strip in range(2):
                mid = cot_all[strip, view, :, lanes].astype(F32)
                after = jnp.where(place == columns - 1, 0.0, pltpu.roll(mid, columns - 1, 0))
                before = jnp.where(place == 0, 0.0, pltpu.roll(mid, 1, 0))
                shifted.append((after, mid, before))
            for strip in range(2):
                total = shifted[strip][1]
                for a, source in ((1, strip), (2 * strip, 1 - strip)):
                    for b in range(3):
                        total = total + kern[3 * a + b : 3 * a + b + 1] * shifted[source][b]
                side = part * chunk // (width // 2)
                rows = pl.ds(pl.multiple_of(view * slot_rows + strip * columns, columns), columns)
                up[side, rows, pl.ds(part * chunk - side * (width // 2), chunk)] = total.astype(BF)
        return carry

    lax.fori_loop(0, views, conv_view, 0)

    for copy in loads:
        copy.wait()

    lane = lax.broadcasted_iota(jnp.int32, (queries, LANES), 1)

    def split_heads(out, rows_f):
        rounded = rows_f.astype(BF).astype(F32)
        for pair in range(pairs):
            block = rounded[:, pair * LANES : (pair + 1) * LANES]
            out[pair, pl.ds(0, queries)] = jnp.where(lane < HEAD_DIM, block, 0.0).astype(BF)
            out[pair, pl.ds(queries, queries)] = jnp.where(lane < HEAD_DIM, 0.0, block).astype(BF)

    split_heads(
        om,
        matmul(up[0], wo[:, pl.ds(0, width // 2)], NT) + matmul(up[1], wo[:, pl.ds(width // 2, width // 2)], NT),
    )
    own_x.wait_recv()
    split_heads(qm, matmul(x[pl.ds(0, views)].reshape(queries, width), wq[...]))

    tile = 2 * LANES
    eye = (
        lax.broadcasted_iota(jnp.int32, (tile, tile), 0) == lax.broadcasted_iota(jnp.int32, (tile, tile), 1)
    ).astype(F32).astype(BF)

    def fold(v, op):
        return op(v.reshape(v.shape[0] // 8, 8, v.shape[1]), axis=0)

    def batch(first, count):
        rows = pl.ds(first * slot_rows, count * slot_rows)
        flat = x[pl.ds(first, count)].reshape(count * slot_rows, width)
        out = matmul(flat, wkv[...]).astype(BF)
        for pair in range(pairs):
            keys[pair, rows] = out[:, pair * LANES : (pair + 1) * LANES]
            values[pair, rows] = out[:, half + pair * LANES : half + (pair + 1) * LANES]

        def turn(j, carry):
            lanes = pl.ds(pl.multiple_of(j * tile, tile), tile)
            part = x[pl.ds(first, count), :, :, lanes].reshape(count * slot_rows, tile)
            xt[lanes, rows] = matmul(eye, part, NT).astype(BF)
            return carry

        lax.fori_loop(0, width // tile, turn, 0)

        def score(pair, carry):
            for head in range(2):
                mine = pl.ds(head * queries, queries)
                s = matmul(keys[pair, rows], qm[pair, mine], NT) * scale
                top = jnp.full((8, queries), -3e38, F32) if first == 0 else tops[2 * pair + head]
                for i in range(count):
                    part = s[i * slot_rows : (i + 1) * slot_rows] + bias[pl.ds(first + i, 1)]
                    s_all[2 * pair + head, pl.ds((first + i) * slot_rows, slot_rows)] = part
                    top = jnp.maximum(top, fold(part, jnp.max))
                tops[2 * pair + head] = top
                dp_all[2 * pair + head, rows] = matmul(values[pair, rows], om[pair, mine], NT)
            return carry

        lax.fori_loop(0, pairs, score, 0)

    size = 4
    parts = [(i, min(size, slots - i)) for i in range(views, slots, size)]
    before = (0, views)
    forwards = []
    for first, count in parts:
        fresh = []
        for slot in range(first, first + count):
            s = slot - views + 1
            blocks[s - 1].wait_recv()
            place_x = x.at[slot, core]
            fresh.append(remote(place_x, place_x, fwd_send.at[s], fwd_recv.at[s], sibling))
        batch(*before)
        for copy in fresh:
            copy.wait_recv()
        forwards += fresh
        before = (first, count)
    batch(*before)
    sent += forwards

    def send_three(axis, source, target, send, recv, base):
        copies = []
        for step in range(1, SIDE):
            at, device = along(axis, step)
            copies.append(
                remote(source(at), target.at[step - 1], send.at[base + step - 1], recv.at[base + step - 1], device)
            )
        sent.extend(copies)
        return copies

    def collect(copies):
        for copy in copies:
            copy.wait_recv()

    place_of = (xx, yy, zz)
    orders = ((0, 1, 2), (1, 2, 0), (2, 0, 1))
    rows1 = gq.shape[3]
    rows2 = rows1 // SIDE

    def phase1(t):
        return [
            send_three(0, lambda at: gq.at[t, at], r1.at[t, 0], s1, d1, 9 * t),
            send_three(1, lambda at: gk.at[t, :, at], r1.at[t, 1], s1, d1, 9 * t + 3),
            send_three(2, lambda at: gv.at[t, at], r1.at[t, 2], s1, d1, 9 * t + 6),
        ]

    def phase2(t, arrived):
        copies = []
        for m in range(3):
            collect(arrived[m])
            for j in range(SIDE):
                own = (gq.at[t, xx, j], gk.at[t, j, yy], gv.at[t, zz, j])[m]
                total = own[...].astype(F32)
                for i in range(SIDE - 1):
                    total = total + r1[t, m, i, j].astype(F32)
                if m == 1:
                    for k in range(SIDE):
                        p2[t, m, k, pl.ds(j * rows2, rows2)] = total[k * rows2 : (k + 1) * rows2]
                else:
                    p2[t, m, j] = total
            copies.append(
                send_three(orders[m][1], lambda at, m=m: p2.at[t, m, at], r2.at[t, m], s2, d2, 9 * t + 3 * m)
            )
        return copies

    def phase3(t, arrived):
        copies = []
        for m in range(3):
            collect(arrived[m])
            total = p2[t, m, place_of[orders[m][1]]] + r2[t, m, 0] + r2[t, m, 1] + r2[t, m, 2]
            for j in range(SIDE):
                p3[t, m, j] = total[j * rows2 : (j + 1) * rows2]
            copies.append(
                send_three(orders[m][2], lambda at, m=m: p3.at[t, m, at], r3.at[t, m], s3, d3, 9 * t + 3 * m)
            )
        return copies

    outs = (out_q, out_k, out_v)

    def phase4(t, arrived):
        for m in range(3):
            collect(arrived[m])
            total = p3[t, m, place_of[orders[m][2]]] + r3[t, m, 0] + r3[t, m, 1] + r3[t, m, 2]
            for j in range(2):
                f_own[j, t, m] = total[j * (rows2 // 2) : (j + 1) * (rows2 // 2)]
            lanes = pl.ds(pl.multiple_of(core * half + t * LANES, LANES), LANES)
            outs[m][:, lanes] = f_own[core, t, m]
        copy = remote(f_own.at[1 - core, t], f_sib.at[t], s4.at[t], d4.at[t], sibling)
        sent.append(copy)
        return copy

    def finish(t, copy):
        copy.wait_recv()
        lanes = pl.ds(pl.multiple_of((1 - core) * half + t * LANES, LANES), LANES)
        for m in range(3):
            outs[m][:, lanes] = f_sib[t, m]

    step = 64
    steps = key_rows // step
    mixes = []

    def attend(t):
        for head in range(2):
            h = 2 * t + head
            mine = pl.ds(head * queries, queries)
            top = jnp.max(tops[h], axis=0, keepdims=True)

            def weigh(i, sums, h=h, top=top):
                rows = pl.ds(pl.multiple_of(i * step, step), step)
                e = jnp.exp(s_all[h, rows] - top)
                s_all[h, rows] = e
                return sums[0] + fold(e, jnp.sum), sums[1] + fold(e * dp_all[h, rows], jnp.sum)

            zero = jnp.zeros((8, queries), F32)
            total, delta = lax.fori_loop(0, steps, weigh, (zero, zero))
            inverse = 1.0 / jnp.sum(total, axis=0, keepdims=True)
            delta = jnp.sum(delta, axis=0, keepdims=True) * inverse

            def close(i, carry, h=h, mine=mine, inverse=inverse, delta=delta):
                rows = pl.ds(pl.multiple_of(i * step, step), step)
                p = s_all[h, rows] * inverse
                p_buf[rows, mine] = p.astype(BF)
                ds_buf[rows, mine] = (p * (dp_all[h, rows] - delta) * scale).astype(BF)
                return carry

            lax.fori_loop(0, steps, close, 0)

        small = eye[:LANES, :LANES]
        vt = matmul(small, values[t], NT).astype(BF)
        both = matmul(vt, p_buf[...]).astype(BF)
        mixed[core, pl.ds(t * LANES, HEAD_DIM)] = both[:HEAD_DIM, :queries]
        mixed[core, pl.ds(t * LANES + HEAD_DIM, HEAD_DIM)] = both[HEAD_DIM:, queries:]
        piece = mixed.at[core, pl.ds(t * LANES, LANES)]
        mixes.append(remote(piece, piece, mix_send.at[t], mix_recv.at[t], sibling))
        kt = matmul(small, keys[t], NT).astype(BF)
        dq = matmul(kt, ds_buf[...])
        dqt = jnp.concatenate((dq[:HEAD_DIM, :queries], dq[HEAD_DIM:, queries:]), axis=0).astype(BF)
        dkv[:, pl.ds(0, LANES)] = matmul(ds_buf[...], qm[t]).astype(BF)
        dkv[:, pl.ds(LANES, LANES)] = matmul(p_buf[...], om[t]).astype(BF)
        for i in range(SIDE):
            rows = pl.ds(i * (width // SIDE), width // SIDE)
            q_part = matmul(xt[rows, pl.ds(0, queries)], dqt, NT).astype(BF)
            gq[t, i] = q_part.reshape(SIDE, rows1, LANES)
            kv = matmul(xt[rows], dkv[...])
            gk[t, i] = kv[:, :LANES].astype(BF).reshape(SIDE, rows1, LANES)
            v_part = kv[:, LANES:]
            for z in range(SIDE):
                turned = jnp.concatenate(
                    [v_part[(SIDE * y + z) * rows2 : (SIDE * y + z + 1) * rows2] for y in range(SIDE)], axis=0
                )
                gv[t, z, i] = turned.astype(BF)

    first, second, third, last = {}, {}, {}, {}
    for t in range(pairs):
        attend(t)
        first[t] = phase1(t)
        if t >= 1:
            second[t - 1] = phase2(t - 1, first[t - 1])
        if t >= 2:
            third[t - 2] = phase3(t - 2, second[t - 2])
    sent += mixes

    collect(mixes)
    channels = 2 * half
    all_mixed = mixed[...].reshape(channels, queries)
    orows = og.shape[3]
    orows2 = orows // SIDE
    wide = og.shape[4]
    for i in range(SIDE):
        part = matmul(all_mixed[i * (channels // SIDE) : (i + 1) * (channels // SIDE)], up[core])
        for u in range(2):
            og[u, i] = part[:, u * wide : (u + 1) * wide].astype(BF).reshape(SIDE, orows, wide)
        for y in range(SIDE):
            for z in range(SIDE):
                top = (SIDE * y + z) * orows2
                go_tmp[z, pl.ds(y * orows2, orows2)] = part[top : top + orows2, 2 * wide : 3 * wide]
        for z in range(SIDE):
            og[2, z, i] = go_tmp[z].astype(BF)
    ofirst = [
        send_three(0, lambda at: og.at[0, at], o1.at[0], s1, d1, 9 * pairs),
        send_three(1, lambda at: og.at[1, :, at], o1.at[1], s1, d1, 9 * pairs + 3),
        send_three(2, lambda at: og.at[2, at], o1.at[2], s1, d1, 9 * pairs + 6),
    ]
    oorders = ((0, 1, 2), (1, 0, 2), (2, 0, 1))

    t = pairs - 1
    third[t - 1] = phase3(t - 1, second[t - 1])
    second[t] = phase2(t, first[t])
    osecond = []
    for u in range(3):
        collect(ofirst[u])
        for j in range(SIDE):
            own = (og.at[0, xx, j], og.at[1, j, yy], og.at[2, zz, j])[u]
            total = own[...].astype(F32)
            for i in range(SIDE - 1):
                total = total + o1[u, i, j].astype(F32)
            po2[u, j] = total
        osecond.append(
            send_three(oorders[u][1], lambda at, u=u: po2.at[u, at], o2.at[u], s2, d2, 9 * pairs + 3 * u)
        )
    last[t - 2] = phase4(t - 2, third[t - 2])
    third[t] = phase3(t, second[t])
    othird = []
    for u in range(3):
        collect(osecond[u])
        total = po2[u, place_of[oorders[u][1]]] + o2[u, 0] + o2[u, 1] + o2[u, 2]
        for j in range(SIDE):
            po3[u, j] = total[j * orows2 : (j + 1) * orows2]
        othird.append(
            send_three(oorders[u][2], lambda at, u=u: po3.at[u, at], o3.at[u], s3, d3, 9 * pairs + 3 * u)
        )
    last[t - 1] = phase4(t - 1, third[t - 1])
    last[t] = phase4(t, third[t])
    for u in range(3):
        collect(othird[u])
        total = po3[u, place_of[oorders[u][2]]] + o3[u, 0] + o3[u, 1] + o3[u, 2]
        for j in range(2):
            fo_own[j, u] = total[j * (orows2 // 2) : (j + 1) * (orows2 // 2)]
    olast = remote(fo_own.at[1 - core], fo_sib, s4.at[pairs], d4.at[pairs], sibling)
    sent.append(olast)
    for u in range(3):
        lanes = pl.ds(pl.multiple_of(core * (width // 2) + u * wide, LANES), wide)
        out_o[:, lanes] = fo_own[core, u]
    for t in range(pairs):
        finish(t, last[t])
    olast.wait_recv()
    for u in range(3):
        lanes = pl.ds(pl.multiple_of((1 - core) * (width // 2) + u * wide, LANES), wide)
        out_o[:, lanes] = fo_sib[u]
    for copy in sent:
        copy.wait_send()


def shards(latents, norm_gain, w_query, w_key, w_value, w_out, kernel, partners, counts, cotangent):
    del counts
    views, _, columns, width = latents.shape[1:]
    inner = w_query.shape[1]
    half = inner // 2
    pairs = half // LANES
    groups = lax.axis_size("view")
    slots = groups - 1 + views
    slot_rows = 2 * columns
    key_rows = slots * slot_rows
    queries = views * slot_rows
    rows1 = width // 16
    orows = inner // 16
    wide = width // 6
    vm = pltpu.VMEM
    dma = pltpu.SemaphoreType.DMA
    in_vmem = pl.BlockSpec(memory_space=pltpu.VMEM)
    in_hbm = pl.BlockSpec(memory_space=pl.ANY)
    units = 9 * (pairs + 1)
    return pl.pallas_call(
        kernel_body,
        out_shape=(jax.ShapeDtypeStruct((rows1 // 8, inner), F32),) * 3
        + (jax.ShapeDtypeStruct((orows // 8, width), F32),),
        in_specs=[in_vmem] * 4 + [pl.BlockSpec(memory_space=pltpu.SMEM)] + [in_hbm] * 4,
        out_specs=(in_vmem,) * 4,
        scratch_shapes=[
            vm((slots, 2, columns, width), BF),
            vm((2, views, columns, width), BF),
            vm((groups, 8, LANES), jnp.int32),
            vm((groups, 8, LANES), jnp.int32),
            vm((groups - 1, columns, width), BF),
            vm((24, queries), F32),
            vm((width, half), BF),
            vm((width, 2 * half), BF),
            vm((half, width), BF),
            vm((width, key_rows), BF),
            vm((pairs, key_rows, LANES), BF),
            vm((pairs, key_rows, LANES), BF),
            vm((pairs, 2 * queries, LANES), BF),
            vm((pairs, 2 * queries, LANES), BF),
            vm((2, queries, width // 2), BF),
            vm((2 * pairs, key_rows, queries), F32),
            vm((2 * pairs, key_rows, queries), F32),
            vm((2 * pairs, 8, queries), F32),
            vm((key_rows, 2 * queries), BF),
            vm((key_rows, 2 * queries), BF),
            vm((key_rows, 2 * LANES), BF),
            vm((2, half, queries), BF),
            vm((pairs, SIDE, SIDE, rows1, LANES), BF),
            vm((pairs, SIDE, SIDE, rows1, LANES), BF),
            vm((pairs, SIDE, SIDE, rows1, LANES), BF),
            vm((pairs, 3, SIDE - 1, SIDE, rows1, LANES), BF),
            vm((pairs, 3, SIDE, rows1, LANES), F32),
            vm((pairs, 3, SIDE - 1, rows1, LANES), F32),
            vm((pairs, 3, SIDE, rows1 // 4, LANES), F32),
            vm((pairs, 3, SIDE - 1, rows1 // 4, LANES), F32),
            vm((2, pairs, 3, rows1 // 8, LANES), F32),
            vm((pairs, 3, rows1 // 8, LANES), F32),
            vm((3, SIDE, SIDE, orows, wide), BF),
            vm((SIDE, orows, wide), F32),
            vm((3, SIDE - 1, SIDE, orows, wide), BF),
            vm((3, SIDE, orows, wide), F32),
            vm((3, SIDE - 1, orows, wide), F32),
            vm((3, SIDE, orows // 4, wide), F32),
            vm((3, SIDE - 1, orows // 4, wide), F32),
            vm((2, 3, orows // 8, wide), F32),
            vm((3, orows // 8, wide), F32),
            dma((4,)), dma((2,)), dma((2,)),
            dma((groups,)), dma((groups,)), dma((groups,)), dma((groups,)), dma((groups,)), dma((groups,)),
            dma((pairs,)), dma((pairs,)),
            dma((units,)), dma((units,)), dma((units,)), dma((units,)), dma((units,)), dma((units,)),
            dma((pairs + 1,)), dma((pairs + 1,)),
        ],
        compiler_params=pltpu.CompilerParams(
            collective_id=0, has_side_effects=True, vmem_limit_bytes=VMEM_LIMIT
        ),
    )(
        latents[0, :, 0], norm_gain.reshape(1, width), cotangent[0, :, 0], kernel, partners[0],
        w_query, w_key, w_value, w_out,
    )


def solution(mesh):
    strips = P("scene", "view", "row", None, None)
    return jax.shard_map(
        shards,
        mesh=mesh,
        in_specs=(
            strips, P(), P(), P(), P(), P(), P(),
            P("scene", "view", None), P("scene", "view"), strips,
        ),
        out_specs=(P(("scene", "view", "row"), None),) * 4,
        check_vma=False,
    )
```

```python
import functools

import jax
import jax.numpy as jnp
from jax import lax
from jax.experimental import pallas as pl
from jax.experimental.pallas import tpu as pltpu
from jax.sharding import PartitionSpec as P

HEAD_DIM = 64
LANES = 128
EPSILON = 1e-06
SIDE = 4
OFFSETS = (
    (2, 2), (1, 2), (2, 1), (3, 2), (2, 3), (0, 2), (2, 0), (1, 1),
    (3, 3), (1, 3), (3, 1), (0, 1), (1, 0), (0, 3), (3, 0),
)
BATCHES = (4, 4, 4, 2, 1)
MESH = pl.DeviceIdType.MESH
VMEM_LIMIT = 62 * 1024 * 1024
NT = (((1,), (1,)), ((), ()))
NN = (((1,), (0,)), ((), ()))
BF = jnp.bfloat16
F32 = jnp.float32


def matmul(a, b, dims=NN):
    return lax.dot_general(a, b, dims, preferred_element_type=F32)


def kernel_body(
    lat, gain, cot, taps, partners, wq_hbm, wk_hbm, wv_hbm, wo_hbm,
    out_q, out_k, out_v, out_o,
    x, cot_all, ask, grant, outbuf, bias,
    wq, wkv, wo, xt, keys, values, qm, om, up, s_all, dp_all, tops, p_buf, ds_buf, dkv, mixed,
    gq, gk, gv, r1, p2, r2, p3, r3, f_own, f_sib,
    og, go_tmp, o1, po2, o2, po3, o3, fo_own, fo_sib,
    load_sem, own_send, own_recv, ask_send, ask_recv, out_send, out_recv, fwd_send, fwd_recv,
    mix_send, mix_recv, s1, d1, s2, d2, s3, d3, s4, d4,
):
    xx, me, core = lax.axis_index("scene"), lax.axis_index("view"), lax.axis_index("row")
    yy, zz = me // SIDE, lax.rem(me, SIDE)
    groups = SIDE * SIDE
    views, columns, width = lat.shape
    half = wq.shape[1]
    pairs = half // LANES
    slots = x.shape[0]
    slot_rows = 2 * columns
    key_rows = slots * slot_rows
    queries = views * slot_rows
    scale = HEAD_DIM ** (-0.5)
    sibling = (xx, me, 1 - core)

    def group_at(step, strip, sign):
        a, b = OFFSETS[step - 1]
        a, b = a + strip * (b - a), b + strip * (a - b)
        return lax.rem(yy + SIDE + sign * a, SIDE) * SIDE + lax.rem(zz + SIDE + sign * b, SIDE)

    def peer(step):
        return group_at(step, core, 1)

    def reverse(step):
        a, b = OFFSETS[step - 1]
        return OFFSETS.index(((SIDE - a) % SIDE, (SIDE - b) % SIDE)) + 1

    def along(axis, step):
        if axis == 0:
            at = lax.rem(xx + step, SIDE)
            return at, (at, me, core)
        if axis == 1:
            at = lax.rem(yy + step, SIDE)
            return at, (xx, at * SIDE + zz, core)
        at = lax.rem(zz + step, SIDE)
        return at, (xx, yy * SIDE + at, core)

    barrier = pltpu.get_barrier_semaphore()
    for step in range(1, groups):
        pl.semaphore_signal(barrier, inc=1, device_id=(xx, peer(step), core), device_id_type=MESH)
    for step in range(1, SIDE):
        pl.semaphore_signal(barrier, inc=1, device_id=along(0, step)[1], device_id_type=MESH)
    pl.semaphore_signal(barrier, inc=1, device_id=sibling, device_id_type=MESH)

    cols = pl.ds(pl.multiple_of(core * half, LANES), half)
    loads = [
        pltpu.make_async_copy(wq_hbm.at[:, cols], wq, load_sem.at[0]),
        pltpu.make_async_copy(wk_hbm.at[:, cols], wkv.at[:, pl.ds(0, half)], load_sem.at[1]),
        pltpu.make_async_copy(wv_hbm.at[:, cols], wkv.at[:, pl.ds(half, half)], load_sem.at[2]),
        pltpu.make_async_copy(wo_hbm.at[cols, :], wo, load_sem.at[3]),
    ]
    for copy in loads:
        copy.start()

    steps_of = lax.broadcasted_iota(jnp.int32, (groups, LANES), 0)
    first_of = jnp.full((groups, LANES), -2 * views, jnp.int32)
    for s in range(1, groups):
        first_of = jnp.where(steps_of == s, peer(s) * views, first_of)
    wanted = jnp.zeros((groups, LANES), jnp.int32)
    for v in range(views):
        for j in range(partners.shape[1]):
            local = partners[v, j] - first_of
            wanted = jnp.maximum(wanted, jnp.where((local >= 0) & (local < views), local, 0))
    for s in range(1, groups):
        ask[s] = jnp.broadcast_to(wanted[s : s + 1], ask.shape[1:])

    pl.semaphore_wait(barrier, groups + SIDE - 1)

    def remote(src, dst, send, recv, device):
        copy = pltpu.make_async_remote_copy(
            src_ref=src, dst_ref=dst, send_sem=send, recv_sem=recv, device_id=device, device_id_type=MESH
        )
        copy.start()
        return copy

    sent = []
    asks = [
        remote(ask.at[s], grant.at[s], ask_send.at[s], ask_recv.at[s], (xx, peer(s), core))
        for s in range(1, groups)
    ]
    own_cot = remote(cot, cot_all.at[core], own_send.at[1], own_recv.at[1], sibling)

    for v in range(views):
        rows = lat[v].astype(F32)
        mean = jnp.mean(rows * rows, -1, keepdims=True)
        x[v, core] = (rows * lax.rsqrt(mean + EPSILON) * gain[...].reshape(1, width)).astype(BF)
    cot_all[core] = cot[...]

    mine = x.at[pl.ds(0, views), core]
    own_x = remote(mine, mine, own_send.at[0], own_recv.at[0], sibling)

    blocks = []
    for s in range(1, groups):
        asks[reverse(s) - 1].wait_recv()
        want = grant[reverse(s)][0:1, 0:1]
        block = x[0, core]
        for v in range(1, views):
            block = jnp.where(want == v, x[v, core], block)
        outbuf[s - 1] = block
        blocks.append(
            remote(
                outbuf.at[s - 1], x.at[views - 1 + s, core], out_send.at[s], out_recv.at[s], (xx, peer(s), core)
            )
        )
    sent += asks + [own_x, own_cot] + blocks

    row_of = lax.broadcasted_iota(jnp.int32, (bias.shape[0], LANES), 0)
    first_of = jnp.full(row_of.shape, -2 * views, jnp.int32)
    for s in range(1, groups):
        for strip in range(2):
            first_of = jnp.where(row_of == 2 * (views - 1 + s) + strip, group_at(s, strip, -1) * views, first_of)
    lane_of = lax.broadcasted_iota(jnp.int32, (bias.shape[0], LANES), 1)
    seen = []
    for v in range(views):
        hit = jnp.where(row_of // 2 == v, 1, 0)
        for j in range(partners.shape[1]):
            number = partners[v, j]
            local = number - first_of
            hit = jnp.where((local >= 0) & (local < views) & (number >= 0), 1, hit)
        seen.append(jnp.where(hit > 0, 0.0, -1e30))
    for part in range(views // 2):
        bias[:, pl.ds(part * LANES, LANES)] = jnp.where(
            lane_of < slot_rows, seen[2 * part], seen[2 * part + 1]
        )

    own_cot.wait_recv()
    chunk = 2 * LANES
    place = lax.broadcasted_iota(jnp.int32, (columns, chunk), 0)

    def conv_view(view, carry):
        for part in range(width // chunk):
            lanes = pl.ds(part * chunk, chunk)
            kern = taps[:, lanes].astype(F32)
            shifted = []
            for strip in range(2):
                mid = cot_all[strip, view, :, lanes].astype(F32)
                after = jnp.where(place == columns - 1, 0.0, pltpu.roll(mid, columns - 1, 0))
                before = jnp.where(place == 0, 0.0, pltpu.roll(mid, 1, 0))
                shifted.append((after, mid, before))
            for strip in range(2):
                total = shifted[strip][1]
                for a, source in ((1, strip), (2 * strip, 1 - strip)):
                    for b in range(3):
                        total = total + kern[3 * a + b : 3 * a + b + 1] * shifted[source][b]
                side = part * chunk // (width // 2)
                rows = pl.ds(pl.multiple_of(view * slot_rows + strip * columns, columns), columns)
                up[side, rows, pl.ds(part * chunk - side * (width // 2), chunk)] = total.astype(BF)
        return carry

    lax.fori_loop(0, views, conv_view, 0)

    for copy in loads:
        copy.wait()

    lane = lax.broadcasted_iota(jnp.int32, (queries, LANES), 1)

    def split_heads(out, rows_f):
        rounded = rows_f.astype(BF).astype(F32)
        for pair in range(pairs):
            block = rounded[:, pair * LANES : (pair + 1) * LANES]
            out[pair, pl.ds(0, queries)] = jnp.where(lane < HEAD_DIM, block, 0.0).astype(BF)
            out[pair, pl.ds(queries, queries)] = jnp.where(lane < HEAD_DIM, 0.0, block).astype(BF)

    split_heads(
        om,
        matmul(up[0], wo[:, pl.ds(0, width // 2)], NT) + matmul(up[1], wo[:, pl.ds(width // 2, width // 2)], NT),
    )
    own_x.wait_recv()
    split_heads(qm, matmul(x[pl.ds(0, views)].reshape(queries, width), wq[...]))

    tile = 2 * LANES
    eye = (
        lax.broadcasted_iota(jnp.int32, (tile, tile), 0) == lax.broadcasted_iota(jnp.int32, (tile, tile), 1)
    ).astype(F32).astype(BF)

    def fold(v, op):
        return op(v.reshape(v.shape[0] // 8, 8, v.shape[1]), axis=0)

    def batch(first, count):
        rows = pl.ds(first * slot_rows, count * slot_rows)
        flat = x[pl.ds(first, count)].reshape(count * slot_rows, width)
        out = matmul(flat, wkv[...]).astype(BF)
        for pair in range(pairs):
            keys[pair, rows] = out[:, pair * LANES : (pair + 1) * LANES]
            values[pair, rows] = out[:, half + pair * LANES : half + (pair + 1) * LANES]

        def turn(j, carry):
            lanes = pl.ds(pl.multiple_of(j * tile, tile), tile)
            part = x[pl.ds(first, count), :, :, lanes].reshape(count * slot_rows, tile)
            xt[lanes, rows] = matmul(eye, part, NT).astype(BF)
            return carry

        lax.fori_loop(0, width // tile, turn, 0)

        def score(pair, carry):
            for head in range(2):
                mine = pl.ds(head * queries, queries)
                s = matmul(keys[pair, rows], qm[pair, mine], NT) * scale
                top = jnp.full((8, queries), -3e38, F32) if first == 0 else tops[2 * pair + head]
                for i in range(2 * count):
                    part = s[i * columns : (i + 1) * columns] + bias[pl.ds(2 * first + i, 1)]
                    s_all[2 * pair + head, pl.ds(first * slot_rows + i * columns, columns)] = part
                    top = jnp.maximum(top, fold(part, jnp.max))
                tops[2 * pair + head] = top
                dp_all[2 * pair + head, rows] = matmul(values[pair, rows], om[pair, mine], NT)
            return carry

        lax.fori_loop(0, pairs, score, 0)

    parts = [(views + sum(BATCHES[:i]), count) for i, count in enumerate(BATCHES)]
    before = (0, views)
    forwards = []
    for first, count in parts:
        fresh = []
        for slot in range(first, first + count):
            s = slot - views + 1
            blocks[s - 1].wait_recv()
            place_x = x.at[slot, core]
            fresh.append(remote(place_x, place_x, fwd_send.at[s], fwd_recv.at[s], sibling))
        batch(*before)
        for copy in fresh:
            copy.wait_recv()
        forwards += fresh
        before = (first, count)
    batch(*before)
    sent += forwards

    def send_three(axis, source, target, send, recv, base):
        copies = []
        for step in (2, 1, 3):
            at, device = along(axis, step)
            copies.append(
                remote(source(at), target.at[step - 1], send.at[base + step - 1], recv.at[base + step - 1], device)
            )
        sent.extend(copies)
        return copies

    def collect(copies):
        for copy in copies:
            copy.wait_recv()

    place_of = (xx, yy, zz)
    orders = ((0, 1, 2), (1, 2, 0), (2, 0, 1))
    rows1 = gq.shape[3]
    rows2 = rows1 // SIDE

    def phase1(t):
        return [
            send_three(0, lambda at: gq.at[t, at], r1.at[t, 0], s1, d1, 9 * t),
            send_three(1, lambda at: gk.at[t, :, at], r1.at[t, 1], s1, d1, 9 * t + 3),
            send_three(2, lambda at: gv.at[t, at], r1.at[t, 2], s1, d1, 9 * t + 6),
        ]

    def phase2(t, arrived):
        copies = []
        for m in range(3):
            collect(arrived[m])
            totals = []
            for j in range(SIDE):
                own = (gq.at[t, xx, j], gk.at[t, j, yy], gv.at[t, zz, j])[m]
                total = own[...].astype(F32)
                for i in range(SIDE - 1):
                    total = total + r1[t, m, i, j].astype(F32)
                totals.append(total)
            if m == 1:
                totals = [
                    jnp.concatenate([total[k * rows2 : (k + 1) * rows2] for total in totals], axis=0)
                    for k in range(SIDE)
                ]
            for j in range(SIDE):
                p2[t, m, j] = totals[j].astype(BF)
            copies.append(
                send_three(orders[m][1], lambda at, m=m: p2.at[t, m, at], r2.at[t, m], s2, d2, 9 * t + 3 * m)
            )
        return copies

    def phase3(t, arrived):
        copies = []
        for m in range(3):
            collect(arrived[m])
            total = p2[t, m, place_of[orders[m][1]]].astype(F32)
            for i in range(SIDE - 1):
                total = total + r2[t, m, i].astype(F32)
            for j in range(SIDE):
                p3[t, m, j] = total[j * rows2 : (j + 1) * rows2]
            copies.append(
                send_three(orders[m][2], lambda at, m=m: p3.at[t, m, at], r3.at[t, m], s3, d3, 9 * t + 3 * m)
            )
        return copies

    outs = (out_q, out_k, out_v)

    def phase4(t, arrived):
        for m in range(3):
            collect(arrived[m])
            total = p3[t, m, place_of[orders[m][2]]] + r3[t, m, 0] + r3[t, m, 1] + r3[t, m, 2]
            for j in range(2):
                f_own[j, t, m] = total[j * (rows2 // 2) : (j + 1) * (rows2 // 2)]
            lanes = pl.ds(pl.multiple_of(core * half + t * LANES, LANES), LANES)
            outs[m][:, lanes] = f_own[core, t, m]
        copy = remote(f_own.at[1 - core, t], f_sib.at[t], s4.at[t], d4.at[t], sibling)
        sent.append(copy)
        return copy

    def finish(t, copy):
        copy.wait_recv()
        lanes = pl.ds(pl.multiple_of((1 - core) * half + t * LANES, LANES), LANES)
        for m in range(3):
            outs[m][:, lanes] = f_sib[t, m]

    step = 64
    steps = key_rows // step
    mixes = []

    def attend(t):
        for head in range(2):
            h = 2 * t + head
            mine = pl.ds(head * queries, queries)
            top = jnp.max(tops[h], axis=0, keepdims=True)

            def weigh(i, sums, h=h, top=top):
                rows = pl.ds(pl.multiple_of(i * step, step), step)
                e = jnp.exp(s_all[h, rows] - top)
                s_all[h, rows] = e
                return sums[0] + fold(e, jnp.sum), sums[1] + fold(e * dp_all[h, rows], jnp.sum)

            zero = jnp.zeros((8, queries), F32)
            total, delta = lax.fori_loop(0, steps, weigh, (zero, zero))
            inverse = 1.0 / jnp.sum(total, axis=0, keepdims=True)
            delta = jnp.sum(delta, axis=0, keepdims=True) * inverse

            def close(i, carry, h=h, mine=mine, inverse=inverse, delta=delta):
                rows = pl.ds(pl.multiple_of(i * step, step), step)
                p = s_all[h, rows] * inverse
                p_buf[rows, mine] = p.astype(BF)
                ds_buf[rows, mine] = (p * (dp_all[h, rows] - delta) * scale).astype(BF)
                return carry

            lax.fori_loop(0, steps, close, 0)

        small = eye[:LANES, :LANES]
        vt = matmul(small, values[t], NT).astype(BF)
        both = matmul(vt, p_buf[...]).astype(BF)
        mixed[core, pl.ds(t * LANES, HEAD_DIM)] = both[:HEAD_DIM, :queries]
        mixed[core, pl.ds(t * LANES + HEAD_DIM, HEAD_DIM)] = both[HEAD_DIM:, queries:]
        piece = mixed.at[core, pl.ds(t * LANES, LANES)]
        mixes.append(remote(piece, piece, mix_send.at[t], mix_recv.at[t], sibling))
        kt = matmul(small, keys[t], NT).astype(BF)
        dq = matmul(kt, ds_buf[...])
        dqt = jnp.concatenate((dq[:HEAD_DIM, :queries], dq[HEAD_DIM:, queries:]), axis=0).astype(BF)
        dkv[:, pl.ds(0, LANES)] = matmul(ds_buf[...], qm[t]).astype(BF)
        dkv[:, pl.ds(LANES, LANES)] = matmul(p_buf[...], om[t]).astype(BF)
        for i in range(SIDE):
            rows = pl.ds(i * (width // SIDE), width // SIDE)
            q_part = matmul(xt[rows, pl.ds(0, queries)], dqt, NT).astype(BF)
            gq[t, i] = q_part.reshape(SIDE, rows1, LANES)
            kv = matmul(xt[rows], dkv[...])
            gk[t, i] = kv[:, :LANES].astype(BF).reshape(SIDE, rows1, LANES)
            v_part = kv[:, LANES:]
            for z in range(SIDE):
                turned = jnp.concatenate(
                    [v_part[(SIDE * y + z) * rows2 : (SIDE * y + z + 1) * rows2] for y in range(SIDE)], axis=0
                )
                gv[t, z, i] = turned.astype(BF)

    first, second, third, last = {}, {}, {}, {}
    for t in range(pairs):
        attend(t)
        first[t] = phase1(t)
        if t >= 1:
            second[t - 1] = phase2(t - 1, first[t - 1])
        if t >= 2:
            third[t - 2] = phase3(t - 2, second[t - 2])
    sent += mixes

    collect(mixes)
    channels = 2 * half
    all_mixed = mixed[...].reshape(channels, queries)
    orows = og.shape[3]
    orows2 = orows // SIDE
    wide = og.shape[4]
    for i in range(SIDE):
        part = matmul(all_mixed[i * (channels // SIDE) : (i + 1) * (channels // SIDE)], up[core])
        for u in range(2):
            og[u, i] = part[:, u * wide : (u + 1) * wide].astype(BF).reshape(SIDE, orows, wide)
        for y in range(SIDE):
            for z in range(SIDE):
                top = (SIDE * y + z) * orows2
                go_tmp[z, pl.ds(y * orows2, orows2)] = part[top : top + orows2, 2 * wide : 3 * wide]
        for z in range(SIDE):
            og[2, z, i] = go_tmp[z].astype(BF)
    ofirst = [
        send_three(0, lambda at: og.at[0, at], o1.at[0], s1, d1, 9 * pairs),
        send_three(1, lambda at: og.at[1, :, at], o1.at[1], s1, d1, 9 * pairs + 3),
        send_three(2, lambda at: og.at[2, at], o1.at[2], s1, d1, 9 * pairs + 6),
    ]
    oorders = ((0, 1, 2), (1, 0, 2), (2, 0, 1))

    t = pairs - 1
    third[t - 1] = phase3(t - 1, second[t - 1])
    second[t] = phase2(t, first[t])
    osecond = []
    for u in range(3):
        collect(ofirst[u])
        for j in range(SIDE):
            own = (og.at[0, xx, j], og.at[1, j, yy], og.at[2, zz, j])[u]
            total = own[...].astype(F32)
            for i in range(SIDE - 1):
                total = total + o1[u, i, j].astype(F32)
            po2[u, j] = total.astype(BF)
        osecond.append(
            send_three(oorders[u][1], lambda at, u=u: po2.at[u, at], o2.at[u], s2, d2, 9 * pairs + 3 * u)
        )
    last[t - 2] = phase4(t - 2, third[t - 2])
    third[t] = phase3(t, second[t])
    othird = []
    for u in range(3):
        collect(osecond[u])
        total = po2[u, place_of[oorders[u][1]]].astype(F32)
        for i in range(SIDE - 1):
            total = total + o2[u, i].astype(F32)
        for j in range(SIDE):
            po3[u, j] = total[j * orows2 : (j + 1) * orows2]
        othird.append(
            send_three(oorders[u][2], lambda at, u=u: po3.at[u, at], o3.at[u], s3, d3, 9 * pairs + 3 * u)
        )
    last[t - 1] = phase4(t - 1, third[t - 1])
    last[t] = phase4(t, third[t])
    for u in range(3):
        collect(othird[u])
        total = po3[u, place_of[oorders[u][2]]] + o3[u, 0] + o3[u, 1] + o3[u, 2]
        for j in range(2):
            fo_own[j, u] = total[j * (orows2 // 2) : (j + 1) * (orows2 // 2)]
    olast = remote(fo_own.at[1 - core], fo_sib, s4.at[pairs], d4.at[pairs], sibling)
    sent.append(olast)
    for u in range(3):
        lanes = pl.ds(pl.multiple_of(core * (width // 2) + u * wide, LANES), wide)
        out_o[:, lanes] = fo_own[core, u]
    for t in range(pairs):
        finish(t, last[t])
    olast.wait_recv()
    for u in range(3):
        lanes = pl.ds(pl.multiple_of((1 - core) * (width // 2) + u * wide, LANES), wide)
        out_o[:, lanes] = fo_sib[u]
    for copy in sent:
        copy.wait_send()


def leave_kernel(*refs):
    count = len(refs) // 2
    for source, target in zip(refs[:count], refs[count:]):
        target[...] = source[...]


def leave(*results):
    return pl.pallas_call(
        leave_kernel,
        out_shape=tuple(jax.ShapeDtypeStruct(r.shape, r.dtype) for r in results),
    )(*results)


def shards(latents, norm_gain, w_query, w_key, w_value, w_out, kernel, partners, counts, cotangent):
    del counts
    views, _, columns, width = latents.shape[1:]
    inner = w_query.shape[1]
    half = inner // 2
    pairs = half // LANES
    groups = lax.axis_size("view")
    slots = groups - 1 + views
    slot_rows = 2 * columns
    key_rows = slots * slot_rows
    queries = views * slot_rows
    rows1 = width // 16
    orows = inner // 16
    wide = width // 6
    vm = pltpu.VMEM
    dma = pltpu.SemaphoreType.DMA
    in_vmem = pl.BlockSpec(memory_space=pltpu.VMEM)
    in_hbm = pl.BlockSpec(memory_space=pl.ANY)
    units = 9 * (pairs + 1)
    results = pl.pallas_call(
        kernel_body,
        out_shape=(jax.ShapeDtypeStruct((rows1 // 8, inner), F32),) * 3
        + (jax.ShapeDtypeStruct((orows // 8, width), F32),),
        in_specs=[in_vmem] * 4 + [pl.BlockSpec(memory_space=pltpu.SMEM)] + [in_hbm] * 4,
        out_specs=(in_vmem,) * 4,
        scratch_shapes=[
            vm((slots, 2, columns, width), BF),
            vm((2, views, columns, width), BF),
            vm((groups, 8, LANES), jnp.int32),
            vm((groups, 8, LANES), jnp.int32),
            vm((groups - 1, columns, width), BF),
            vm((48, queries), F32),
            vm((width, half), BF),
            vm((width, 2 * half), BF),
            vm((half, width), BF),
            vm((width, key_rows), BF),
            vm((pairs, key_rows, LANES), BF),
            vm((pairs, key_rows, LANES), BF),
            vm((pairs, 2 * queries, LANES), BF),
            vm((pairs, 2 * queries, LANES), BF),
            vm((2, queries, width // 2), BF),
            vm((2 * pairs, key_rows, queries), F32),
            vm((2 * pairs, key_rows, queries), F32),
            vm((2 * pairs, 8, queries), F32),
            vm((key_rows, 2 * queries), BF),
            vm((key_rows, 2 * queries), BF),
            vm((key_rows, 2 * LANES), BF),
            vm((2, half, queries), BF),
            vm((pairs, SIDE, SIDE, rows1, LANES), BF),
            vm((pairs, SIDE, SIDE, rows1, LANES), BF),
            vm((pairs, SIDE, SIDE, rows1, LANES), BF),
            vm((pairs, 3, SIDE - 1, SIDE, rows1, LANES), BF),
            vm((pairs, 3, SIDE, rows1, LANES), BF),
            vm((pairs, 3, SIDE - 1, rows1, LANES), BF),
            vm((pairs, 3, SIDE, rows1 // 4, LANES), F32),
            vm((pairs, 3, SIDE - 1, rows1 // 4, LANES), F32),
            vm((2, pairs, 3, rows1 // 8, LANES), F32),
            vm((pairs, 3, rows1 // 8, LANES), F32),
            vm((3, SIDE, SIDE, orows, wide), BF),
            vm((SIDE, orows, wide), F32),
            vm((3, SIDE - 1, SIDE, orows, wide), BF),
            vm((3, SIDE, orows, wide), BF),
            vm((3, SIDE - 1, orows, wide), BF),
            vm((3, SIDE, orows // 4, wide), F32),
            vm((3, SIDE - 1, orows // 4, wide), F32),
            vm((2, 3, orows // 8, wide), F32),
            vm((3, orows // 8, wide), F32),
            dma((4,)), dma((2,)), dma((2,)),
            dma((groups,)), dma((groups,)), dma((groups,)), dma((groups,)), dma((groups,)), dma((groups,)),
            dma((pairs,)), dma((pairs,)),
            dma((units,)), dma((units,)), dma((units,)), dma((units,)), dma((units,)), dma((units,)),
            dma((pairs + 1,)), dma((pairs + 1,)),
        ],
        compiler_params=pltpu.CompilerParams(
            collective_id=0, has_side_effects=True, vmem_limit_bytes=VMEM_LIMIT
        ),
    )(
        latents[0, :, 0], norm_gain, cotangent[0, :, 0], kernel, partners[0],
        w_query, w_key, w_value, w_out,
    )
    return leave(*results)


def solution(mesh):
    strips = P("scene", "view", "row", None, None)
    return jax.shard_map(
        shards,
        mesh=mesh,
        in_specs=(
            strips, P(), P(), P(), P(), P(), P(),
            P("scene", "view", None), P("scene", "view"), strips,
        ),
        out_specs=(P(("scene", "view", "row"), None),) * 4,
        check_vma=False,
    )
```

```python
import functools

import jax
import jax.numpy as jnp
from jax import lax
from jax.experimental import pallas as pl
from jax.experimental.pallas import tpu as pltpu
from jax.sharding import PartitionSpec as P

HEAD_DIM = 64
LANES = 128
EPSILON = 1e-06
SIDE = 4
OFFSETS = (
    (0, 1), (1, 0), (0, 3), (3, 0), (2, 2), (1, 1), (3, 3), (0, 2),
    (2, 0), (1, 3), (3, 1), (1, 2), (2, 1), (3, 2), (2, 3),
)
BATCHES = (4, 4, 4, 2, 1)
MESH = pl.DeviceIdType.MESH
VMEM_LIMIT = 62 * 1024 * 1024
NT = (((1,), (1,)), ((), ()))
NN = (((1,), (0,)), ((), ()))
BF = jnp.bfloat16
F32 = jnp.float32


def matmul(a, b, dims=NN):
    return lax.dot_general(a, b, dims, preferred_element_type=F32)


def kernel_body(
    lat, gain, cot, taps, partners, wq_hbm, wk_hbm, wv_hbm, wo_hbm,
    out_q, out_k, out_v, out_o,
    x, cot_all, ask, grant, outbuf, bias,
    wq, wkv, wo, xt, keys, values, qm, om, qmt, omt, up, s_all, dp_all, tops, p_buf, ds_buf, dkv, mixed,
    gq, gk, gv, r1, p2, r2, p3, r3, f_own, f_sib,
    og, go_tmp, o1, po2, o2, po3, o3, fo_own, fo_sib,
    load_sem, own_send, own_recv, ask_send, ask_recv, out_send, out_recv, fwd_send, fwd_recv,
    mix_send, mix_recv, s1, d1, s2, d2, s3, d3, s4, d4,
):
    xx, me, core = lax.axis_index("scene"), lax.axis_index("view"), lax.axis_index("row")
    yy, zz = me // SIDE, lax.rem(me, SIDE)
    groups = SIDE * SIDE
    views, columns, width = lat.shape
    half = wq.shape[1]
    pairs = half // LANES
    slots = x.shape[0]
    slot_rows = 2 * columns
    key_rows = slots * slot_rows
    queries = views * slot_rows
    scale = HEAD_DIM ** (-0.5)
    sibling = (xx, me, 1 - core)

    def group_at(step, strip, sign):
        a, b = OFFSETS[step - 1]
        a, b = a + strip * (b - a), b + strip * (a - b)
        return lax.rem(yy + SIDE + sign * a, SIDE) * SIDE + lax.rem(zz + SIDE + sign * b, SIDE)

    def peer(step):
        return group_at(step, core, 1)

    def reverse(step):
        a, b = OFFSETS[step - 1]
        return OFFSETS.index(((SIDE - a) % SIDE, (SIDE - b) % SIDE)) + 1

    def along(axis, step):
        if axis == 0:
            at = lax.rem(xx + step, SIDE)
            return at, (at, me, core)
        if axis == 1:
            at = lax.rem(yy + step, SIDE)
            return at, (xx, at * SIDE + zz, core)
        at = lax.rem(zz + step, SIDE)
        return at, (xx, yy * SIDE + at, core)

    barrier = pltpu.get_barrier_semaphore()
    for step in range(1, groups):
        pl.semaphore_signal(barrier, inc=1, device_id=(xx, peer(step), core), device_id_type=MESH)
    for step in range(1, SIDE):
        pl.semaphore_signal(barrier, inc=1, device_id=along(0, step)[1], device_id_type=MESH)
    pl.semaphore_signal(barrier, inc=1, device_id=sibling, device_id_type=MESH)

    cols = pl.ds(pl.multiple_of(core * half, LANES), half)
    loads = [
        pltpu.make_async_copy(wq_hbm.at[:, cols], wq, load_sem.at[0]),
        pltpu.make_async_copy(wk_hbm.at[:, cols], wkv.at[:, pl.ds(0, half)], load_sem.at[1]),
        pltpu.make_async_copy(wv_hbm.at[:, cols], wkv.at[:, pl.ds(half, half)], load_sem.at[2]),
        pltpu.make_async_copy(wo_hbm.at[cols, :], wo, load_sem.at[3]),
    ]
    for copy in loads:
        copy.start()

    steps_of = lax.broadcasted_iota(jnp.int32, (groups, LANES), 0)
    first_of = jnp.full((groups, LANES), -2 * views, jnp.int32)
    for s in range(1, groups):
        first_of = jnp.where(steps_of == s, peer(s) * views, first_of)
    wanted = jnp.zeros((groups, LANES), jnp.int32)
    for v in range(views):
        for j in range(partners.shape[1]):
            local = partners[v, j] - first_of
            wanted = jnp.maximum(wanted, jnp.where((local >= 0) & (local < views), local, 0))
    for s in range(1, groups):
        ask[s] = jnp.broadcast_to(wanted[s : s + 1], ask.shape[1:])

    pl.semaphore_wait(barrier, groups + SIDE - 1)

    def remote(src, dst, send, recv, device):
        copy = pltpu.make_async_remote_copy(
            src_ref=src, dst_ref=dst, send_sem=send, recv_sem=recv, device_id=device, device_id_type=MESH
        )
        copy.start()
        return copy

    sent = []
    asks = [
        remote(ask.at[s], grant.at[s], ask_send.at[s], ask_recv.at[s], (xx, peer(s), core))
        for s in range(1, groups)
    ]
    own_cot = remote(cot, cot_all.at[core], own_send.at[1], own_recv.at[1], sibling)

    for v in range(views):
        rows = lat[v].astype(F32)
        mean = jnp.mean(rows * rows, -1, keepdims=True)
        x[v, core] = (rows * lax.rsqrt(mean + EPSILON) * gain[...].reshape(1, width)).astype(BF)
    cot_all[core] = cot[...]

    mine = x.at[pl.ds(0, views), core]
    own_x = remote(mine, mine, own_send.at[0], own_recv.at[0], sibling)

    blocks = []
    for s in range(1, groups):
        asks[reverse(s) - 1].wait_recv()
        want = grant[reverse(s)][0:1, 0:1]
        block = x[0, core]
        for v in range(1, views):
            block = jnp.where(want == v, x[v, core], block)
        outbuf[s - 1] = block
        blocks.append(
            remote(
                outbuf.at[s - 1], x.at[views - 1 + s, core], out_send.at[s], out_recv.at[s], (xx, peer(s), core)
            )
        )
    sent += asks + [own_x, own_cot] + blocks

    row_of = lax.broadcasted_iota(jnp.int32, (bias.shape[0], LANES), 0)
    first_of = jnp.full(row_of.shape, -2 * views, jnp.int32)
    for s in range(1, groups):
        for strip in range(2):
            first_of = jnp.where(row_of == 2 * (views - 1 + s) + strip, group_at(s, strip, -1) * views, first_of)
    lane_of = lax.broadcasted_iota(jnp.int32, (bias.shape[0], LANES), 1)
    seen = []
    for v in range(views):
        hit = jnp.where(row_of // 2 == v, 1, 0)
        for j in range(partners.shape[1]):
            number = partners[v, j]
            local = number - first_of
            hit = jnp.where((local >= 0) & (local < views) & (number >= 0), 1, hit)
        seen.append(jnp.where(hit > 0, 0.0, -1e30))
    for part in range(views // 2):
        both = jnp.where(lane_of < slot_rows, seen[2 * part], seen[2 * part + 1])
        for head in range(2):
            bias[:, pl.ds(head * queries + part * LANES, LANES)] = both

    own_cot.wait_recv()
    chunk = 2 * LANES
    place = lax.broadcasted_iota(jnp.int32, (columns, chunk), 0)

    def conv_view(view, carry):
        for part in range(width // chunk):
            lanes = pl.ds(part * chunk, chunk)
            kern = taps[:, lanes].astype(F32)
            shifted = []
            for strip in range(2):
                mid = cot_all[strip, view, :, lanes].astype(F32)
                after = jnp.where(place == columns - 1, 0.0, pltpu.roll(mid, columns - 1, 0))
                before = jnp.where(place == 0, 0.0, pltpu.roll(mid, 1, 0))
                shifted.append((after, mid, before))
            for strip in range(2):
                total = shifted[strip][1]
                for a, source in ((1, strip), (2 * strip, 1 - strip)):
                    for b in range(3):
                        total = total + kern[3 * a + b : 3 * a + b + 1] * shifted[source][b]
                side = part * chunk // (width // 2)
                rows = pl.ds(pl.multiple_of(view * slot_rows + strip * columns, columns), columns)
                up[side, rows, pl.ds(part * chunk - side * (width // 2), chunk)] = total.astype(BF)
        return carry

    lax.fori_loop(0, views, conv_view, 0)

    for copy in loads:
        copy.wait()

    lane = lax.broadcasted_iota(jnp.int32, (queries, LANES), 1)
    sublane = lax.broadcasted_iota(jnp.int32, (LANES, queries), 0)

    def split_heads(out, turned, rows_f):
        rounded = rows_f.astype(BF).astype(F32)
        for pair in range(pairs):
            block = rounded[:, pair * LANES : (pair + 1) * LANES]
            out[pair, pl.ds(0, queries)] = jnp.where(lane < HEAD_DIM, block, 0.0).astype(BF)
            out[pair, pl.ds(queries, queries)] = jnp.where(lane < HEAD_DIM, 0.0, block).astype(BF)
            block = block.T
            turned[pair, :, pl.ds(0, queries)] = jnp.where(sublane < HEAD_DIM, block, 0.0).astype(BF)
            turned[pair, :, pl.ds(queries, queries)] = jnp.where(sublane < HEAD_DIM, 0.0, block).astype(BF)

    split_heads(
        om, omt,
        matmul(up[0], wo[:, pl.ds(0, width // 2)], NT) + matmul(up[1], wo[:, pl.ds(width // 2, width // 2)], NT),
    )
    own_x.wait_recv()
    split_heads(qm, qmt, matmul(x[pl.ds(0, views)].reshape(queries, width), wq[...]))

    tile = 2 * LANES

    def fold(v, op):
        return op(v.reshape(v.shape[0] // 8, 8, v.shape[1]), axis=0)

    def batch(first, count):
        rows = pl.ds(first * slot_rows, count * slot_rows)
        flat = x[pl.ds(first, count)].reshape(count * slot_rows, width)
        out = matmul(flat, wkv[...]).astype(BF)
        for pair in range(pairs):
            keys[pair, rows] = out[:, pair * LANES : (pair + 1) * LANES]
            values[pair, rows] = out[:, half + pair * LANES : half + (pair + 1) * LANES]

        for j in range(width // tile):
            lanes = pl.ds(j * tile, tile)
            xt[lanes, rows] = flat[:, j * tile : (j + 1) * tile].T

        for pair in range(pairs):
            s = matmul(keys[pair, rows], qmt[pair]) * scale
            top = jnp.full((8, 2 * queries), -3e38, F32) if first == 0 else tops[pair]
            for i in range(2 * count):
                part = s[i * columns : (i + 1) * columns] + bias[pl.ds(2 * first + i, 1)]
                s_all[pair, pl.ds(first * slot_rows + i * columns, columns)] = part
                top = jnp.maximum(top, fold(part, jnp.max))
            tops[pair] = top
            dp_all[pair, rows] = matmul(values[pair, rows], omt[pair])

    parts = [(views + sum(BATCHES[:i]), count) for i, count in enumerate(BATCHES)]
    before = None
    batch(0, views)
    forwards = []
    for first, count in parts:
        fresh = []
        for slot in range(first, first + count):
            s = slot - views + 1
            blocks[s - 1].wait_recv()
            place_x = x.at[slot, core]
            fresh.append(remote(place_x, place_x, fwd_send.at[s], fwd_recv.at[s], sibling))
        if before:
            batch(*before)
        for copy in fresh:
            copy.wait_recv()
        forwards += fresh
        before = (first, count)
    batch(*before)
    sent += forwards

    def send_three(axis, source, target, send, recv, base):
        copies = []
        for step in (2, 1, 3):
            at, device = along(axis, step)
            copies.append(
                remote(source(at), target.at[step - 1], send.at[base + step - 1], recv.at[base + step - 1], device)
            )
        sent.extend(copies)
        return copies

    def collect(copies):
        for copy in copies:
            copy.wait_recv()

    place_of = (xx, yy, zz)
    orders = ((0, 1, 2), (1, 2, 0), (2, 0, 1))
    rows1 = gq.shape[3]
    rows2 = rows1 // SIDE

    def phase1(t):
        return [
            send_three(0, lambda at: gq.at[t, at], r1.at[t, 0], s1, d1, 9 * t),
            send_three(1, lambda at: gk.at[t, :, at], r1.at[t, 1], s1, d1, 9 * t + 3),
            send_three(2, lambda at: gv.at[t, at], r1.at[t, 2], s1, d1, 9 * t + 6),
        ]

    def phase2(t, arrived):
        copies = []
        for m in range(3):
            collect(arrived[m])
            totals = []
            for j in range(SIDE):
                own = (gq.at[t, xx, j], gk.at[t, j, yy], gv.at[t, zz, j])[m]
                total = own[...].astype(F32)
                for i in range(SIDE - 1):
                    total = total + r1[t, m, i, j].astype(F32)
                totals.append(total)
            if m == 1:
                totals = [
                    jnp.concatenate([total[k * rows2 : (k + 1) * rows2] for total in totals], axis=0)
                    for k in range(SIDE)
                ]
            for j in range(SIDE):
                p2[t, m, j] = totals[j].astype(BF)
            copies.append(
                send_three(orders[m][1], lambda at, m=m: p2.at[t, m, at], r2.at[t, m], s2, d2, 9 * t + 3 * m)
            )
        return copies

    def phase3(t, arrived):
        copies = []
        for m in range(3):
            collect(arrived[m])
            total = p2[t, m, place_of[orders[m][1]]].astype(F32)
            for i in range(SIDE - 1):
                total = total + r2[t, m, i].astype(F32)
            for j in range(SIDE):
                p3[t, m, j] = total[j * rows2 : (j + 1) * rows2]
            copies.append(
                send_three(orders[m][2], lambda at, m=m: p3.at[t, m, at], r3.at[t, m], s3, d3, 9 * t + 3 * m)
            )
        return copies

    outs = (out_q, out_k, out_v)

    def phase4(t, arrived):
        for m in range(3):
            collect(arrived[m])
            total = p3[t, m, place_of[orders[m][2]]] + r3[t, m, 0] + r3[t, m, 1] + r3[t, m, 2]
            for j in range(2):
                f_own[j, t, m] = total[j * (rows2 // 2) : (j + 1) * (rows2 // 2)]
            lanes = pl.ds(pl.multiple_of(core * half + t * LANES, LANES), LANES)
            outs[m][:, lanes] = f_own[core, t, m]
        copy = remote(f_own.at[1 - core, t], f_sib.at[t], s4.at[t], d4.at[t], sibling)
        sent.append(copy)
        return copy

    def finish(t, copy):
        copy.wait_recv()
        lanes = pl.ds(pl.multiple_of((1 - core) * half + t * LANES, LANES), LANES)
        for m in range(3):
            outs[m][:, lanes] = f_sib[t, m]

    step = 64
    steps = key_rows // step
    mixes = []

    def attend(t):
        top = jnp.max(tops[t], axis=0, keepdims=True)

        def weigh(i, sums):
            rows = pl.ds(pl.multiple_of(i * step, step), step)
            e = jnp.exp(s_all[t, rows] - top)
            s_all[t, rows] = e
            return sums[0] + fold(e, jnp.sum), sums[1] + fold(e * dp_all[t, rows], jnp.sum)

        zero = jnp.zeros((8, 2 * queries), F32)
        total, delta = lax.fori_loop(0, steps, weigh, (zero, zero))
        inverse = 1.0 / jnp.sum(total, axis=0, keepdims=True)
        delta = jnp.sum(delta, axis=0, keepdims=True) * inverse
        scaled = inverse * scale

        def close(i, carry):
            rows = pl.ds(pl.multiple_of(i * step, step), step)
            e = s_all[t, rows]
            p_buf[rows] = (e * inverse).astype(BF)
            ds_buf[rows] = (e * scaled * (dp_all[t, rows] - delta)).astype(BF)
            return carry

        lax.fori_loop(0, steps, close, 0)

        both = matmul(values[t].T, p_buf[...]).astype(BF)
        mixed[core, pl.ds(t * LANES, HEAD_DIM)] = both[:HEAD_DIM, :queries]
        mixed[core, pl.ds(t * LANES + HEAD_DIM, HEAD_DIM)] = both[HEAD_DIM:, queries:]
        piece = mixed.at[core, pl.ds(t * LANES, LANES)]
        mixes.append(remote(piece, piece, mix_send.at[t], mix_recv.at[t], sibling))
        dq = matmul(keys[t].T, ds_buf[...])
        dq = jnp.concatenate((dq[:HEAD_DIM, :queries], dq[HEAD_DIM:, queries:]), axis=0).T.astype(BF)
        dkv[:, pl.ds(0, LANES)] = matmul(ds_buf[...], qm[t]).astype(BF)
        dkv[:, pl.ds(LANES, LANES)] = matmul(p_buf[...], om[t]).astype(BF)
        for i in range(SIDE):
            rows = pl.ds(i * (width // SIDE), width // SIDE)
            q_part = matmul(xt[rows, pl.ds(0, queries)], dq).astype(BF)
            gq[t, i] = q_part.reshape(SIDE, rows1, LANES)
            kv = matmul(xt[rows], dkv[...])
            gk[t, i] = kv[:, :LANES].astype(BF).reshape(SIDE, rows1, LANES)
            v_part = kv[:, LANES:]
            for z in range(SIDE):
                turned = jnp.concatenate(
                    [v_part[(SIDE * y + z) * rows2 : (SIDE * y + z + 1) * rows2] for y in range(SIDE)], axis=0
                )
                gv[t, z, i] = turned.astype(BF)

    first, second, third, last = {}, {}, {}, {}
    for t in range(pairs):
        attend(t)
        first[t] = phase1(t)
        if t >= 1:
            second[t - 1] = phase2(t - 1, first[t - 1])
        if t >= 2:
            third[t - 2] = phase3(t - 2, second[t - 2])
    sent += mixes

    collect(mixes)
    channels = 2 * half
    all_mixed = mixed[...].reshape(channels, queries)
    orows = og.shape[3]
    orows2 = orows // SIDE
    wide = og.shape[4]
    for i in range(SIDE):
        part = matmul(all_mixed[i * (channels // SIDE) : (i + 1) * (channels // SIDE)], up[core])
        for u in range(2):
            og[u, i] = part[:, u * wide : (u + 1) * wide].astype(BF).reshape(SIDE, orows, wide)
        for y in range(SIDE):
            for z in range(SIDE):
                top = (SIDE * y + z) * orows2
                go_tmp[z, pl.ds(y * orows2, orows2)] = part[top : top + orows2, 2 * wide : 3 * wide]
        for z in range(SIDE):
            og[2, z, i] = go_tmp[z].astype(BF)
    ofirst = [
        send_three(0, lambda at: og.at[0, at], o1.at[0], s1, d1, 9 * pairs),
        send_three(1, lambda at: og.at[1, :, at], o1.at[1], s1, d1, 9 * pairs + 3),
        send_three(2, lambda at: og.at[2, at], o1.at[2], s1, d1, 9 * pairs + 6),
    ]
    oorders = ((0, 1, 2), (1, 0, 2), (2, 0, 1))

    t = pairs - 1
    third[t - 1] = phase3(t - 1, second[t - 1])
    second[t] = phase2(t, first[t])
    osecond = []
    for u in range(3):
        collect(ofirst[u])
        for j in range(SIDE):
            own = (og.at[0, xx, j], og.at[1, j, yy], og.at[2, zz, j])[u]
            total = own[...].astype(F32)
            for i in range(SIDE - 1):
                total = total + o1[u, i, j].astype(F32)
            po2[u, j] = total.astype(BF)
        osecond.append(
            send_three(oorders[u][1], lambda at, u=u: po2.at[u, at], o2.at[u], s2, d2, 9 * pairs + 3 * u)
        )
    last[t - 2] = phase4(t - 2, third[t - 2])
    third[t] = phase3(t, second[t])
    othird = []
    for u in range(3):
        collect(osecond[u])
        total = po2[u, place_of[oorders[u][1]]].astype(F32)
        for i in range(SIDE - 1):
            total = total + o2[u, i].astype(F32)
        for j in range(SIDE):
            po3[u, j] = total[j * orows2 : (j + 1) * orows2]
        othird.append(
            send_three(oorders[u][2], lambda at, u=u: po3.at[u, at], o3.at[u], s3, d3, 9 * pairs + 3 * u)
        )
    last[t - 1] = phase4(t - 1, third[t - 1])
    last[t] = phase4(t, third[t])
    for u in range(3):
        collect(othird[u])
        total = po3[u, place_of[oorders[u][2]]] + o3[u, 0] + o3[u, 1] + o3[u, 2]
        for j in range(2):
            fo_own[j, u] = total[j * (orows2 // 2) : (j + 1) * (orows2 // 2)]
    olast = remote(fo_own.at[1 - core], fo_sib, s4.at[pairs], d4.at[pairs], sibling)
    sent.append(olast)
    for u in range(3):
        lanes = pl.ds(pl.multiple_of(core * (width // 2) + u * wide, LANES), wide)
        out_o[:, lanes] = fo_own[core, u]
    for t in range(pairs):
        finish(t, last[t])
    olast.wait_recv()
    for u in range(3):
        lanes = pl.ds(pl.multiple_of((1 - core) * (width // 2) + u * wide, LANES), wide)
        out_o[:, lanes] = fo_sib[u]
    for copy in sent:
        copy.wait_send()


def leave_kernel(*refs):
    count = len(refs) // 2
    for source, target in zip(refs[:count], refs[count:]):
        target[...] = source[...]


def leave(*results):
    return pl.pallas_call(
        leave_kernel,
        out_shape=tuple(jax.ShapeDtypeStruct(r.shape, r.dtype) for r in results),
    )(*results)


def shards(latents, norm_gain, w_query, w_key, w_value, w_out, kernel, partners, counts, cotangent):
    del counts
    views, _, columns, width = latents.shape[1:]
    inner = w_query.shape[1]
    half = inner // 2
    pairs = half // LANES
    groups = lax.axis_size("view")
    slots = groups - 1 + views
    slot_rows = 2 * columns
    key_rows = slots * slot_rows
    queries = views * slot_rows
    rows1 = width // 16
    orows = inner // 16
    wide = width // 6
    vm = pltpu.VMEM
    dma = pltpu.SemaphoreType.DMA
    in_vmem = pl.BlockSpec(memory_space=pltpu.VMEM)
    in_hbm = pl.BlockSpec(memory_space=pl.ANY)
    units = 9 * (pairs + 1)
    results = pl.pallas_call(
        kernel_body,
        out_shape=(jax.ShapeDtypeStruct((rows1 // 8, inner), F32),) * 3
        + (jax.ShapeDtypeStruct((orows // 8, width), F32),),
        in_specs=[in_vmem] * 4 + [pl.BlockSpec(memory_space=pltpu.SMEM)] + [in_hbm] * 4,
        out_specs=(in_vmem,) * 4,
        scratch_shapes=[
            vm((slots, 2, columns, width), BF),
            vm((2, views, columns, width), BF),
            vm((groups, 8, LANES), jnp.int32),
            vm((groups, 8, LANES), jnp.int32),
            vm((groups - 1, columns, width), BF),
            vm((48, 2 * queries), F32),
            vm((width, half), BF),
            vm((width, 2 * half), BF),
            vm((half, width), BF),
            vm((width, key_rows), BF),
            vm((pairs, key_rows, LANES), BF),
            vm((pairs, key_rows, LANES), BF),
            vm((pairs, 2 * queries, LANES), BF),
            vm((pairs, 2 * queries, LANES), BF),
            vm((pairs, LANES, 2 * queries), BF),
            vm((pairs, LANES, 2 * queries), BF),
            vm((2, queries, width // 2), BF),
            vm((pairs, key_rows, 2 * queries), F32),
            vm((pairs, key_rows, 2 * queries), F32),
            vm((pairs, 8, 2 * queries), F32),
            vm((key_rows, 2 * queries), BF),
            vm((key_rows, 2 * queries), BF),
            vm((key_rows, 2 * LANES), BF),
            vm((2, half, queries), BF),
            vm((pairs, SIDE, SIDE, rows1, LANES), BF),
            vm((pairs, SIDE, SIDE, rows1, LANES), BF),
            vm((pairs, SIDE, SIDE, rows1, LANES), BF),
            vm((pairs, 3, SIDE - 1, SIDE, rows1, LANES), BF),
            vm((pairs, 3, SIDE, rows1, LANES), BF),
            vm((pairs, 3, SIDE - 1, rows1, LANES), BF),
            vm((pairs, 3, SIDE, rows1 // 4, LANES), F32),
            vm((pairs, 3, SIDE - 1, rows1 // 4, LANES), F32),
            vm((2, pairs, 3, rows1 // 8, LANES), F32),
            vm((pairs, 3, rows1 // 8, LANES), F32),
            vm((3, SIDE, SIDE, orows, wide), BF),
            vm((SIDE, orows, wide), F32),
            vm((3, SIDE - 1, SIDE, orows, wide), BF),
            vm((3, SIDE, orows, wide), BF),
            vm((3, SIDE - 1, orows, wide), BF),
            vm((3, SIDE, orows // 4, wide), F32),
            vm((3, SIDE - 1, orows // 4, wide), F32),
            vm((2, 3, orows // 8, wide), F32),
            vm((3, orows // 8, wide), F32),
            dma((4,)), dma((2,)), dma((2,)),
            dma((groups,)), dma((groups,)), dma((groups,)), dma((groups,)), dma((groups,)), dma((groups,)),
            dma((pairs,)), dma((pairs,)),
            dma((units,)), dma((units,)), dma((units,)), dma((units,)), dma((units,)), dma((units,)),
            dma((pairs + 1,)), dma((pairs + 1,)),
        ],
        compiler_params=pltpu.CompilerParams(
            collective_id=0, has_side_effects=True, vmem_limit_bytes=VMEM_LIMIT
        ),
    )(
        latents[0, :, 0], norm_gain, cotangent[0, :, 0], kernel, partners[0],
        w_query, w_key, w_value, w_out,
    )
    return leave(*results)


def solution(mesh):
    strips = P("scene", "view", "row", None, None)
    return jax.shard_map(
        shards,
        mesh=mesh,
        in_specs=(
            strips, P(), P(), P(), P(), P(), P(),
            P("scene", "view", None), P("scene", "view"), strips,
        ),
        out_specs=(P(("scene", "view", "row"), None),) * 4,
        check_vma=False,
    )
```

```python
import functools

import jax
import jax.numpy as jnp
from jax import lax
from jax.experimental import pallas as pl
from jax.experimental.pallas import tpu as pltpu
from jax.sharding import PartitionSpec as P

HEAD_DIM = 64
LANES = 128
EPSILON = 1e-06
SIDE = 4
OFFSETS = (
    (0, 1), (1, 0), (0, 3), (3, 0), (2, 2), (1, 1), (3, 3), (0, 2),
    (2, 0), (1, 3), (3, 1), (1, 2), (2, 1), (3, 2), (2, 3),
)
BATCHES = (4, 4, 4, 2, 1)
MESH = pl.DeviceIdType.MESH
VMEM_LIMIT = 62 * 1024 * 1024
NT = (((1,), (1,)), ((), ()))
NN = (((1,), (0,)), ((), ()))
BF = jnp.bfloat16
F32 = jnp.float32


def matmul(a, b, dims=NN):
    return lax.dot_general(a, b, dims, preferred_element_type=F32)


def kernel_body(
    lat, gain, cot, taps, partners, wq_hbm, wk_hbm, wv_hbm, wo_hbm,
    out_q, out_k, out_v, out_o,
    x, cot_all, ask, grant, outbuf, bias,
    wq, wkv, wo, xt, keys, values, qm, om, qmt, omt, up, s_all, dp_all, tops, p_buf, ds_buf, dkv, mixed,
    gk, gv, r1, p2, r2, stage, got, near,
    xn_r, xq, up_r, dq_all, mx_r, q2, rq2, stage_q, got_q, near_q, o2, ro2, stage_o, got_o, near_o,
    load_sem, own_send, own_recv, ask_send, ask_recv, out_send, out_recv, fwd_send, fwd_recv,
    mix_send, mix_recv, x_send, x_recv, s1, d1, s2, d2, s3, d3,
):
    xx, me, core = lax.axis_index("scene"), lax.axis_index("view"), lax.axis_index("row")
    yy, zz = me // SIDE, lax.rem(me, SIDE)
    groups = SIDE * SIDE
    views, columns, width = lat.shape
    half = wq.shape[1]
    pairs = half // LANES
    slots = x.shape[0]
    slot_rows = 2 * columns
    key_rows = slots * slot_rows
    queries = views * slot_rows
    scale = HEAD_DIM ** (-0.5)
    sibling = (xx, me, 1 - core)

    def group_at(step, strip, sign):
        a, b = OFFSETS[step - 1]
        a, b = a + strip * (b - a), b + strip * (a - b)
        return lax.rem(yy + SIDE + sign * a, SIDE) * SIDE + lax.rem(zz + SIDE + sign * b, SIDE)

    def peer(step):
        return group_at(step, core, 1)

    def reverse(step):
        a, b = OFFSETS[step - 1]
        return OFFSETS.index(((SIDE - a) % SIDE, (SIDE - b) % SIDE)) + 1

    def along(axis, step):
        if axis == 0:
            at = lax.rem(xx + step, SIDE)
            return at, (at, me, core)
        if axis == 1:
            at = lax.rem(yy + step, SIDE)
            return at, (xx, at * SIDE + zz, core)
        at = lax.rem(zz + step, SIDE)
        return at, (xx, yy * SIDE + at, core)

    barrier = pltpu.get_barrier_semaphore()
    for step in range(1, groups):
        pl.semaphore_signal(barrier, inc=1, device_id=(xx, peer(step), core), device_id_type=MESH)
    for step in range(1, SIDE):
        pl.semaphore_signal(barrier, inc=1, device_id=along(0, step)[1], device_id_type=MESH)
        for axis in range(3):
            there = along(axis, step)[1][:2] + (1 - core,)
            pl.semaphore_signal(barrier, inc=1, device_id=there, device_id_type=MESH)
    pl.semaphore_signal(barrier, inc=1, device_id=sibling, device_id_type=MESH)

    cols = pl.ds(pl.multiple_of(core * half, LANES), half)
    loads = [
        pltpu.make_async_copy(wq_hbm.at[:, cols], wq, load_sem.at[0]),
        pltpu.make_async_copy(wk_hbm.at[:, cols], wkv.at[:, pl.ds(0, half)], load_sem.at[1]),
        pltpu.make_async_copy(wv_hbm.at[:, cols], wkv.at[:, pl.ds(half, half)], load_sem.at[2]),
        pltpu.make_async_copy(wo_hbm.at[cols, :], wo, load_sem.at[3]),
    ]
    for copy in loads:
        copy.start()

    steps_of = lax.broadcasted_iota(jnp.int32, (groups, LANES), 0)
    first_of = jnp.full((groups, LANES), -2 * views, jnp.int32)
    for s in range(1, groups):
        first_of = jnp.where(steps_of == s, peer(s) * views, first_of)
    wanted = jnp.zeros((groups, LANES), jnp.int32)
    for v in range(views):
        for j in range(partners.shape[1]):
            local = partners[v, j] - first_of
            wanted = jnp.maximum(wanted, jnp.where((local >= 0) & (local < views), local, 0))
    for s in range(1, groups):
        ask[s] = jnp.broadcast_to(wanted[s : s + 1], ask.shape[1:])

    pl.semaphore_wait(barrier, groups + 4 * (SIDE - 1))

    def remote(src, dst, send, recv, device):
        copy = pltpu.make_async_remote_copy(
            src_ref=src, dst_ref=dst, send_sem=send, recv_sem=recv, device_id=device, device_id_type=MESH
        )
        copy.start()
        return copy

    sent = []
    asks = [
        remote(ask.at[s], grant.at[s], ask_send.at[s], ask_recv.at[s], (xx, peer(s), core))
        for s in range(1, groups)
    ]
    own_cot = remote(cot, cot_all.at[core], own_send.at[1], own_recv.at[1], sibling)

    for v in range(views):
        rows = lat[v].astype(F32)
        mean = jnp.mean(rows * rows, -1, keepdims=True)
        x[v, core] = (rows * lax.rsqrt(mean + EPSILON) * gain[...].reshape(1, width)).astype(BF)
    cot_all[core] = cot[...]

    mine = x.at[pl.ds(0, views), core]
    own_x = remote(mine, mine, own_send.at[0], own_recv.at[0], sibling)

    blocks = []
    for s in range(1, groups):
        asks[reverse(s) - 1].wait_recv()
        want = grant[reverse(s)][0:1, 0:1]
        block = x[0, core]
        for v in range(1, views):
            block = jnp.where(want == v, x[v, core], block)
        outbuf[s - 1] = block
        blocks.append(
            remote(
                outbuf.at[s - 1], x.at[views - 1 + s, core], out_send.at[s], out_recv.at[s], (xx, peer(s), core)
            )
        )
    sent += asks + [own_x, own_cot] + blocks

    quarter = width // SIDE
    own_x.wait_recv()
    early = []
    for step in range(1, SIDE):
        at, device = along(0, step)
        lanes = pl.ds(pl.multiple_of(at * quarter, LANES), quarter)
        early.append(
            remote(x.at[pl.ds(0, views), :, :, lanes], xn_r.at[step - 1], x_send.at[step], x_recv.at[step], device)
        )

    row_of = lax.broadcasted_iota(jnp.int32, (bias.shape[0], LANES), 0)
    first_of = jnp.full(row_of.shape, -2 * views, jnp.int32)
    for s in range(1, groups):
        for strip in range(2):
            first_of = jnp.where(row_of == 2 * (views - 1 + s) + strip, group_at(s, strip, -1) * views, first_of)
    lane_of = lax.broadcasted_iota(jnp.int32, (bias.shape[0], LANES), 1)
    seen = []
    for v in range(views):
        hit = jnp.where(row_of // 2 == v, 1, 0)
        for j in range(partners.shape[1]):
            number = partners[v, j]
            local = number - first_of
            hit = jnp.where((local >= 0) & (local < views) & (number >= 0), 1, hit)
        seen.append(jnp.where(hit > 0, 0.0, -1e30))
    for part in range(views // 2):
        both = jnp.where(lane_of < slot_rows, seen[2 * part], seen[2 * part + 1])
        for head in range(2):
            bias[:, pl.ds(head * queries + part * LANES, LANES)] = both

    own_cot.wait_recv()
    chunk = 2 * LANES
    place = lax.broadcasted_iota(jnp.int32, (columns, chunk), 0)

    def conv_view(view, carry):
        for part in range(width // chunk):
            lanes = pl.ds(part * chunk, chunk)
            kern = taps[:, lanes].astype(F32)
            shifted = []
            for strip in range(2):
                mid = cot_all[strip, view, :, lanes].astype(F32)
                after = jnp.where(place == columns - 1, 0.0, pltpu.roll(mid, columns - 1, 0))
                before = jnp.where(place == 0, 0.0, pltpu.roll(mid, 1, 0))
                shifted.append((after, mid, before))
            for strip in range(2):
                total = shifted[strip][1]
                for a, source in ((1, strip), (2 * strip, 1 - strip)):
                    for b in range(3):
                        total = total + kern[3 * a + b : 3 * a + b + 1] * shifted[source][b]
                side = part * chunk // (width // 2)
                rows = pl.ds(pl.multiple_of(view * slot_rows + strip * columns, columns), columns)
                up[side, rows, pl.ds(part * chunk - side * (width // 2), chunk)] = total.astype(BF)
        return carry

    lax.fori_loop(0, views, conv_view, 0)
    early_up = []
    for step in range(1, SIDE):
        early_up.append(
            remote(
                up.at[core], up_r.at[step - 1], x_send.at[SIDE + step], x_recv.at[SIDE + step], along(0, step)[1]
            )
        )
    sent += early + early_up

    for copy in loads:
        copy.wait()

    lane = lax.broadcasted_iota(jnp.int32, (queries, LANES), 1)
    sublane = lax.broadcasted_iota(jnp.int32, (LANES, queries), 0)

    def split_heads(out, turned, rows_f):
        rounded = rows_f.astype(BF).astype(F32)
        for pair in range(pairs):
            block = rounded[:, pair * LANES : (pair + 1) * LANES]
            out[pair, pl.ds(0, queries)] = jnp.where(lane < HEAD_DIM, block, 0.0).astype(BF)
            out[pair, pl.ds(queries, queries)] = jnp.where(lane < HEAD_DIM, 0.0, block).astype(BF)
            block = block.T
            turned[pair, :, pl.ds(0, queries)] = jnp.where(sublane < HEAD_DIM, block, 0.0).astype(BF)
            turned[pair, :, pl.ds(queries, queries)] = jnp.where(sublane < HEAD_DIM, 0.0, block).astype(BF)

    split_heads(
        om, omt,
        matmul(up[0], wo[:, pl.ds(0, width // 2)], NT) + matmul(up[1], wo[:, pl.ds(width // 2, width // 2)], NT),
    )
    split_heads(qm, qmt, matmul(x[pl.ds(0, views)].reshape(queries, width), wq[...]))

    tile = 2 * LANES

    def fold(v, op):
        return op(v.reshape(v.shape[0] // 8, 8, v.shape[1]), axis=0)

    def batch(first, count):
        rows = pl.ds(first * slot_rows, count * slot_rows)
        flat = x[pl.ds(first, count)].reshape(count * slot_rows, width)
        out = matmul(flat, wkv[...]).astype(BF)
        for pair in range(pairs):
            keys[pair, rows] = out[:, pair * LANES : (pair + 1) * LANES]
            values[pair, rows] = out[:, half + pair * LANES : half + (pair + 1) * LANES]

        for j in range(width // tile):
            lanes = pl.ds(j * tile, tile)
            xt[lanes, rows] = flat[:, j * tile : (j + 1) * tile].T

        for pair in range(pairs):
            s = matmul(keys[pair, rows], qmt[pair]) * scale
            top = jnp.full((8, 2 * queries), -3e38, F32) if first == 0 else tops[pair]
            for i in range(2 * count):
                part = s[i * columns : (i + 1) * columns] + bias[pl.ds(2 * first + i, 1)]
                s_all[pair, pl.ds(first * slot_rows + i * columns, columns)] = part
                top = jnp.maximum(top, fold(part, jnp.max))
            tops[pair] = top
            dp_all[pair, rows] = matmul(values[pair, rows], omt[pair])

    parts = [(views + sum(BATCHES[:i]), count) for i, count in enumerate(BATCHES)]
    before = None
    batch(0, views)
    forwards = []
    for first, count in parts:
        fresh = []
        for slot in range(first, first + count):
            s = slot - views + 1
            blocks[s - 1].wait_recv()
            place_x = x.at[slot, core]
            fresh.append(remote(place_x, place_x, fwd_send.at[s], fwd_recv.at[s], sibling))
        if before:
            batch(*before)
        for copy in fresh:
            copy.wait_recv()
        forwards += fresh
        before = (first, count)
    batch(*before)
    sent += forwards

    lanes = pl.ds(pl.multiple_of(xx * quarter, LANES), quarter)
    xq[:, pl.ds(0, queries)] = x[pl.ds(0, views), :, :, lanes].reshape(queries, quarter).T
    for step in range(1, SIDE):
        early[step - 1].wait_recv()
        xq[:, pl.ds(step * queries, queries)] = xn_r[step - 1].reshape(queries, quarter).T

    def send_three(axis, source, target, send, recv, base):
        copies = []
        for step in (2, 1, 3):
            at, device = along(axis, step)
            copies.append(
                remote(source(at), target.at[step - 1], send.at[base + step - 1], recv.at[base + step - 1], device)
            )
        sent.extend(copies)
        return copies

    def collect(copies):
        for copy in copies:
            copy.wait_recv()

    place_of = (xx, yy, zz)
    orders = ((1, 2, 0), (2, 0, 1))
    rows1 = gk.shape[3]
    rows2 = rows1 // SIDE

    def phase1(t):
        return [
            send_three(1, lambda at: gk.at[t, :, at], r1.at[t, 0], s1, d1, 6 * t),
            send_three(2, lambda at: gv.at[t, at], r1.at[t, 1], s1, d1, 6 * t + 3),
        ]

    def regroup(parts, rows):
        return [
            jnp.concatenate([part[k * rows : (k + 1) * rows] for part in parts], axis=0) for k in range(SIDE)
        ]

    def phase2(t, arrived):
        copies = []
        for m in range(2):
            collect(arrived[m])
            totals = []
            for j in range(SIDE):
                own = (gk.at[t, j, yy], gv.at[t, zz, j])[m]
                total = own[...].astype(F32)
                for i in range(SIDE - 1):
                    total = total + r1[t, m, i, j].astype(F32)
                totals.append(total)
            if m == 0:
                totals = regroup(totals, rows2)
            for j in range(SIDE):
                p2[t, m, j] = totals[j].astype(BF)
            copies.append(
                send_three(orders[m][1], lambda at, m=m: p2.at[t, m, at], r2.at[t, m], s2, d2, 6 * t + 3 * m)
            )
        return copies

    def second_sum(own, others):
        total = own[...].astype(F32)
        for i in range(SIDE - 1):
            total = total + others[i].astype(F32)
        return total

    def last_hop(total, axis, pieces, target, beside, unit):
        rows = total.shape[0] // (2 * SIDE)
        for j in range(SIDE):
            for h in range(2):
                pieces[j, h] = total[(2 * j + h) * rows : (2 * j + h + 1) * rows]
        copies = []
        for step in (2, 1, 3):
            at, device = along(axis, step)
            for cross in range(2):
                to = 1 - core if cross else core
                slot = 7 * unit + 2 * (step - 1) + cross
                copies.append(
                    remote(
                        pieces.at[at, to], target.at[cross, step - 1], s3.at[slot], d3.at[slot], device[:2] + (to,)
                    )
                )
        slot = 7 * unit + 6
        copies.append(remote(pieces.at[place_of[axis], 1 - core], beside, s3.at[slot], d3.at[slot], sibling))
        sent.extend(copies)
        return copies

    def arrive(copies, axis, pieces, target, beside, out, size, offset):
        collect(copies)
        span = out.shape[1] // 2
        total = pieces[place_of[axis], core] + target[0, 0] + target[0, 1] + target[0, 2]
        out[:, pl.ds(pl.multiple_of(core * span + offset, LANES), size)] = total
        total = beside[...] + target[1, 0] + target[1, 1] + target[1, 2]
        out[:, pl.ds(pl.multiple_of((1 - core) * span + offset, LANES), size)] = total

    def phase3(t, arrived):
        copies = []
        for m in range(2):
            collect(arrived[m])
            total = second_sum(p2.at[t, m, place_of[orders[m][1]]], r2.at[t, m])
            copies.append(
                last_hop(total, orders[m][2], stage.at[t, m], got.at[t, m], near.at[t, m], 2 * t + m)
            )
        return copies

    def finish(t, arrived):
        for m in range(2):
            arrive(
                arrived[m], orders[m][2], stage.at[t, m], got.at[t, m], near.at[t, m],
                (out_k, out_v)[m], LANES, t * LANES,
            )

    step = 64
    steps = key_rows // step
    mixes, dqs = [], []

    def weights(t):
        top = jnp.max(tops[t], axis=0, keepdims=True)

        def weigh(i, sums):
            rows = pl.ds(pl.multiple_of(i * step, step), step)
            e = jnp.exp(s_all[t, rows] - top)
            s_all[t, rows] = e
            return sums[0] + fold(e, jnp.sum), sums[1] + fold(e * dp_all[t, rows], jnp.sum)

        zero = jnp.zeros((8, 2 * queries), F32)
        total, delta = lax.fori_loop(0, steps, weigh, (zero, zero))
        inverse = 1.0 / jnp.sum(total, axis=0, keepdims=True)
        delta = jnp.sum(delta, axis=0, keepdims=True) * inverse
        scaled = inverse * scale

        def close(i, carry):
            rows = pl.ds(pl.multiple_of(i * step, step), step)
            e = s_all[t, rows]
            p_buf[rows] = (e * inverse).astype(BF)
            ds_buf[rows] = (e * scaled * (dp_all[t, rows] - delta)).astype(BF)
            return carry

        lax.fori_loop(0, steps, close, 0)

        both = matmul(values[t].T, p_buf[...]).astype(BF)
        top = pl.multiple_of(core * half + t * LANES, LANES)
        mixed[pl.ds(top, HEAD_DIM)] = both[:HEAD_DIM, :queries]
        mixed[pl.ds(top + HEAD_DIM, HEAD_DIM)] = both[HEAD_DIM:, queries:]
        piece = mixed.at[pl.ds(top, LANES)]
        mixes.append(remote(piece, piece, mix_send.at[t], mix_recv.at[t], sibling))
        dq = matmul(keys[t].T, ds_buf[...])
        dq = jnp.concatenate((dq[:HEAD_DIM, :queries], dq[HEAD_DIM:, queries:]), axis=0).T
        dq_all[t, pl.ds(0, queries)] = dq.astype(BF)
        copies = []
        for hop in (2, 1, 3):
            slot = SIDE * (2 + t) + hop
            copies.append(
                remote(
                    dq_all.at[t, pl.ds(0, queries)], dq_all.at[t, pl.ds(hop * queries, queries)],
                    x_send.at[slot], x_recv.at[slot], along(0, hop)[1],
                )
            )
        dqs.append(copies)
        sent.extend(copies)

    def key_grads(t):
        dkv[:, pl.ds(0, LANES)] = matmul(ds_buf[...], qm[t]).astype(BF)
        dkv[:, pl.ds(LANES, LANES)] = matmul(p_buf[...], om[t]).astype(BF)
        for i in range(SIDE):
            rows = pl.ds(i * quarter, quarter)
            kv = matmul(xt[rows], dkv[...])
            gk[t, i] = kv[:, :LANES].astype(BF).reshape(SIDE, rows1, LANES)
            v_part = kv[:, LANES:]
            parts = [v_part[y * rows1 : (y + 1) * rows1] for y in range(SIDE)]
            for z, turned in enumerate(regroup(parts, rows2)):
                gv[t, z, i] = turned.astype(BF)

    first, second, third = {}, {}, {}
    for t in range(pairs - 1):
        weights(t)
        key_grads(t)
        first[t] = phase1(t)
    t = pairs - 1
    weights(t)
    second[0] = phase2(0, first[0])
    collect(mixes)
    sent += mixes
    channels = 2 * half
    share = channels // SIDE
    mxs = []
    for hop in (2, 1, 3):
        at, device = along(0, hop)
        slot = SIDE * (2 + pairs) + hop
        mxs.append(
            remote(
                mixed.at[pl.ds(pl.multiple_of(at * share, 16), share)], mx_r.at[hop - 1],
                x_send.at[slot], x_recv.at[slot], device,
            )
        )
    sent += mxs
    key_grads(t)
    first[t] = phase1(t)

    def query_grad(t):
        collect(dqs[t])
        g = matmul(xq[...], dq_all[t])
        parts = [g[y * rows1 : (y + 1) * rows1] for y in range(SIDE)]
        for z, turned in enumerate(regroup(parts, rows2)):
            q2[z, :, pl.ds(t * LANES, LANES)] = turned.astype(BF)

    for t in range(pairs - 1):
        query_grad(t)
    second[1] = phase2(1, first[1])
    query_grad(pairs - 1)
    q_second = send_three(2, lambda at: q2.at[at], rq2, s2, d2, 6 * pairs)
    third[0] = phase3(0, second[0])

    collect(early_up)
    own = mixed[pl.ds(pl.multiple_of(xx * share, 16), share)]
    g = matmul(own, up[core])
    collect(mxs)
    for hop in range(1, SIDE):
        g = g + matmul(mx_r[hop - 1], up_r[hop - 1])
    o2[...] = g.astype(BF).reshape(SIDE, share // SIDE, width // 2)
    o_second = send_three(1, lambda at: o2.at[at], ro2, s2, d2, 6 * pairs + 3)

    second[2] = phase2(2, first[2])
    third[1] = phase3(1, second[1])
    collect(q_second)
    q_third = last_hop(second_sum(q2.at[zz], rq2), 1, stage_q, got_q, near_q, 2 * pairs)
    collect(o_second)
    o_third = last_hop(second_sum(o2.at[yy], ro2), 2, stage_o, got_o, near_o, 2 * pairs + 1)
    finish(0, third[0])
    third[2] = phase3(2, second[2])
    finish(1, third[1])
    arrive(q_third, 1, stage_q, got_q, near_q, out_q, half, 0)
    arrive(o_third, 2, stage_o, got_o, near_o, out_o, width // 2, 0)
    finish(2, third[2])
    for copy in sent:
        copy.wait_send()


def leave_kernel(*refs):
    count = len(refs) // 2
    for source, target in zip(refs[:count], refs[count:]):
        target[...] = source[...]


def leave(*results):
    return pl.pallas_call(
        leave_kernel,
        out_shape=tuple(jax.ShapeDtypeStruct(r.shape, r.dtype) for r in results),
    )(*results)


def shards(latents, norm_gain, w_query, w_key, w_value, w_out, kernel, partners, counts, cotangent):
    del counts
    views, _, columns, width = latents.shape[1:]
    inner = w_query.shape[1]
    half = inner // 2
    pairs = half // LANES
    groups = lax.axis_size("view")
    slots = groups - 1 + views
    slot_rows = 2 * columns
    key_rows = slots * slot_rows
    queries = views * slot_rows
    rows1 = width // 16
    orows = inner // 16
    vm = pltpu.VMEM
    dma = pltpu.SemaphoreType.DMA
    in_vmem = pl.BlockSpec(memory_space=pltpu.VMEM)
    in_hbm = pl.BlockSpec(memory_space=pl.ANY)
    results = pl.pallas_call(
        kernel_body,
        out_shape=(jax.ShapeDtypeStruct((rows1 // 8, inner), F32),) * 3
        + (jax.ShapeDtypeStruct((orows // 8, width), F32),),
        in_specs=[in_vmem] * 4 + [pl.BlockSpec(memory_space=pltpu.SMEM)] + [in_hbm] * 4,
        out_specs=(in_vmem,) * 4,
        scratch_shapes=[
            vm((slots, 2, columns, width), BF),
            vm((2, views, columns, width), BF),
            vm((groups, 8, LANES), jnp.int32),
            vm((groups, 8, LANES), jnp.int32),
            vm((groups - 1, columns, width), BF),
            vm((48, 2 * queries), F32),
            vm((width, half), BF),
            vm((width, 2 * half), BF),
            vm((half, width), BF),
            vm((width, key_rows), BF),
            vm((pairs, key_rows, LANES), BF),
            vm((pairs, key_rows, LANES), BF),
            vm((pairs, 2 * queries, LANES), BF),
            vm((pairs, 2 * queries, LANES), BF),
            vm((pairs, LANES, 2 * queries), BF),
            vm((pairs, LANES, 2 * queries), BF),
            vm((2, queries, width // 2), BF),
            vm((pairs, key_rows, 2 * queries), F32),
            vm((pairs, key_rows, 2 * queries), F32),
            vm((pairs, 8, 2 * queries), F32),
            vm((key_rows, 2 * queries), BF),
            vm((key_rows, 2 * queries), BF),
            vm((key_rows, 2 * LANES), BF),
            vm((2 * half, queries), BF),
            vm((pairs, SIDE, SIDE, rows1, LANES), BF),
            vm((pairs, SIDE, SIDE, rows1, LANES), BF),
            vm((pairs, 2, SIDE - 1, SIDE, rows1, LANES), BF),
            vm((pairs, 2, SIDE, rows1, LANES), BF),
            vm((pairs, 2, SIDE - 1, rows1, LANES), BF),
            vm((pairs, 2, SIDE, 2, rows1 // 8, LANES), F32),
            vm((pairs, 2, 2, SIDE - 1, rows1 // 8, LANES), F32),
            vm((pairs, 2, rows1 // 8, LANES), F32),
            vm((SIDE - 1, views, 2, columns, width // SIDE), BF),
            vm((width // SIDE, SIDE * queries), BF),
            vm((SIDE - 1, queries, width // 2), BF),
            vm((pairs, SIDE * queries, LANES), BF),
            vm((SIDE - 1, inner // SIDE, queries), BF),
            vm((SIDE, rows1, half), BF),
            vm((SIDE - 1, rows1, half), BF),
            vm((SIDE, 2, rows1 // 8, half), F32),
            vm((2, SIDE - 1, rows1 // 8, half), F32),
            vm((rows1 // 8, half), F32),
            vm((SIDE, orows, width // 2), BF),
            vm((SIDE - 1, orows, width // 2), BF),
            vm((SIDE, 2, orows // 8, width // 2), F32),
            vm((2, SIDE - 1, orows // 8, width // 2), F32),
            vm((orows // 8, width // 2), F32),
            dma((4,)), dma((2,)), dma((2,)),
            dma((groups,)), dma((groups,)), dma((groups,)), dma((groups,)), dma((groups,)), dma((groups,)),
            dma((pairs,)), dma((pairs,)), dma((SIDE * (pairs + 3),)), dma((SIDE * (pairs + 3),)),
            dma((6 * pairs,)), dma((6 * pairs,)), dma((6 * pairs + 6,)), dma((6 * pairs + 6,)),
            dma((14 * pairs + 14,)), dma((14 * pairs + 14,)),
        ],
        compiler_params=pltpu.CompilerParams(
            collective_id=0, has_side_effects=True, vmem_limit_bytes=VMEM_LIMIT
        ),
    )(
        latents[0, :, 0], norm_gain, cotangent[0, :, 0], kernel, partners[0],
        w_query, w_key, w_value, w_out,
    )
    return leave(*results)


def solution(mesh):
    strips = P("scene", "view", "row", None, None)
    return jax.shard_map(
        shards,
        mesh=mesh,
        in_specs=(
            strips, P(), P(), P(), P(), P(), P(),
            P("scene", "view", None), P("scene", "view"), strips,
        ),
        out_specs=(P(("scene", "view", "row"), None),) * 4,
        check_vma=False,
    )
```

```python
import functools

import jax
import jax.numpy as jnp
from jax import lax
from jax.experimental import pallas as pl
from jax.experimental.pallas import tpu as pltpu
from jax.sharding import PartitionSpec as P

HEAD_DIM = 64
LANES = 128
EPSILON = 1e-06
SIDE = 4
OFFSETS = (
    (0, 1), (1, 0), (0, 3), (3, 0), (2, 2), (1, 1), (3, 3), (0, 2),
    (2, 0), (1, 3), (3, 1), (1, 2), (2, 1), (3, 2), (2, 3),
)
BATCHES = (4, 4, 4, 2, 1)
EARLY = 12
MESH = pl.DeviceIdType.MESH
VMEM_LIMIT = 62 * 1024 * 1024
NT = (((1,), (1,)), ((), ()))
NN = (((1,), (0,)), ((), ()))
BF = jnp.bfloat16
F32 = jnp.float32


def matmul(a, b, dims=NN):
    return lax.dot_general(a, b, dims, preferred_element_type=F32)


def kernel_body(
    lat, gain, cot, taps, partners, wq_hbm, wk_hbm, wv_hbm, wo_hbm,
    out_q, out_k, out_v, out_o,
    x, cot_all, ask, grant, outbuf, bias,
    wq, wkv, wo, xt, keys, values, qm, om, qmt, omt, up, s_all, dp_all, tops, p_buf, ds_buf, dkv, mixed,
    gk, gv, r1, p2, r2, stage, got, near,
    xn_r, xq, up_r, dq_all, mx_r, sums, o2, ro2, stage_o, got_o, near_o,
    load_sem, own_send, own_recv, ask_send, ask_recv, out_send, out_recv, fwd_send, fwd_recv,
    mix_send, mix_recv, x_send, x_recv, s1, d1, s2, d2, s3, d3,
):
    xx, me, core = lax.axis_index("scene"), lax.axis_index("view"), lax.axis_index("row")
    yy, zz = me // SIDE, lax.rem(me, SIDE)
    groups = SIDE * SIDE
    views, columns, width = lat.shape
    half = wq.shape[1]
    pairs = half // LANES
    slots = x.shape[0]
    slot_rows = 2 * columns
    key_rows = slots * slot_rows
    queries = views * slot_rows
    scale = HEAD_DIM ** (-0.5)
    sibling = (xx, me, 1 - core)

    def group_at(step, strip, sign):
        a, b = OFFSETS[step - 1]
        a, b = a + strip * (b - a), b + strip * (a - b)
        return lax.rem(yy + SIDE + sign * a, SIDE) * SIDE + lax.rem(zz + SIDE + sign * b, SIDE)

    def peer(step):
        return group_at(step, core, 1)

    def reverse(step):
        a, b = OFFSETS[step - 1]
        return OFFSETS.index(((SIDE - a) % SIDE, (SIDE - b) % SIDE)) + 1

    def along(axis, step):
        if axis == 0:
            at = lax.rem(xx + step, SIDE)
            return at, (at, me, core)
        if axis == 1:
            at = lax.rem(yy + step, SIDE)
            return at, (xx, at * SIDE + zz, core)
        at = lax.rem(zz + step, SIDE)
        return at, (xx, yy * SIDE + at, core)

    barrier = pltpu.get_barrier_semaphore()
    for step in range(1, groups):
        pl.semaphore_signal(barrier, inc=1, device_id=(xx, peer(step), core), device_id_type=MESH)
    for step in range(1, SIDE):
        pl.semaphore_signal(barrier, inc=1, device_id=along(0, step)[1], device_id_type=MESH)
        for axis in range(3):
            there = along(axis, step)[1][:2] + (1 - core,)
            pl.semaphore_signal(barrier, inc=1, device_id=there, device_id_type=MESH)
    pl.semaphore_signal(barrier, inc=1, device_id=sibling, device_id_type=MESH)

    cols = pl.ds(pl.multiple_of(core * half, LANES), half)
    loads = [
        pltpu.make_async_copy(wq_hbm.at[:, cols], wq, load_sem.at[0]),
        pltpu.make_async_copy(wk_hbm.at[:, cols], wkv.at[:, pl.ds(0, half)], load_sem.at[1]),
        pltpu.make_async_copy(wv_hbm.at[:, cols], wkv.at[:, pl.ds(half, half)], load_sem.at[2]),
        pltpu.make_async_copy(wo_hbm.at[cols, :], wo, load_sem.at[3]),
    ]
    for copy in loads:
        copy.start()

    steps_of = lax.broadcasted_iota(jnp.int32, (groups, LANES), 0)
    first_of = jnp.full((groups, LANES), -2 * views, jnp.int32)
    for s in range(1, groups):
        first_of = jnp.where(steps_of == s, peer(s) * views, first_of)
    wanted = jnp.zeros((groups, LANES), jnp.int32)
    for v in range(views):
        for j in range(partners.shape[1]):
            local = partners[v, j] - first_of
            wanted = jnp.maximum(wanted, jnp.where((local >= 0) & (local < views), local, 0))
    for s in range(1, groups):
        ask[s] = jnp.broadcast_to(wanted[s : s + 1], ask.shape[1:])

    pl.semaphore_wait(barrier, groups + 4 * (SIDE - 1))

    def remote(src, dst, send, recv, device):
        copy = pltpu.make_async_remote_copy(
            src_ref=src, dst_ref=dst, send_sem=send, recv_sem=recv, device_id=device, device_id_type=MESH
        )
        copy.start()
        return copy

    sent = []
    asks = [
        remote(ask.at[s], grant.at[s], ask_send.at[s], ask_recv.at[s], (xx, peer(s), core))
        for s in range(1, groups)
    ]
    own_cot = remote(cot, cot_all.at[core], own_send.at[1], own_recv.at[1], sibling)

    for v in range(views):
        rows = lat[v].astype(F32)
        mean = jnp.mean(rows * rows, -1, keepdims=True)
        x[v, core] = (rows * lax.rsqrt(mean + EPSILON) * gain[...].reshape(1, width)).astype(BF)
    cot_all[core] = cot[...]

    mine = x.at[pl.ds(0, views), core]
    own_x = remote(mine, mine, own_send.at[0], own_recv.at[0], sibling)

    blocks = []
    for s in range(1, groups):
        asks[reverse(s) - 1].wait_recv()
        want = grant[reverse(s)][0:1, 0:1]
        block = x[0, core]
        for v in range(1, views):
            block = jnp.where(want == v, x[v, core], block)
        outbuf[s - 1] = block
        blocks.append(
            remote(
                outbuf.at[s - 1], x.at[views - 1 + s, core], out_send.at[s], out_recv.at[s], (xx, peer(s), core)
            )
        )
    sent += asks + [own_x, own_cot] + blocks

    quarter = width // SIDE
    own_x.wait_recv()
    early = []
    for step in range(1, SIDE):
        at, device = along(0, step)
        lanes = pl.ds(pl.multiple_of(at * quarter, LANES), quarter)
        early.append(
            remote(x.at[pl.ds(0, views), :, :, lanes], xn_r.at[step - 1], x_send.at[step], x_recv.at[step], device)
        )

    row_of = lax.broadcasted_iota(jnp.int32, (bias.shape[0], LANES), 0)
    first_of = jnp.full(row_of.shape, -2 * views, jnp.int32)
    for s in range(1, groups):
        for strip in range(2):
            first_of = jnp.where(row_of == 2 * (views - 1 + s) + strip, group_at(s, strip, -1) * views, first_of)
    lane_of = lax.broadcasted_iota(jnp.int32, (bias.shape[0], LANES), 1)
    seen = []
    for v in range(views):
        hit = jnp.where(row_of // 2 == v, 1, 0)
        for j in range(partners.shape[1]):
            number = partners[v, j]
            local = number - first_of
            hit = jnp.where((local >= 0) & (local < views) & (number >= 0), 1, hit)
        seen.append(jnp.where(hit > 0, 0.0, -1e30))
    for part in range(views // 2):
        both = jnp.where(lane_of < slot_rows, seen[2 * part], seen[2 * part + 1])
        for head in range(2):
            bias[:, pl.ds(head * queries + part * LANES, LANES)] = both

    own_cot.wait_recv()
    chunk = 2 * LANES
    place = lax.broadcasted_iota(jnp.int32, (columns, chunk), 0)

    def conv_view(view, carry):
        for part in range(width // chunk):
            lanes = pl.ds(part * chunk, chunk)
            kern = taps[:, lanes].astype(F32)
            shifted = []
            for strip in range(2):
                mid = cot_all[strip, view, :, lanes].astype(F32)
                after = jnp.where(place == columns - 1, 0.0, pltpu.roll(mid, columns - 1, 0))
                before = jnp.where(place == 0, 0.0, pltpu.roll(mid, 1, 0))
                shifted.append((after, mid, before))
            for strip in range(2):
                total = shifted[strip][1]
                for a, source in ((1, strip), (2 * strip, 1 - strip)):
                    for b in range(3):
                        total = total + kern[3 * a + b : 3 * a + b + 1] * shifted[source][b]
                side = part * chunk // (width // 2)
                rows = pl.ds(pl.multiple_of(view * slot_rows + strip * columns, columns), columns)
                up[side, rows, pl.ds(part * chunk - side * (width // 2), chunk)] = total.astype(BF)
        return carry

    lax.fori_loop(0, views, conv_view, 0)
    early_up = []
    for step in range(1, SIDE):
        early_up.append(
            remote(
                up.at[core], up_r.at[step - 1], x_send.at[SIDE + step], x_recv.at[SIDE + step], along(0, step)[1]
            )
        )
    sent += early + early_up

    for copy in loads:
        copy.wait()

    lane = lax.broadcasted_iota(jnp.int32, (queries, LANES), 1)
    sublane = lax.broadcasted_iota(jnp.int32, (LANES, queries), 0)

    def split_heads(out, turned, rows_f):
        rounded = rows_f.astype(BF).astype(F32)
        for pair in range(pairs):
            block = rounded[:, pair * LANES : (pair + 1) * LANES]
            out[pair, pl.ds(0, queries)] = jnp.where(lane < HEAD_DIM, block, 0.0).astype(BF)
            out[pair, pl.ds(queries, queries)] = jnp.where(lane < HEAD_DIM, 0.0, block).astype(BF)
            block = block.T
            turned[pair, :, pl.ds(0, queries)] = jnp.where(sublane < HEAD_DIM, block, 0.0).astype(BF)
            turned[pair, :, pl.ds(queries, queries)] = jnp.where(sublane < HEAD_DIM, 0.0, block).astype(BF)

    split_heads(
        om, omt,
        matmul(up[0], wo[:, pl.ds(0, width // 2)], NT) + matmul(up[1], wo[:, pl.ds(width // 2, width // 2)], NT),
    )
    split_heads(qm, qmt, matmul(x[pl.ds(0, views)].reshape(queries, width), wq[...]))

    tile = 2 * LANES

    def fold(v, op):
        return op(v.reshape(v.shape[0] // 8, 8, v.shape[1]), axis=0)

    def batch(first, count):
        rows = pl.ds(first * slot_rows, count * slot_rows)
        flat = x[pl.ds(first, count)].reshape(count * slot_rows, width)
        out = matmul(flat, wkv[...]).astype(BF)
        for pair in range(pairs):
            keys[pair, rows] = out[:, pair * LANES : (pair + 1) * LANES]
            values[pair, rows] = out[:, half + pair * LANES : half + (pair + 1) * LANES]

        for j in range(width // tile):
            lanes = pl.ds(j * tile, tile)
            xt[lanes, rows] = flat[:, j * tile : (j + 1) * tile].T

        for pair in range(pairs):
            s = matmul(keys[pair, rows], qmt[pair]) * scale
            top = jnp.full((8, 2 * queries), -3e38, F32) if first == 0 else tops[pair]
            for i in range(2 * count):
                part = s[i * columns : (i + 1) * columns] + bias[pl.ds(2 * first + i, 1)]
                s_all[pair, pl.ds(first * slot_rows + i * columns, columns)] = part
                top = jnp.maximum(top, fold(part, jnp.max))
            tops[pair] = top
            dp_all[pair, rows] = matmul(values[pair, rows], omt[pair])

    stride = 64
    strides = key_rows // stride

    def weigh(t, top, low, high):
        def body(i, carry):
            rows = pl.ds(pl.multiple_of(i * stride, stride), stride)
            e = jnp.exp(s_all[t, rows] - top)
            s_all[t, rows] = e
            return carry[0] + fold(e, jnp.sum), carry[1] + fold(e * dp_all[t, rows], jnp.sum)

        zero = jnp.zeros((8, 2 * queries), F32)
        total, delta = lax.fori_loop(low, high, body, (zero, zero))
        return jnp.sum(total, axis=0, keepdims=True), jnp.sum(delta, axis=0, keepdims=True)

    parts = [(views + sum(BATCHES[:i]), count) for i, count in enumerate(BATCHES)]
    before = None
    batch(0, views)
    forwards = []
    for first, count in parts:
        fresh = []
        for slot in range(first, first + count):
            s = slot - views + 1
            blocks[s - 1].wait_recv()
            place_x = x.at[slot, core]
            fresh.append(remote(place_x, place_x, fwd_send.at[s], fwd_recv.at[s], sibling))
        if before:
            batch(*before)
            if sum(before) == EARLY:
                for t in range(pairs):
                    top = jnp.max(tops[t], axis=0, keepdims=True)
                    total, delta = weigh(t, top, 0, EARLY * slot_rows // stride)
                    for i, row in enumerate((top, total, delta)):
                        sums[t, pl.ds(i, 1)] = row
        for copy in fresh:
            copy.wait_recv()
        forwards += fresh
        before = (first, count)
    batch(*before)
    sent += forwards

    lanes = pl.ds(pl.multiple_of(xx * quarter, LANES), quarter)
    xq[:, pl.ds(0, queries)] = x[pl.ds(0, views), :, :, lanes].reshape(queries, quarter).T
    for step in range(1, SIDE):
        early[step - 1].wait_recv()
        xq[:, pl.ds(step * queries, queries)] = xn_r[step - 1].reshape(queries, quarter).T

    def send_three(axis, source, target, send, recv, base):
        copies = []
        for step in (2, 1, 3):
            at, device = along(axis, step)
            copies.append(
                remote(source(at), target.at[step - 1], send.at[base + step - 1], recv.at[base + step - 1], device)
            )
        sent.extend(copies)
        return copies

    def collect(copies):
        for copy in copies:
            copy.wait_recv()

    place_of = (xx, yy, zz)
    orders = ((1, 2, 0), (2, 0, 1), (0, 2, 1))
    rows1 = gk.shape[3]
    rows2 = rows1 // SIDE

    def regroup(parts, rows):
        return [
            jnp.concatenate([part[k * rows : (k + 1) * rows] for part in parts], axis=0) for k in range(SIDE)
        ]

    def phase2(t, arrived):
        copies = []
        for m in range(2):
            arrived[m]()
            totals = []
            for j in range(SIDE):
                own = (gk.at[t, j, yy], gv.at[t, zz, j])[m]
                total = own[...].astype(F32)
                for i in range(SIDE - 1):
                    total = total + r1[t, m, i, j].astype(F32)
                totals.append(total)
            if m == 0:
                totals = regroup(totals, rows2)
            for j in range(SIDE):
                p2[t, m, j] = totals[j].astype(BF)
            copies.append(
                send_three(orders[m][1], lambda at, m=m: p2.at[t, m, at], r2.at[t, m], s2, d2, 9 * t + 3 * m)
            )
        return copies

    def second_sum(own, others):
        total = own[...].astype(F32)
        for i in range(SIDE - 1):
            total = total + others[i].astype(F32)
        return total

    def last_hop(total, axis, pieces, target, beside, unit):
        rows = total.shape[0] // (2 * SIDE)
        for j in range(SIDE):
            for h in range(2):
                pieces[j, h] = total[(2 * j + h) * rows : (2 * j + h + 1) * rows]
        copies = []
        for step in (2, 1, 3):
            at, device = along(axis, step)
            for cross in range(2):
                to = 1 - core if cross else core
                slot = 7 * unit + 2 * (step - 1) + cross
                copies.append(
                    remote(
                        pieces.at[at, to], target.at[cross, step - 1], s3.at[slot], d3.at[slot], device[:2] + (to,)
                    )
                )
        slot = 7 * unit + 6
        copies.append(remote(pieces.at[place_of[axis], 1 - core], beside, s3.at[slot], d3.at[slot], sibling))
        sent.extend(copies)
        return copies

    def arrive(copies, axis, pieces, target, beside, out, size, offset):
        collect(copies)
        span = out.shape[1] // 2
        total = pieces[place_of[axis], core] + target[0, 0] + target[0, 1] + target[0, 2]
        out[:, pl.ds(pl.multiple_of(core * span + offset, LANES), size)] = total
        total = beside[...] + target[1, 0] + target[1, 1] + target[1, 2]
        out[:, pl.ds(pl.multiple_of((1 - core) * span + offset, LANES), size)] = total

    def phase3(t, m, arrived):
        collect(arrived)
        total = second_sum(p2.at[t, m, place_of[orders[m][1]]], r2.at[t, m])
        return last_hop(total, orders[m][2], stage.at[t, m], got.at[t, m], near.at[t, m], 3 * t + m)

    def finish(t, m, arrived):
        arrive(
            arrived, orders[m][2], stage.at[t, m], got.at[t, m], near.at[t, m],
            (out_k, out_v, out_q)[m], LANES, t * LANES,
        )

    mixes, dqs = [], []

    def weights(t):
        top = jnp.max(tops[t], axis=0, keepdims=True)
        early_strides = EARLY * slot_rows // stride
        factor = jnp.exp(sums[t, 0:1] - top)
        total, delta = weigh(t, top, early_strides, strides)
        inverse = 1.0 / (total + factor * sums[t, 1:2])
        delta = (delta + factor * sums[t, 2:3]) * inverse

        def close(low, high, inverse):
            scaled = inverse * scale

            def body(i, carry):
                rows = pl.ds(pl.multiple_of(i * stride, stride), stride)
                e = s_all[t, rows]
                p_buf[rows] = (e * inverse).astype(BF)
                ds_buf[rows] = (e * scaled * (dp_all[t, rows] - delta)).astype(BF)
                return carry

            lax.fori_loop(low, high, body, 0)

        close(0, early_strides, inverse * factor)
        close(early_strides, strides, inverse)

        both = matmul(values[t].T, p_buf[...]).astype(BF)
        top = pl.multiple_of(core * half + t * LANES, LANES)
        mixed[pl.ds(top, HEAD_DIM)] = both[:HEAD_DIM, :queries]
        mixed[pl.ds(top + HEAD_DIM, HEAD_DIM)] = both[HEAD_DIM:, queries:]
        piece = mixed.at[pl.ds(top, LANES)]
        mixes.append(remote(piece, piece, mix_send.at[t], mix_recv.at[t], sibling))
        dq = matmul(keys[t].T, ds_buf[...])
        dq = jnp.concatenate((dq[:HEAD_DIM, :queries], dq[HEAD_DIM:, queries:]), axis=0).T
        dq_all[t, pl.ds(0, queries)] = dq.astype(BF)
        copies = []
        for hop in (2, 1, 3):
            slot = SIDE * (2 + t) + hop
            copies.append(
                remote(
                    dq_all.at[t, pl.ds(0, queries)], dq_all.at[t, pl.ds(hop * queries, queries)],
                    x_send.at[slot], x_recv.at[slot], along(0, hop)[1],
                )
            )
        dqs.append(copies)
        sent.extend(copies)

    def first_hop(t, m, i):
        copies = []
        for hop in (2, 1, 3):
            at, device = along(orders[m][0], hop)
            slot = 6 * t + 3 * m + hop - 1
            source, target = (gk.at[t, :, at], gv.at[t, at])[m], r1.at[t, m, hop - 1]
            if i is None:
                copies.append(
                    pltpu.make_async_remote_copy(
                        src_ref=source, dst_ref=target, send_sem=s1.at[slot], recv_sem=d1.at[slot],
                        device_id=device, device_id_type=MESH,
                    )
                )
            else:
                source = (gk.at[t, i, at], gv.at[t, at, i])[m]
                remote(source, target.at[i], s1.at[slot], d1.at[slot], device)
        return copies

    def key_grads(t):
        dkv[:, pl.ds(0, LANES)] = matmul(ds_buf[...], qm[t]).astype(BF)
        dkv[:, pl.ds(LANES, LANES)] = matmul(p_buf[...], om[t]).astype(BF)
        for i in range(SIDE):
            rows = pl.ds(i * quarter, quarter)
            kv = matmul(xt[rows], dkv[...])
            gk[t, i] = kv[:, :LANES].astype(BF).reshape(SIDE, rows1, LANES)
            first_hop(t, 0, i)
            v_part = kv[:, LANES:]
            parts = [v_part[y * rows1 : (y + 1) * rows1] for y in range(SIDE)]
            for z, turned in enumerate(regroup(parts, rows2)):
                gv[t, z, i] = turned.astype(BF)
            first_hop(t, 1, i)
        whole = [first_hop(t, m, None) for m in range(2)]
        sent.extend(whole[0] + whole[1])
        return [functools.partial(collect, copies) for copies in whole]

    channels = 2 * half
    share = channels // SIDE
    mxs = [[], []]

    def send_mixed(part):
        low, high = ((0, share // 3), (share // 3, share))[part]
        for hop in (2, 1, 3):
            at, device = along(0, hop)
            slot = SIDE * (2 + pairs + part) + hop
            mxs[part].append(
                remote(
                    mixed.at[pl.ds(pl.multiple_of(at * share + low, 16), high - low)],
                    mx_r.at[hop - 1, pl.ds(low, high - low)], x_send.at[slot], x_recv.at[slot], device,
                )
            )
        sent.extend(mxs[part])

    def query_grad(t):
        collect(dqs[t])
        g = matmul(xq[...], dq_all[t])
        parts = [g[y * rows1 : (y + 1) * rows1] for y in range(SIDE)]
        for z, turned in enumerate(regroup(parts, rows2)):
            p2[t, 2, z] = turned.astype(BF)
        return send_three(2, lambda at: p2.at[t, 2, at], r2.at[t, 2], s2, d2, 9 * t + 6)

    first, second, third = {}, {}, {}

    def hop2(t):
        second[t, 0], second[t, 1] = phase2(t, first[t])

    def hop3(t, *ms):
        for m in ms:
            third[t, m] = phase3(t, m, second[t, m])

    weights(0)
    first[0] = key_grads(0)
    weights(1)
    first[1] = key_grads(1)
    collect(mixes[:2])
    send_mixed(0)
    second[0, 2] = query_grad(0)
    weights(2)
    hop2(0)
    collect(mixes[2:])
    send_mixed(1)
    first[2] = key_grads(2)
    sent += mixes

    second[1, 2] = query_grad(1)
    hop3(0, 2, 0, 1)
    hop2(1)
    second[2, 2] = query_grad(2)
    hop3(1, 2)

    collect(early_up)
    own = mixed[pl.ds(pl.multiple_of(xx * share, 16), share)]
    g = matmul(own, up[core])
    for part in range(2):
        collect(mxs[part])
    for hop in range(1, SIDE):
        g = g + matmul(mx_r[hop - 1], up_r[hop - 1])
    o2[...] = g.astype(BF).reshape(SIDE, share // SIDE, width // 2)
    o_second = send_three(1, lambda at: o2.at[at], ro2, s2, d2, 9 * pairs)

    hop2(2)
    hop3(1, 0, 1)
    for m in range(3):
        finish(0, m, third[0, m])
    hop3(2, 2)
    collect(o_second)
    o_third = last_hop(second_sum(o2.at[yy], ro2), 2, stage_o, got_o, near_o, 3 * pairs)
    hop3(2, 0, 1)
    for m in range(3):
        finish(1, m, third[1, m])
    for m in (2, 0, 1):
        finish(2, m, third[2, m])
    arrive(o_third, 2, stage_o, got_o, near_o, out_o, width // 2, 0)
    for copy in sent:
        copy.wait_send()


def leave_kernel(*refs):
    count = len(refs) // 2
    for source, target in zip(refs[:count], refs[count:]):
        target[...] = source[...]


def leave(*results):
    return pl.pallas_call(
        leave_kernel,
        out_shape=tuple(jax.ShapeDtypeStruct(r.shape, r.dtype) for r in results),
    )(*results)


def shards(latents, norm_gain, w_query, w_key, w_value, w_out, kernel, partners, counts, cotangent):
    del counts
    views, _, columns, width = latents.shape[1:]
    inner = w_query.shape[1]
    half = inner // 2
    pairs = half // LANES
    groups = lax.axis_size("view")
    slots = groups - 1 + views
    slot_rows = 2 * columns
    key_rows = slots * slot_rows
    queries = views * slot_rows
    rows1 = width // 16
    orows = inner // 16
    vm = pltpu.VMEM
    dma = pltpu.SemaphoreType.DMA
    in_vmem = pl.BlockSpec(memory_space=pltpu.VMEM)
    in_hbm = pl.BlockSpec(memory_space=pl.ANY)
    results = pl.pallas_call(
        kernel_body,
        out_shape=(jax.ShapeDtypeStruct((rows1 // 8, inner), F32),) * 3
        + (jax.ShapeDtypeStruct((orows // 8, width), F32),),
        in_specs=[in_vmem] * 4 + [pl.BlockSpec(memory_space=pltpu.SMEM)] + [in_hbm] * 4,
        out_specs=(in_vmem,) * 4,
        scratch_shapes=[
            vm((slots, 2, columns, width), BF),
            vm((2, views, columns, width), BF),
            vm((groups, 8, LANES), jnp.int32),
            vm((groups, 8, LANES), jnp.int32),
            vm((groups - 1, columns, width), BF),
            vm((48, 2 * queries), F32),
            vm((width, half), BF),
            vm((width, 2 * half), BF),
            vm((half, width), BF),
            vm((width, key_rows), BF),
            vm((pairs, key_rows, LANES), BF),
            vm((pairs, key_rows, LANES), BF),
            vm((pairs, 2 * queries, LANES), BF),
            vm((pairs, 2 * queries, LANES), BF),
            vm((pairs, LANES, 2 * queries), BF),
            vm((pairs, LANES, 2 * queries), BF),
            vm((2, queries, width // 2), BF),
            vm((pairs, key_rows, 2 * queries), F32),
            vm((pairs, key_rows, 2 * queries), F32),
            vm((pairs, 8, 2 * queries), F32),
            vm((key_rows, 2 * queries), BF),
            vm((key_rows, 2 * queries), BF),
            vm((key_rows, 2 * LANES), BF),
            vm((2 * half, queries), BF),
            vm((pairs, SIDE, SIDE, rows1, LANES), BF),
            vm((pairs, SIDE, SIDE, rows1, LANES), BF),
            vm((pairs, 2, SIDE - 1, SIDE, rows1, LANES), BF),
            vm((pairs, 3, SIDE, rows1, LANES), BF),
            vm((pairs, 3, SIDE - 1, rows1, LANES), BF),
            vm((pairs, 3, SIDE, 2, rows1 // 8, LANES), F32),
            vm((pairs, 3, 2, SIDE - 1, rows1 // 8, LANES), F32),
            vm((pairs, 3, rows1 // 8, LANES), F32),
            vm((SIDE - 1, views, 2, columns, width // SIDE), BF),
            vm((width // SIDE, SIDE * queries), BF),
            vm((SIDE - 1, queries, width // 2), BF),
            vm((pairs, SIDE * queries, LANES), BF),
            vm((SIDE - 1, inner // SIDE, queries), BF),
            vm((pairs, 8, 2 * queries), F32),
            vm((SIDE, orows, width // 2), BF),
            vm((SIDE - 1, orows, width // 2), BF),
            vm((SIDE, 2, orows // 8, width // 2), F32),
            vm((2, SIDE - 1, orows // 8, width // 2), F32),
            vm((orows // 8, width // 2), F32),
            dma((4,)), dma((2,)), dma((2,)),
            dma((groups,)), dma((groups,)), dma((groups,)), dma((groups,)), dma((groups,)), dma((groups,)),
            dma((pairs,)), dma((pairs,)), dma((SIDE * (pairs + 4),)), dma((SIDE * (pairs + 4),)),
            dma((6 * pairs,)), dma((6 * pairs,)), dma((9 * pairs + 3,)), dma((9 * pairs + 3,)),
            dma((21 * pairs + 7,)), dma((21 * pairs + 7,)),
        ],
        compiler_params=pltpu.CompilerParams(
            collective_id=0, has_side_effects=True, vmem_limit_bytes=VMEM_LIMIT
        ),
    )(
        latents[0, :, 0], norm_gain, cotangent[0, :, 0], kernel, partners[0],
        w_query, w_key, w_value, w_out,
    )
    return leave(*results)


def solution(mesh):
    strips = P("scene", "view", "row", None, None)
    return jax.shard_map(
        shards,
        mesh=mesh,
        in_specs=(
            strips, P(), P(), P(), P(), P(), P(),
            P("scene", "view", None), P("scene", "view"), strips,
        ),
        out_specs=(P(("scene", "view", "row"), None),) * 4,
        check_vma=False,
    )
```

```python
import functools

import jax
import jax.numpy as jnp
from jax import lax
from jax.experimental import pallas as pl
from jax.experimental.pallas import tpu as pltpu
from jax.sharding import PartitionSpec as P

HEAD_DIM = 64
LANES = 128
EPSILON = 1e-06
SIDE = 4
OFFSETS = (
    (0, 1), (1, 0), (0, 3), (3, 0), (2, 2), (1, 1), (3, 3), (0, 2),
    (2, 0), (1, 3), (3, 1), (1, 2), (2, 1), (3, 2), (2, 3),
)
BATCHES = (4, 4, 4, 3)
EARLY = 8
MESH = pl.DeviceIdType.MESH
VMEM_LIMIT = 62 * 1024 * 1024
NT = (((1,), (1,)), ((), ()))
NN = (((1,), (0,)), ((), ()))
BF = jnp.bfloat16
F32 = jnp.float32


def matmul(a, b, dims=NN):
    return lax.dot_general(a, b, dims, preferred_element_type=F32)


def kernel_body(
    lat_hbm, gain_hbm, cot_hbm, taps_hbm, partners_hbm, wq_hbm, wk_hbm, wv_hbm, wo_hbm,
    out_q, out_k, out_v, out_o,
    lat, gain, taps, partners, x, cot_all, ask, grant, outbuf, bias,
    wq, wkv, wo, xt, keys, values, qm, om, qmt, omt, up, s_all, dp_all, tops, p_buf, ds_buf, dkv, mixed,
    gk, gv, r1, p2, r2, stage, got, near,
    xn_r, xq, up_r, dq_all, mx_r, sums, q2, rq2, stage_q, got_q, near_q, o2, ro2, stage_o, got_o, near_o,
    load_sem, small_sem, own_send, own_recv, ask_send, ask_recv, out_send, out_recv, fwd_send, fwd_recv,
    mix_send, mix_recv, x_send, x_recv, s1, d1, s2, d2, s3, d3,
):
    xx, me, core = lax.axis_index("scene"), lax.axis_index("view"), lax.axis_index("row")
    yy, zz = me // SIDE, lax.rem(me, SIDE)
    groups = SIDE * SIDE
    views, columns, width = lat.shape
    half = wq.shape[1]
    pairs = half // LANES
    slots = x.shape[0]
    slot_rows = 2 * columns
    key_rows = slots * slot_rows
    queries = views * slot_rows
    scale = HEAD_DIM ** (-0.5)
    sibling = (xx, me, 1 - core)

    def group_at(step, strip, sign):
        a, b = OFFSETS[step - 1]
        a, b = a + strip * (b - a), b + strip * (a - b)
        return lax.rem(yy + SIDE + sign * a, SIDE) * SIDE + lax.rem(zz + SIDE + sign * b, SIDE)

    def peer(step):
        return group_at(step, core, 1)

    def reverse(step):
        a, b = OFFSETS[step - 1]
        return OFFSETS.index(((SIDE - a) % SIDE, (SIDE - b) % SIDE)) + 1

    def along(axis, step):
        if axis == 0:
            at = lax.rem(xx + step, SIDE)
            return at, (at, me, core)
        if axis == 1:
            at = lax.rem(yy + step, SIDE)
            return at, (xx, at * SIDE + zz, core)
        at = lax.rem(zz + step, SIDE)
        return at, (xx, yy * SIDE + at, core)

    small = [
        pltpu.make_async_copy(partners_hbm, partners, small_sem.at[0]),
        pltpu.make_async_copy(lat_hbm, lat, small_sem.at[1]),
        pltpu.make_async_copy(gain_hbm, gain, small_sem.at[2]),
        pltpu.make_async_copy(cot_hbm, cot_all.at[core], small_sem.at[3]),
        pltpu.make_async_copy(taps_hbm, taps, small_sem.at[4]),
    ]
    for copy in small:
        copy.start()
    barrier = pltpu.get_barrier_semaphore()
    for step in range(1, groups):
        pl.semaphore_signal(barrier, inc=1, device_id=(xx, peer(step), core), device_id_type=MESH)
    for step in range(1, SIDE):
        pl.semaphore_signal(barrier, inc=1, device_id=along(0, step)[1], device_id_type=MESH)
        for axis in range(3):
            there = along(axis, step)[1][:2] + (1 - core,)
            pl.semaphore_signal(barrier, inc=1, device_id=there, device_id_type=MESH)
    pl.semaphore_signal(barrier, inc=1, device_id=sibling, device_id_type=MESH)

    cols = pl.ds(pl.multiple_of(core * half, LANES), half)
    loads = [
        pltpu.make_async_copy(wq_hbm.at[:, cols], wq, load_sem.at[0]),
        pltpu.make_async_copy(wk_hbm.at[:, cols], wkv.at[:, pl.ds(0, half)], load_sem.at[1]),
        pltpu.make_async_copy(wv_hbm.at[:, cols], wkv.at[:, pl.ds(half, half)], load_sem.at[2]),
        pltpu.make_async_copy(wo_hbm.at[cols, :], wo, load_sem.at[3]),
    ]
    for copy in loads:
        copy.start()

    steps_of = lax.broadcasted_iota(jnp.int32, (groups, LANES), 0)
    first_of = jnp.full((groups, LANES), -2 * views, jnp.int32)
    for s in range(1, groups):
        first_of = jnp.where(steps_of == s, peer(s) * views, first_of)
    wanted = jnp.zeros((groups, LANES), jnp.int32)
    small[0].wait()
    for v in range(views):
        for j in range(partners.shape[1]):
            local = partners[v, j] - first_of
            wanted = jnp.maximum(wanted, jnp.where((local >= 0) & (local < views), local, 0))
    for s in range(1, groups):
        ask[s] = jnp.broadcast_to(wanted[s : s + 1], ask.shape[1:])

    pl.semaphore_wait(barrier, groups + 4 * (SIDE - 1))

    def remote(src, dst, send, recv, device):
        copy = pltpu.make_async_remote_copy(
            src_ref=src, dst_ref=dst, send_sem=send, recv_sem=recv, device_id=device, device_id_type=MESH
        )
        copy.start()
        return copy

    sent = []
    asks = [
        remote(ask.at[s], grant.at[s], ask_send.at[s], ask_recv.at[s], (xx, peer(s), core))
        for s in range(1, groups)
    ]
    own_cot = remote(cot_hbm, cot_all.at[core], own_send.at[1], own_recv.at[1], sibling)

    for copy in small[1:3]:
        copy.wait()
    for v in range(views):
        rows = lat[v].astype(F32)
        mean = jnp.mean(rows * rows, -1, keepdims=True)
        x[v, core] = (rows * lax.rsqrt(mean + EPSILON) * gain[...].reshape(1, width)).astype(BF)

    mine = x.at[pl.ds(0, views), core]
    own_x = remote(mine, mine, own_send.at[0], own_recv.at[0], sibling)

    blocks = []
    for s in range(1, groups):
        asks[reverse(s) - 1].wait_recv()
        want = grant[reverse(s)][0:1, 0:1]
        block = x[0, core]
        for v in range(1, views):
            block = jnp.where(want == v, x[v, core], block)
        outbuf[s - 1] = block
        blocks.append(
            remote(
                outbuf.at[s - 1], x.at[views - 1 + s, core], out_send.at[s], out_recv.at[s], (xx, peer(s), core)
            )
        )
    sent += asks + [own_x, own_cot] + blocks

    quarter = width // SIDE
    own_x.wait_recv()
    early = []
    for step in range(1, SIDE):
        at, device = along(0, step)
        lanes = pl.ds(pl.multiple_of(at * quarter, LANES), quarter)
        early.append(
            remote(x.at[pl.ds(0, views), :, :, lanes], xn_r.at[step - 1], x_send.at[step], x_recv.at[step], device)
        )

    row_of = lax.broadcasted_iota(jnp.int32, (bias.shape[0], LANES), 0)
    first_of = jnp.full(row_of.shape, -2 * views, jnp.int32)
    for s in range(1, groups):
        for strip in range(2):
            first_of = jnp.where(row_of == 2 * (views - 1 + s) + strip, group_at(s, strip, -1) * views, first_of)
    lane_of = lax.broadcasted_iota(jnp.int32, (bias.shape[0], LANES), 1)
    seen = []
    for v in range(views):
        hit = jnp.where(row_of // 2 == v, 1, 0)
        for j in range(partners.shape[1]):
            number = partners[v, j]
            local = number - first_of
            hit = jnp.where((local >= 0) & (local < views) & (number >= 0), 1, hit)
        seen.append(jnp.where(hit > 0, 0.0, -1e30))
    for part in range(views // 2):
        both = jnp.where(lane_of < slot_rows, seen[2 * part], seen[2 * part + 1])
        for head in range(2):
            bias[:, pl.ds(head * queries + part * LANES, LANES)] = both

    for copy in small[3:]:
        copy.wait()
    own_cot.wait_recv()
    chunk = 2 * LANES
    place = lax.broadcasted_iota(jnp.int32, (columns, chunk), 0)

    def conv_view(view, carry):
        for part in range(width // chunk):
            lanes = pl.ds(part * chunk, chunk)
            kern = taps[:, lanes].astype(F32)
            shifted = []
            for strip in range(2):
                mid = cot_all[strip, view, :, lanes].astype(F32)
                after = jnp.where(place == columns - 1, 0.0, pltpu.roll(mid, columns - 1, 0))
                before = jnp.where(place == 0, 0.0, pltpu.roll(mid, 1, 0))
                shifted.append((after, mid, before))
            for strip in range(2):
                total = shifted[strip][1]
                for a, source in ((1, strip), (2 * strip, 1 - strip)):
                    for b in range(3):
                        total = total + kern[3 * a + b : 3 * a + b + 1] * shifted[source][b]
                side = part * chunk // (width // 2)
                rows = pl.ds(pl.multiple_of(view * slot_rows + strip * columns, columns), columns)
                up[side, rows, pl.ds(part * chunk - side * (width // 2), chunk)] = total.astype(BF)
        return carry

    lax.fori_loop(0, views, conv_view, 0)
    early_up = []
    for step in range(1, SIDE):
        early_up.append(
            remote(
                up.at[core], up_r.at[step - 1], x_send.at[SIDE + step], x_recv.at[SIDE + step], along(0, step)[1]
            )
        )
    sent += early + early_up

    for copy in loads:
        copy.wait()

    lane = lax.broadcasted_iota(jnp.int32, (queries, LANES), 1)
    sublane = lax.broadcasted_iota(jnp.int32, (LANES, queries), 0)

    def split_heads(out, turned, rows_f):
        rounded = rows_f.astype(BF).astype(F32)
        for pair in range(pairs):
            block = rounded[:, pair * LANES : (pair + 1) * LANES]
            out[pair, pl.ds(0, queries)] = jnp.where(lane < HEAD_DIM, block, 0.0).astype(BF)
            out[pair, pl.ds(queries, queries)] = jnp.where(lane < HEAD_DIM, 0.0, block).astype(BF)
            block = block.T
            turned[pair, :, pl.ds(0, queries)] = jnp.where(sublane < HEAD_DIM, block, 0.0).astype(BF)
            turned[pair, :, pl.ds(queries, queries)] = jnp.where(sublane < HEAD_DIM, 0.0, block).astype(BF)

    split_heads(
        om, omt,
        matmul(up[0], wo[:, pl.ds(0, width // 2)], NT) + matmul(up[1], wo[:, pl.ds(width // 2, width // 2)], NT),
    )
    split_heads(qm, qmt, matmul(x[pl.ds(0, views)].reshape(queries, width), wq[...]))

    tile = 2 * LANES

    def fold(v, op):
        return op(v.reshape(v.shape[0] // 8, 8, v.shape[1]), axis=0)

    def batch(first, count):
        rows = pl.ds(first * slot_rows, count * slot_rows)
        flat = x[pl.ds(first, count)].reshape(count * slot_rows, width)
        out = matmul(flat, wkv[...]).astype(BF)
        for pair in range(pairs):
            keys[pair, rows] = out[:, pair * LANES : (pair + 1) * LANES]
            values[pair, rows] = out[:, half + pair * LANES : half + (pair + 1) * LANES]

        for j in range(width // tile):
            lanes = pl.ds(j * tile, tile)
            xt[lanes, rows] = flat[:, j * tile : (j + 1) * tile].T

        for pair in range(pairs):
            s = matmul(keys[pair, rows], qmt[pair]) * scale
            top = jnp.full((8, 2 * queries), -3e38, F32) if first == 0 else tops[pair]
            for i in range(2 * count):
                part = s[i * columns : (i + 1) * columns] + bias[pl.ds(2 * first + i, 1)]
                s_all[pair, pl.ds(first * slot_rows + i * columns, columns)] = part
                top = jnp.maximum(top, fold(part, jnp.max))
            tops[pair] = top
            dp_all[pair, rows] = matmul(values[pair, rows], omt[pair])

    stride = 64
    strides = key_rows // stride

    def weigh(t, top, low, high):
        def body(i, carry):
            rows = pl.ds(pl.multiple_of(i * stride, stride), stride)
            e = jnp.exp(s_all[t, rows] - top)
            s_all[t, rows] = e
            return carry[0] + fold(e, jnp.sum), carry[1] + fold(e * dp_all[t, rows], jnp.sum)

        zero = jnp.zeros((8, 2 * queries), F32)
        total, delta = lax.fori_loop(low, high, body, (zero, zero))
        return jnp.sum(total, axis=0, keepdims=True), jnp.sum(delta, axis=0, keepdims=True)

    parts = [(views + sum(BATCHES[:i]), count) for i, count in enumerate(BATCHES)]
    def turn_quarters():
        lanes = pl.ds(pl.multiple_of(xx * quarter, LANES), quarter)
        xq[:, pl.ds(0, queries)] = x[pl.ds(0, views), :, :, lanes].reshape(queries, quarter).T
        for hop in range(1, SIDE):
            early[hop - 1].wait_recv()
            xq[:, pl.ds(hop * queries, queries)] = xn_r[hop - 1].reshape(queries, quarter).T

    before = None
    batch(0, views)
    forwards = []
    for first, count in parts:
        fresh = []
        for slot in range(first, first + count):
            s = slot - views + 1
            blocks[s - 1].wait_recv()
            place_x = x.at[slot, core]
            fresh.append(remote(place_x, place_x, fwd_send.at[s], fwd_recv.at[s], sibling))
        if before:
            batch(*before)
            if sum(before) == EARLY:
                for t in range(pairs):
                    top = jnp.max(tops[t], axis=0, keepdims=True)
                    total, delta = weigh(t, top, 0, EARLY * slot_rows // stride)
                    for i, row in enumerate((top, total, delta)):
                        sums[t, pl.ds(i, 1)] = row
            if sum(before) == EARLY + BATCHES[1]:
                turn_quarters()
        for copy in fresh:
            copy.wait_recv()
        forwards += fresh
        before = (first, count)
    batch(*before)
    sent += forwards

    def send_three(axis, source, target, send, recv, base):
        copies = []
        for step in (2, 1, 3):
            at, device = along(axis, step)
            copies.append(
                remote(source(at), target.at[step - 1], send.at[base + step - 1], recv.at[base + step - 1], device)
            )
        sent.extend(copies)
        return copies

    def collect(copies):
        for copy in copies:
            copy.wait_recv()

    place_of = (xx, yy, zz)
    orders = ((1, 2, 0), (2, 0, 1))
    rows1 = gk.shape[3]
    rows2 = rows1 // SIDE

    def regroup(parts, rows):
        return [
            jnp.concatenate([part[k * rows : (k + 1) * rows] for part in parts], axis=0) for k in range(SIDE)
        ]

    def phase2(t, arrived):
        copies = []
        for m in range(2):
            collect(arrived[m])
            totals = []
            for j in range(SIDE):
                own = (gk.at[t, j, yy], gv.at[t, zz, j])[m]
                total = own[...].astype(F32)
                for i in range(SIDE - 1):
                    total = total + r1[t, m, i, j].astype(F32)
                totals.append(total)
            if m == 0:
                totals = regroup(totals, rows2)
            for j in range(SIDE):
                p2[t, m, j] = totals[j].astype(BF)
            copies.append(
                send_three(orders[m][1], lambda at, m=m: p2.at[t, m, at], r2.at[t, m], s2, d2, 9 * t + 3 * m)
            )
        return copies

    def second_sum(own, others):
        total = own[...].astype(F32)
        for i in range(SIDE - 1):
            total = total + others[i].astype(F32)
        return total

    def last_hop(total, axis, pieces, target, beside, unit):
        rows = total.shape[0] // (2 * SIDE)
        for j in range(SIDE):
            for h in range(2):
                pieces[j, h] = total[(2 * j + h) * rows : (2 * j + h + 1) * rows]
        copies = []
        for step in (2, 1, 3):
            at, device = along(axis, step)
            for cross in range(2):
                to = 1 - core if cross else core
                slot = 7 * unit + 2 * (step - 1) + cross
                copies.append(
                    remote(
                        pieces.at[at, to], target.at[cross, step - 1], s3.at[slot], d3.at[slot], device[:2] + (to,)
                    )
                )
        slot = 7 * unit + 6
        copies.append(remote(pieces.at[place_of[axis], 1 - core], beside, s3.at[slot], d3.at[slot], sibling))
        sent.extend(copies)
        return copies

    def arrive(copies, axis, pieces, target, beside, out, size, offset):
        collect(copies)
        span = out.shape[1] // 2
        total = pieces[place_of[axis], core] + target[0, 0] + target[0, 1] + target[0, 2]
        out[:, pl.ds(pl.multiple_of(core * span + offset, LANES), size)] = total
        total = beside[...] + target[1, 0] + target[1, 1] + target[1, 2]
        out[:, pl.ds(pl.multiple_of((1 - core) * span + offset, LANES), size)] = total

    def phase3(t, m, arrived):
        collect(arrived)
        total = second_sum(p2.at[t, m, place_of[orders[m][1]]], r2.at[t, m])
        return last_hop(total, orders[m][2], stage.at[t, m], got.at[t, m], near.at[t, m], 3 * t + m)

    def finish(t, m, arrived):
        arrive(
            arrived, orders[m][2], stage.at[t, m], got.at[t, m], near.at[t, m],
            (out_k, out_v)[m], LANES, t * LANES,
        )

    mixes, dqs = [], []

    def weights(t):
        top = jnp.max(tops[t], axis=0, keepdims=True)
        early_strides = EARLY * slot_rows // stride
        factor = jnp.exp(sums[t, 0:1] - top)
        total, delta = weigh(t, top, early_strides, strides)
        inverse = 1.0 / (total + factor * sums[t, 1:2])
        delta = (delta + factor * sums[t, 2:3]) * inverse

        def close(low, high, inverse):
            scaled = inverse * scale

            def body(i, carry):
                rows = pl.ds(pl.multiple_of(i * stride, stride), stride)
                e = s_all[t, rows]
                p_buf[rows] = (e * inverse).astype(BF)
                ds_buf[rows] = (e * scaled * (dp_all[t, rows] - delta)).astype(BF)
                return carry

            lax.fori_loop(low, high, body, 0)

        close(0, early_strides, inverse * factor)
        close(early_strides, strides, inverse)

        both = matmul(values[t].T, p_buf[...]).astype(BF)
        top = pl.multiple_of(core * half + t * LANES, LANES)
        mixed[pl.ds(top, HEAD_DIM)] = both[:HEAD_DIM, :queries]
        mixed[pl.ds(top + HEAD_DIM, HEAD_DIM)] = both[HEAD_DIM:, queries:]
        piece = mixed.at[pl.ds(top, LANES)]
        mixes.append(remote(piece, piece, mix_send.at[t], mix_recv.at[t], sibling))
        dq = matmul(keys[t].T, ds_buf[...])
        dq = jnp.concatenate((dq[:HEAD_DIM, :queries], dq[HEAD_DIM:, queries:]), axis=0).T
        dq_all[t, pl.ds(0, queries)] = dq.astype(BF)
        copies = []
        for hop in (2, 1, 3):
            slot = SIDE * (2 + t) + hop
            copies.append(
                remote(
                    dq_all.at[t, pl.ds(0, queries)], dq_all.at[t, pl.ds(hop * queries, queries)],
                    x_send.at[slot], x_recv.at[slot], along(0, hop)[1],
                )
            )
        dqs.append(copies)
        sent.extend(copies)

    def first_hop(t):
        return [
            send_three(1, lambda at: gk.at[t, :, at], r1.at[t, 0], s1, d1, 6 * t),
            send_three(2, lambda at: gv.at[t, at], r1.at[t, 1], s1, d1, 6 * t + 3),
        ]

    def key_grads(t, between=None):
        dkv[:, pl.ds(0, LANES)] = matmul(ds_buf[...], qm[t]).astype(BF)
        dkv[:, pl.ds(LANES, LANES)] = matmul(p_buf[...], om[t]).astype(BF)
        for i in range(SIDE):
            rows = pl.ds(i * quarter, quarter)
            kv = matmul(xt[rows], dkv[...])
            gk[t, i] = kv[:, :LANES].astype(BF).reshape(SIDE, rows1, LANES)
            v_part = kv[:, LANES:]
            parts = [v_part[y * rows1 : (y + 1) * rows1] for y in range(SIDE)]
            for z, turned in enumerate(regroup(parts, rows2)):
                gv[t, z, i] = turned.astype(BF)
            if i == 1 and between:
                between()
        return first_hop(t)

    channels = 2 * half
    share = channels // SIDE
    mxs = [[], []]

    def send_mixed(part):
        low, high = ((0, share // 3), (share // 3, share))[part]
        for hop in (2, 1, 3):
            at, device = along(0, hop)
            slot = SIDE * (2 + pairs + part) + hop
            mxs[part].append(
                remote(
                    mixed.at[pl.ds(pl.multiple_of(at * share + low, 16), high - low)],
                    mx_r.at[hop - 1, pl.ds(low, high - low)], x_send.at[slot], x_recv.at[slot], device,
                )
            )
        sent.extend(mxs[part])

    def query_grad(t):
        collect(dqs[t])
        g = matmul(xq[...], dq_all[t])
        parts = [g[y * rows1 : (y + 1) * rows1] for y in range(SIDE)]
        for z, turned in enumerate(regroup(parts, rows2)):
            q2[z, :, pl.ds(t * LANES, LANES)] = turned.astype(BF)

    first, second, third = {}, {}, {}

    def hop2(t):
        second[t, 0], second[t, 1] = phase2(t, first[t])

    def hop3(t, *ms):
        for m in ms:
            third[t, m] = phase3(t, m, second[t, m])

    weights(0)
    first[0] = key_grads(0)
    weights(1)
    first[1] = key_grads(1)
    collect(mixes[:2])
    send_mixed(0)
    query_grad(0)
    weights(2)

    def last_mixed():
        collect(mixes[2:])
        send_mixed(1)

    first[2] = key_grads(2, last_mixed)
    hop2(0)
    sent += mixes

    query_grad(1)
    hop2(1)
    query_grad(2)
    q_second = send_three(2, lambda at: q2.at[at], rq2, s2, d2, 9 * pairs + 3)
    hop3(0, 0, 1)

    collect(early_up)
    own = mixed[pl.ds(pl.multiple_of(xx * share, 16), share)]
    g = matmul(own, up[core])
    for part in range(2):
        collect(mxs[part])
    for hop in range(1, SIDE):
        g = g + matmul(mx_r[hop - 1], up_r[hop - 1])
    o2[...] = g.astype(BF).reshape(SIDE, share // SIDE, width // 2)
    o_second = send_three(1, lambda at: o2.at[at], ro2, s2, d2, 9 * pairs)

    hop2(2)
    hop3(1, 0, 1)
    for m in range(2):
        finish(0, m, third[0, m])
    collect(q_second)
    q_third = last_hop(second_sum(q2.at[zz], rq2), 1, stage_q, got_q, near_q, 3 * pairs + 1)
    hop3(2, 0, 1)
    collect(o_second)
    o_third = last_hop(second_sum(o2.at[yy], ro2), 2, stage_o, got_o, near_o, 3 * pairs)
    for m in range(2):
        finish(1, m, third[1, m])
    arrive(q_third, 1, stage_q, got_q, near_q, out_q, half, 0)
    for m in range(2):
        finish(2, m, third[2, m])
    arrive(o_third, 2, stage_o, got_o, near_o, out_o, width // 2, 0)
    for copy in sent:
        copy.wait_send()


def leave_kernel(*refs):
    count = len(refs) // 2
    for source, target in zip(refs[:count], refs[count:]):
        target[...] = source[...]


def leave(*results):
    return pl.pallas_call(
        leave_kernel,
        out_shape=tuple(jax.ShapeDtypeStruct(r.shape, r.dtype) for r in results),
    )(*results)


def shards(latents, norm_gain, w_query, w_key, w_value, w_out, kernel, partners, counts, cotangent):
    del counts
    views, _, columns, width = latents.shape[1:]
    inner = w_query.shape[1]
    half = inner // 2
    pairs = half // LANES
    groups = lax.axis_size("view")
    slots = groups - 1 + views
    slot_rows = 2 * columns
    key_rows = slots * slot_rows
    queries = views * slot_rows
    rows1 = width // 16
    orows = inner // 16
    vm = pltpu.VMEM
    dma = pltpu.SemaphoreType.DMA
    in_vmem = pl.BlockSpec(memory_space=pltpu.VMEM)
    in_hbm = pl.BlockSpec(memory_space=pl.ANY)
    results = pl.pallas_call(
        kernel_body,
        out_shape=(jax.ShapeDtypeStruct((rows1 // 8, inner), F32),) * 3
        + (jax.ShapeDtypeStruct((orows // 8, width), F32),),
        in_specs=[in_hbm] * 9,
        out_specs=(in_vmem,) * 4,
        scratch_shapes=[
            vm((views, columns, width), BF),
            vm((width,), F32),
            vm(kernel.shape, BF),
            pltpu.SMEM(partners.shape[1:], jnp.int32),
            vm((slots, 2, columns, width), BF),
            vm((2, views, columns, width), BF),
            vm((groups, 8, LANES), jnp.int32),
            vm((groups, 8, LANES), jnp.int32),
            vm((groups - 1, columns, width), BF),
            vm((48, 2 * queries), F32),
            vm((width, half), BF),
            vm((width, 2 * half), BF),
            vm((half, width), BF),
            vm((width, key_rows), BF),
            vm((pairs, key_rows, LANES), BF),
            vm((pairs, key_rows, LANES), BF),
            vm((pairs, 2 * queries, LANES), BF),
            vm((pairs, 2 * queries, LANES), BF),
            vm((pairs, LANES, 2 * queries), BF),
            vm((pairs, LANES, 2 * queries), BF),
            vm((2, queries, width // 2), BF),
            vm((pairs, key_rows, 2 * queries), F32),
            vm((pairs, key_rows, 2 * queries), F32),
            vm((pairs, 8, 2 * queries), F32),
            vm((key_rows, 2 * queries), BF),
            vm((key_rows, 2 * queries), BF),
            vm((key_rows, 2 * LANES), BF),
            vm((2 * half, queries), BF),
            vm((pairs, SIDE, SIDE, rows1, LANES), BF),
            vm((pairs, SIDE, SIDE, rows1, LANES), BF),
            vm((pairs, 2, SIDE - 1, SIDE, rows1, LANES), BF),
            vm((pairs, 2, SIDE, rows1, LANES), BF),
            vm((pairs, 2, SIDE - 1, rows1, LANES), BF),
            vm((pairs, 2, SIDE, 2, rows1 // 8, LANES), F32),
            vm((pairs, 2, 2, SIDE - 1, rows1 // 8, LANES), F32),
            vm((pairs, 2, rows1 // 8, LANES), F32),
            vm((SIDE - 1, views, 2, columns, width // SIDE), BF),
            vm((width // SIDE, SIDE * queries), BF),
            vm((SIDE - 1, queries, width // 2), BF),
            vm((pairs, SIDE * queries, LANES), BF),
            vm((SIDE - 1, inner // SIDE, queries), BF),
            vm((pairs, 8, 2 * queries), F32),
            vm((SIDE, rows1, half), BF),
            vm((SIDE - 1, rows1, half), BF),
            vm((SIDE, 2, rows1 // 8, half), F32),
            vm((2, SIDE - 1, rows1 // 8, half), F32),
            vm((rows1 // 8, half), F32),
            vm((SIDE, orows, width // 2), BF),
            vm((SIDE - 1, orows, width // 2), BF),
            vm((SIDE, 2, orows // 8, width // 2), F32),
            vm((2, SIDE - 1, orows // 8, width // 2), F32),
            vm((orows // 8, width // 2), F32),
            dma((4,)), dma((5,)), dma((2,)), dma((2,)),
            dma((groups,)), dma((groups,)), dma((groups,)), dma((groups,)), dma((groups,)), dma((groups,)),
            dma((pairs,)), dma((pairs,)), dma((SIDE * (pairs + 4),)), dma((SIDE * (pairs + 4),)),
            dma((6 * pairs,)), dma((6 * pairs,)), dma((9 * pairs + 6,)), dma((9 * pairs + 6,)),
            dma((21 * pairs + 14,)), dma((21 * pairs + 14,)),
        ],
        compiler_params=pltpu.CompilerParams(
            collective_id=0, has_side_effects=True, vmem_limit_bytes=VMEM_LIMIT
        ),
    )(
        latents[0, :, 0], norm_gain, cotangent[0, :, 0], kernel, partners[0],
        w_query, w_key, w_value, w_out,
    )
    return leave(*results)


def solution(mesh):
    strips = P("scene", "view", "row", None, None)
    return jax.shard_map(
        shards,
        mesh=mesh,
        in_specs=(
            strips, P(), P(), P(), P(), P(), P(),
            P("scene", "view", None), P("scene", "view"), strips,
        ),
        out_specs=(P(("scene", "view", "row"), None),) * 4,
        check_vma=False,
    )
```

```python
import functools

import jax
import jax.numpy as jnp
from jax import lax
from jax.experimental import pallas as pl
from jax.experimental.pallas import tpu as pltpu
from jax.sharding import PartitionSpec as P

HEAD_DIM = 64
LANES = 128
EPSILON = 1e-06
SIDE = 4
OFFSETS = (
    (0, 1), (1, 0), (0, 3), (3, 0), (2, 2), (1, 1), (3, 3), (0, 2),
    (2, 0), (1, 3), (3, 1), (1, 2), (2, 1), (3, 2), (2, 3),
)
BATCHES = (4, 4, 4, 3)
EARLY = 8
MESH = pl.DeviceIdType.MESH
VMEM_LIMIT = 62 * 1024 * 1024
NT = (((1,), (1,)), ((), ()))
NN = (((1,), (0,)), ((), ()))
BF = jnp.bfloat16
F32 = jnp.float32


def matmul(a, b, dims=NN):
    return lax.dot_general(a, b, dims, preferred_element_type=F32)


def kernel_body(
    lat_hbm, gain_hbm, cot_hbm, taps_hbm, partners_hbm, wq_hbm, wk_hbm, wv_hbm, wo_hbm,
    out_q, out_k, out_v, out_o,
    lat, gain, taps, partners, x, cot_all, ask, grant, outbuf, bias,
    wq, wkv, wo, xt, keys, values, qm, om, qmt, omt, up, s_all, dp_all, tops, p_buf, ds_buf, dkv, mixed,
    gk, gv, r1, p2, r2, stage, got, near,
    xn_r, xq, up_r, dq_all, mx_r, sums, q2, rq2, stage_q, got_q, near_q, o2, ro2, stage_o, got_o, near_o,
    load_sem, small_sem, own_send, own_recv, ask_send, ask_recv, out_send, out_recv, fwd_send, fwd_recv,
    mix_send, mix_recv, x_send, x_recv, s1, d1, s2, d2, s3, d3,
):
    xx, me, core = lax.axis_index("scene"), lax.axis_index("view"), lax.axis_index("row")
    yy, zz = me // SIDE, lax.rem(me, SIDE)
    groups = SIDE * SIDE
    views, columns, width = lat.shape
    half = wq.shape[1]
    pairs = half // LANES
    slots = x.shape[0]
    slot_rows = 2 * columns
    key_rows = slots * slot_rows
    queries = views * slot_rows
    scale = HEAD_DIM ** (-0.5)
    sibling = (xx, me, 1 - core)

    def group_at(step, strip, sign):
        a, b = OFFSETS[step - 1]
        a, b = a + strip * (b - a), b + strip * (a - b)
        return lax.rem(yy + SIDE + sign * a, SIDE) * SIDE + lax.rem(zz + SIDE + sign * b, SIDE)

    def peer(step):
        return group_at(step, core, 1)

    def reverse(step):
        a, b = OFFSETS[step - 1]
        return OFFSETS.index(((SIDE - a) % SIDE, (SIDE - b) % SIDE)) + 1

    def along(axis, step):
        if axis == 0:
            at = lax.rem(xx + step, SIDE)
            return at, (at, me, core)
        if axis == 1:
            at = lax.rem(yy + step, SIDE)
            return at, (xx, at * SIDE + zz, core)
        at = lax.rem(zz + step, SIDE)
        return at, (xx, yy * SIDE + at, core)

    small = [
        pltpu.make_async_copy(partners_hbm, partners, small_sem.at[0]),
        pltpu.make_async_copy(lat_hbm, lat, small_sem.at[1]),
        pltpu.make_async_copy(gain_hbm, gain, small_sem.at[2]),
        pltpu.make_async_copy(cot_hbm, cot_all.at[core], small_sem.at[3]),
        pltpu.make_async_copy(taps_hbm, taps, small_sem.at[4]),
    ]
    for copy in small:
        copy.start()
    barrier = pltpu.get_barrier_semaphore()
    for step in range(1, groups):
        pl.semaphore_signal(barrier, inc=1, device_id=(xx, peer(step), core), device_id_type=MESH)
    for step in range(1, SIDE):
        pl.semaphore_signal(barrier, inc=1, device_id=along(0, step)[1], device_id_type=MESH)
        for axis in range(3):
            there = along(axis, step)[1][:2] + (1 - core,)
            pl.semaphore_signal(barrier, inc=1, device_id=there, device_id_type=MESH)
    pl.semaphore_signal(barrier, inc=1, device_id=sibling, device_id_type=MESH)

    cols = pl.ds(pl.multiple_of(core * half, LANES), half)
    loads = [
        pltpu.make_async_copy(wq_hbm.at[:, cols], wq, load_sem.at[0]),
        pltpu.make_async_copy(wk_hbm.at[:, cols], wkv.at[:, pl.ds(0, half)], load_sem.at[1]),
        pltpu.make_async_copy(wv_hbm.at[:, cols], wkv.at[:, pl.ds(half, half)], load_sem.at[2]),
        pltpu.make_async_copy(wo_hbm.at[cols, :], wo, load_sem.at[3]),
    ]
    for copy in loads:
        copy.start()

    steps_of = lax.broadcasted_iota(jnp.int32, (groups, LANES), 0)
    first_of = jnp.full((groups, LANES), -2 * views, jnp.int32)
    for s in range(1, groups):
        first_of = jnp.where(steps_of == s, peer(s) * views, first_of)
    wanted = jnp.zeros((groups, LANES), jnp.int32)
    small[0].wait()
    for v in range(views):
        for j in range(partners.shape[1]):
            local = partners[v, j] - first_of
            wanted = jnp.maximum(wanted, jnp.where((local >= 0) & (local < views), local, 0))
    for s in range(1, groups):
        ask[s] = jnp.broadcast_to(wanted[s : s + 1], ask.shape[1:])

    pl.semaphore_wait(barrier, groups + 4 * (SIDE - 1))

    def remote(src, dst, send, recv, device):
        copy = pltpu.make_async_remote_copy(
            src_ref=src, dst_ref=dst, send_sem=send, recv_sem=recv, device_id=device, device_id_type=MESH
        )
        copy.start()
        return copy

    sent = []
    asks = [
        remote(ask.at[s], grant.at[s], ask_send.at[s], ask_recv.at[s], (xx, peer(s), core))
        for s in range(1, groups)
    ]
    own_cot = remote(cot_hbm, cot_all.at[core], own_send.at[1], own_recv.at[1], sibling)

    for copy in small[1:3]:
        copy.wait()
    for v in range(views):
        rows = lat[v].astype(F32)
        mean = jnp.mean(rows * rows, -1, keepdims=True)
        x[v, core] = (rows * lax.rsqrt(mean + EPSILON) * gain[...].reshape(1, width)).astype(BF)

    mine = x.at[pl.ds(0, views), core]
    own_x = remote(mine, mine, own_send.at[0], own_recv.at[0], sibling)

    blocks = []
    for s in range(1, groups):
        asks[reverse(s) - 1].wait_recv()
        want = grant[reverse(s)][0:1, 0:1]
        block = x[0, core]
        for v in range(1, views):
            block = jnp.where(want == v, x[v, core], block)
        outbuf[s - 1] = block
        blocks.append(
            remote(
                outbuf.at[s - 1], x.at[views - 1 + s, core], out_send.at[s], out_recv.at[s], (xx, peer(s), core)
            )
        )
    sent += asks + [own_x, own_cot] + blocks

    quarter = width // SIDE
    own_x.wait_recv()
    early = []
    for step in range(1, SIDE):
        at, device = along(0, step)
        lanes = pl.ds(pl.multiple_of(at * quarter, LANES), quarter)
        early.append(
            remote(x.at[pl.ds(0, views), :, :, lanes], xn_r.at[step - 1], x_send.at[step], x_recv.at[step], device)
        )

    row_of = lax.broadcasted_iota(jnp.int32, (bias.shape[0], LANES), 0)
    first_of = jnp.full(row_of.shape, -2 * views, jnp.int32)
    for s in range(1, groups):
        for strip in range(2):
            first_of = jnp.where(row_of == 2 * (views - 1 + s) + strip, group_at(s, strip, -1) * views, first_of)
    lane_of = lax.broadcasted_iota(jnp.int32, (bias.shape[0], LANES), 1)
    seen = []
    for v in range(views):
        hit = jnp.where(row_of // 2 == v, 1, 0)
        for j in range(partners.shape[1]):
            number = partners[v, j]
            local = number - first_of
            hit = jnp.where((local >= 0) & (local < views) & (number >= 0), 1, hit)
        seen.append(jnp.where(hit > 0, 0.0, -1e30))
    for part in range(views // 2):
        both = jnp.where(lane_of < slot_rows, seen[2 * part], seen[2 * part + 1])
        for head in range(2):
            bias[:, pl.ds(head * queries + part * LANES, LANES)] = both

    for copy in small[3:]:
        copy.wait()
    own_cot.wait_recv()
    chunk = 2 * LANES
    place = lax.broadcasted_iota(jnp.int32, (columns, chunk), 0)

    def conv_view(view, carry):
        for part in range(width // chunk):
            lanes = pl.ds(part * chunk, chunk)
            kern = taps[:, lanes].astype(F32)
            shifted = []
            for strip in range(2):
                mid = cot_all[strip, view, :, lanes].astype(F32)
                after = jnp.where(place == columns - 1, 0.0, pltpu.roll(mid, columns - 1, 0))
                before = jnp.where(place == 0, 0.0, pltpu.roll(mid, 1, 0))
                shifted.append((after, mid, before))
            for strip in range(2):
                total = shifted[strip][1]
                for a, source in ((1, strip), (2 * strip, 1 - strip)):
                    for b in range(3):
                        total = total + kern[3 * a + b : 3 * a + b + 1] * shifted[source][b]
                side = part * chunk // (width // 2)
                rows = pl.ds(pl.multiple_of(view * slot_rows + strip * columns, columns), columns)
                up[side, rows, pl.ds(part * chunk - side * (width // 2), chunk)] = total.astype(BF)
        return carry

    lax.fori_loop(0, views, conv_view, 0)
    early_up = []
    for step in range(1, SIDE):
        early_up.append(
            remote(
                up.at[core], up_r.at[step - 1], x_send.at[SIDE + step], x_recv.at[SIDE + step], along(0, step)[1]
            )
        )
    sent += early + early_up

    for copy in loads:
        copy.wait()

    lane = lax.broadcasted_iota(jnp.int32, (queries, LANES), 1)
    sublane = lax.broadcasted_iota(jnp.int32, (LANES, queries), 0)

    def split_heads(out, turned, rows_f):
        rounded = rows_f.astype(BF).astype(F32)
        for pair in range(pairs):
            block = rounded[:, pair * LANES : (pair + 1) * LANES]
            out[pair, pl.ds(0, queries)] = jnp.where(lane < HEAD_DIM, block, 0.0).astype(BF)
            out[pair, pl.ds(queries, queries)] = jnp.where(lane < HEAD_DIM, 0.0, block).astype(BF)
            block = block.T
            turned[pair, :, pl.ds(0, queries)] = jnp.where(sublane < HEAD_DIM, block, 0.0).astype(BF)
            turned[pair, :, pl.ds(queries, queries)] = jnp.where(sublane < HEAD_DIM, 0.0, block).astype(BF)

    split_heads(
        om, omt,
        matmul(up[0], wo[:, pl.ds(0, width // 2)], NT) + matmul(up[1], wo[:, pl.ds(width // 2, width // 2)], NT),
    )
    split_heads(qm, qmt, matmul(x[pl.ds(0, views)].reshape(queries, width), wq[...]))

    tile = 2 * LANES

    def fold(v, op):
        return op(v.reshape(v.shape[0] // 8, 8, v.shape[1]), axis=0)

    def batch(first, count):
        rows = pl.ds(first * slot_rows, count * slot_rows)
        flat = x[pl.ds(first, count)].reshape(count * slot_rows, width)
        out = matmul(flat, wkv[...]).astype(BF)
        for pair in range(pairs):
            keys[pair, rows] = out[:, pair * LANES : (pair + 1) * LANES]
            values[pair, rows] = out[:, half + pair * LANES : half + (pair + 1) * LANES]

        for j in range(width // tile):
            lanes = pl.ds(j * tile, tile)
            xt[lanes, rows] = flat[:, j * tile : (j + 1) * tile].T

        for pair in range(pairs):
            s = matmul(keys[pair, rows], qmt[pair]) * scale
            top = jnp.full((8, 2 * queries), -3e38, F32) if first == 0 else tops[pair]
            for i in range(2 * count):
                part = s[i * columns : (i + 1) * columns] + bias[pl.ds(2 * first + i, 1)]
                s_all[pair, pl.ds(first * slot_rows + i * columns, columns)] = part
                top = jnp.maximum(top, fold(part, jnp.max))
            tops[pair] = top
            dp_all[pair, rows] = matmul(values[pair, rows], omt[pair])

    stride = 64
    strides = key_rows // stride

    def weigh(t, top, low, high):
        def body(i, carry):
            rows = pl.ds(pl.multiple_of(i * stride, stride), stride)
            e = jnp.exp(s_all[t, rows] - top)
            s_all[t, rows] = e
            return carry[0] + fold(e, jnp.sum), carry[1] + fold(e * dp_all[t, rows], jnp.sum)

        zero = jnp.zeros((8, 2 * queries), F32)
        total, delta = lax.fori_loop(low, high, body, (zero, zero))
        return jnp.sum(total, axis=0, keepdims=True), jnp.sum(delta, axis=0, keepdims=True)

    parts = [(views + sum(BATCHES[:i]), count) for i, count in enumerate(BATCHES)]
    def turn_quarters():
        lanes = pl.ds(pl.multiple_of(xx * quarter, LANES), quarter)
        xq[:, pl.ds(0, queries)] = x[pl.ds(0, views), :, :, lanes].reshape(queries, quarter).T
        for hop in range(1, SIDE):
            early[hop - 1].wait_recv()
            xq[:, pl.ds(hop * queries, queries)] = xn_r[hop - 1].reshape(queries, quarter).T

    before = None
    batch(0, views)
    forwards = []
    for first, count in parts:
        fresh = []
        for slot in range(first, first + count):
            s = slot - views + 1
            blocks[s - 1].wait_recv()
            place_x = x.at[slot, core]
            fresh.append(remote(place_x, place_x, fwd_send.at[s], fwd_recv.at[s], sibling))
        if before:
            batch(*before)
            if sum(before) == EARLY:
                for t in range(pairs):
                    top = jnp.max(tops[t], axis=0, keepdims=True)
                    total, delta = weigh(t, top, 0, EARLY * slot_rows // stride)
                    for i, row in enumerate((top, total, delta)):
                        sums[t, pl.ds(i, 1)] = row
            if sum(before) == EARLY + BATCHES[1]:
                turn_quarters()
        for copy in fresh:
            copy.wait_recv()
        forwards += fresh
        before = (first, count)
    batch(*before)
    sent += forwards

    def send_three(axis, source, target, send, recv, base):
        copies = []
        for step in (2, 1, 3):
            at, device = along(axis, step)
            copies.append(
                remote(source(at), target.at[step - 1], send.at[base + step - 1], recv.at[base + step - 1], device)
            )
        sent.extend(copies)
        return copies

    def collect(copies):
        for copy in copies:
            copy.wait_recv()

    place_of = (xx, yy, zz)
    orders = ((1, 2, 0), (2, 0, 1))
    rows1 = gk.shape[3]
    rows2 = rows1 // SIDE

    def regroup(parts, rows):
        return [
            jnp.concatenate([part[k * rows : (k + 1) * rows] for part in parts], axis=0) for k in range(SIDE)
        ]

    def phase2(t, arrived):
        copies = []
        for m in range(2):
            collect(arrived[m])
            totals = []
            for j in range(SIDE):
                own = (gk.at[t, j, yy], gv.at[t, zz, j])[m]
                total = own[...].astype(F32)
                for i in range(SIDE - 1):
                    total = total + r1[t, m, i, j].astype(F32)
                totals.append(total)
            if m == 0:
                totals = regroup(totals, rows2)
            for j in range(SIDE):
                p2[t, m, j] = totals[j].astype(BF)
            copies.append(
                send_three(orders[m][1], lambda at, m=m: p2.at[t, m, at], r2.at[t, m], s2, d2, 9 * t + 3 * m)
            )
        return copies

    def second_sum(own, others):
        total = own[...].astype(F32)
        for i in range(SIDE - 1):
            total = total + others[i].astype(F32)
        return total

    def last_hop(total, axis, pieces, target, beside, unit):
        rows = total.shape[0] // (2 * SIDE)
        for j in range(SIDE):
            for h in range(2):
                pieces[j, h] = total[(2 * j + h) * rows : (2 * j + h + 1) * rows]
        copies = []
        for step in (2, 1, 3):
            at, device = along(axis, step)
            for cross in range(2):
                to = 1 - core if cross else core
                slot = 7 * unit + 2 * (step - 1) + cross
                copies.append(
                    remote(
                        pieces.at[at, to], target.at[cross, step - 1], s3.at[slot], d3.at[slot], device[:2] + (to,)
                    )
                )
        slot = 7 * unit + 6
        copies.append(remote(pieces.at[place_of[axis], 1 - core], beside, s3.at[slot], d3.at[slot], sibling))
        sent.extend(copies)
        return copies

    def arrive(copies, axis, pieces, target, beside, out, size, offset):
        collect(copies)
        span = out.shape[1] // 2
        total = pieces[place_of[axis], core] + target[0, 0] + target[0, 1] + target[0, 2]
        out[:, pl.ds(pl.multiple_of(core * span + offset, LANES), size)] = total
        total = beside[...] + target[1, 0] + target[1, 1] + target[1, 2]
        out[:, pl.ds(pl.multiple_of((1 - core) * span + offset, LANES), size)] = total

    def phase3(t, m, arrived):
        collect(arrived)
        total = second_sum(p2.at[t, m, place_of[orders[m][1]]], r2.at[t, m])
        return last_hop(total, orders[m][2], stage.at[t, m], got.at[t, m], near.at[t, m], 3 * t + m)

    def finish(t, m, arrived):
        arrive(
            arrived, orders[m][2], stage.at[t, m], got.at[t, m], near.at[t, m],
            (out_k, out_v)[m], LANES, t * LANES,
        )

    mixes, dqs = [], []

    early_strides = EARLY * slot_rows // stride

    def rest(t, unrolled):
        top = jnp.max(tops[t], axis=0, keepdims=True)
        factor = jnp.exp(sums[t, 0:1] - top)
        if unrolled:
            total, delta = jnp.zeros((8, 2 * queries), F32), jnp.zeros((8, 2 * queries), F32)
            for i in range(early_strides, strides):
                rows = pl.ds(i * stride, stride)
                e = jnp.exp(s_all[t, rows] - top)
                s_all[t, rows] = e
                total, delta = total + fold(e, jnp.sum), delta + fold(e * dp_all[t, rows], jnp.sum)
            total, delta = jnp.sum(total, axis=0, keepdims=True), jnp.sum(delta, axis=0, keepdims=True)
        else:
            total, delta = weigh(t, top, early_strides, strides)
        inverse = 1.0 / (total + factor * sums[t, 1:2])
        return inverse * factor, inverse, (delta + factor * sums[t, 2:3]) * inverse

    def close(t, low, high, inverse, delta, unrolled):
        scaled = inverse * scale

        def body(i, carry):
            start = i * stride if unrolled else pl.multiple_of(i * stride, stride)
            rows = pl.ds(start, stride)
            e = s_all[t, rows]
            p_buf[rows] = (e * inverse).astype(BF)
            ds_buf[rows] = (e * scaled * (dp_all[t, rows] - delta)).astype(BF)
            return carry

        if unrolled:
            for i in range(low, high):
                body(i, 0)
        else:
            lax.fori_loop(low, high, body, 0)

    def weights(t):
        first_inverse, inverse, delta = rest(t, False)
        close(t, 0, early_strides, first_inverse, delta, False)
        close(t, early_strides, strides, inverse, delta, False)

    def from_queries(t):
        both = matmul(values[t].T, p_buf[...]).astype(BF)
        top = pl.multiple_of(core * half + t * LANES, LANES)
        mixed[pl.ds(top, HEAD_DIM)] = both[:HEAD_DIM, :queries]
        mixed[pl.ds(top + HEAD_DIM, HEAD_DIM)] = both[HEAD_DIM:, queries:]
        piece = mixed.at[pl.ds(top, LANES)]
        mixes.append(remote(piece, piece, mix_send.at[t], mix_recv.at[t], sibling))
        dq = matmul(keys[t].T, ds_buf[...])
        dq = jnp.concatenate((dq[:HEAD_DIM, :queries], dq[HEAD_DIM:, queries:]), axis=0).T
        dq_all[t, pl.ds(0, queries)] = dq.astype(BF)
        copies = []
        for hop in (2, 1, 3):
            slot = SIDE * (2 + t) + hop
            copies.append(
                remote(
                    dq_all.at[t, pl.ds(0, queries)], dq_all.at[t, pl.ds(hop * queries, queries)],
                    x_send.at[slot], x_recv.at[slot], along(0, hop)[1],
                )
            )
        dqs.append(copies)
        sent.extend(copies)

    def first_hop(t):
        return [
            send_three(1, lambda at: gk.at[t, :, at], r1.at[t, 0], s1, d1, 6 * t),
            send_three(2, lambda at: gv.at[t, at], r1.at[t, 1], s1, d1, 6 * t + 3),
        ]

    def key_grads(t, between=None, follow=None):
        dkv[:, pl.ds(0, LANES)] = matmul(ds_buf[...], qm[t]).astype(BF)
        dkv[:, pl.ds(LANES, LANES)] = matmul(p_buf[...], om[t]).astype(BF)
        for i in range(SIDE):
            rows = pl.ds(i * quarter, quarter)
            kv = matmul(xt[rows], dkv[...])
            gk[t, i] = kv[:, :LANES].astype(BF).reshape(SIDE, rows1, LANES)
            v_part = kv[:, LANES:]
            parts = [v_part[y * rows1 : (y + 1) * rows1] for y in range(SIDE)]
            for z, turned in enumerate(regroup(parts, rows2)):
                gv[t, z, i] = turned.astype(BF)
            if i == 1 and between:
                between()
            if follow is not None and i == 0:
                first_inverse, inverse, delta = rest(follow, True)
            elif follow is not None:
                low = early_strides + (strides - early_strides) * (i - 2) // 2
                high = early_strides + (strides - early_strides) * (i - 1) // 2
                if i == 1:
                    close(follow, 0, early_strides, first_inverse, delta, True)
                else:
                    close(follow, low, high, inverse, delta, True)
        return first_hop(t)

    channels = 2 * half
    share = channels // SIDE
    mxs = [[], []]

    def send_mixed(part):
        low, high = ((0, share // 3), (share // 3, share))[part]
        for hop in (2, 1, 3):
            at, device = along(0, hop)
            slot = SIDE * (2 + pairs + part) + hop
            mxs[part].append(
                remote(
                    mixed.at[pl.ds(pl.multiple_of(at * share + low, 16), high - low)],
                    mx_r.at[hop - 1, pl.ds(low, high - low)], x_send.at[slot], x_recv.at[slot], device,
                )
            )
        sent.extend(mxs[part])

    def query_grad(t):
        collect(dqs[t])
        g = matmul(xq[...], dq_all[t])
        parts = [g[y * rows1 : (y + 1) * rows1] for y in range(SIDE)]
        for z, turned in enumerate(regroup(parts, rows2)):
            q2[z, :, pl.ds(t * LANES, LANES)] = turned.astype(BF)

    first, second, third = {}, {}, {}

    def hop2(t):
        second[t, 0], second[t, 1] = phase2(t, first[t])

    def hop3(t, *ms):
        for m in ms:
            third[t, m] = phase3(t, m, second[t, m])

    weights(0)
    from_queries(0)
    first[0] = key_grads(0, follow=1)
    from_queries(1)
    first[1] = key_grads(1, follow=2)
    collect(mixes[:2])
    send_mixed(0)
    query_grad(0)
    from_queries(2)

    def last_mixed():
        collect(mixes[2:])
        send_mixed(1)

    first[2] = key_grads(2, last_mixed)
    hop2(0)
    sent += mixes

    query_grad(1)
    hop2(1)
    query_grad(2)
    q_second = send_three(2, lambda at: q2.at[at], rq2, s2, d2, 9 * pairs + 3)
    hop3(0, 0, 1)

    collect(early_up)
    own = mixed[pl.ds(pl.multiple_of(xx * share, 16), share)]
    g = matmul(own, up[core])
    for part in range(2):
        collect(mxs[part])
    for hop in range(1, SIDE):
        g = g + matmul(mx_r[hop - 1], up_r[hop - 1])
    o2[...] = g.astype(BF).reshape(SIDE, share // SIDE, width // 2)
    o_second = send_three(1, lambda at: o2.at[at], ro2, s2, d2, 9 * pairs)

    hop2(2)
    hop3(1, 0, 1)
    for m in range(2):
        finish(0, m, third[0, m])
    collect(q_second)
    q_third = last_hop(second_sum(q2.at[zz], rq2), 1, stage_q, got_q, near_q, 3 * pairs + 1)
    hop3(2, 0, 1)
    collect(o_second)
    o_third = last_hop(second_sum(o2.at[yy], ro2), 2, stage_o, got_o, near_o, 3 * pairs)
    for copy in sent:
        copy.wait_send()
    for m in range(2):
        finish(1, m, third[1, m])
    arrive(q_third, 1, stage_q, got_q, near_q, out_q, half, 0)
    for m in range(2):
        finish(2, m, third[2, m])
    arrive(o_third, 2, stage_o, got_o, near_o, out_o, width // 2, 0)


def leave_kernel(*refs):
    count = len(refs) // 2
    for source, target in zip(refs[:count], refs[count:]):
        target[...] = source[...]


def leave(*results):
    return pl.pallas_call(
        leave_kernel,
        out_shape=tuple(jax.ShapeDtypeStruct(r.shape, r.dtype) for r in results),
    )(*results)


def shards(latents, norm_gain, w_query, w_key, w_value, w_out, kernel, partners, counts, cotangent):
    del counts
    views, _, columns, width = latents.shape[1:]
    inner = w_query.shape[1]
    half = inner // 2
    pairs = half // LANES
    groups = lax.axis_size("view")
    slots = groups - 1 + views
    slot_rows = 2 * columns
    key_rows = slots * slot_rows
    queries = views * slot_rows
    rows1 = width // 16
    orows = inner // 16
    vm = pltpu.VMEM
    dma = pltpu.SemaphoreType.DMA
    in_vmem = pl.BlockSpec(memory_space=pltpu.VMEM)
    in_hbm = pl.BlockSpec(memory_space=pl.ANY)
    results = pl.pallas_call(
        kernel_body,
        out_shape=(jax.ShapeDtypeStruct((rows1 // 8, inner), F32),) * 3
        + (jax.ShapeDtypeStruct((orows // 8, width), F32),),
        in_specs=[in_hbm] * 9,
        out_specs=(in_vmem,) * 4,
        scratch_shapes=[
            vm((views, columns, width), BF),
            vm((width,), F32),
            vm(kernel.shape, BF),
            pltpu.SMEM(partners.shape[1:], jnp.int32),
            vm((slots, 2, columns, width), BF),
            vm((2, views, columns, width), BF),
            vm((groups, 8, LANES), jnp.int32),
            vm((groups, 8, LANES), jnp.int32),
            vm((groups - 1, columns, width), BF),
            vm((48, 2 * queries), F32),
            vm((width, half), BF),
            vm((width, 2 * half), BF),
            vm((half, width), BF),
            vm((width, key_rows), BF),
            vm((pairs, key_rows, LANES), BF),
            vm((pairs, key_rows, LANES), BF),
            vm((pairs, 2 * queries, LANES), BF),
            vm((pairs, 2 * queries, LANES), BF),
            vm((pairs, LANES, 2 * queries), BF),
            vm((pairs, LANES, 2 * queries), BF),
            vm((2, queries, width // 2), BF),
            vm((pairs, key_rows, 2 * queries), F32),
            vm((pairs, key_rows, 2 * queries), F32),
            vm((pairs, 8, 2 * queries), F32),
            vm((key_rows, 2 * queries), BF),
            vm((key_rows, 2 * queries), BF),
            vm((key_rows, 2 * LANES), BF),
            vm((2 * half, queries), BF),
            vm((pairs, SIDE, SIDE, rows1, LANES), BF),
            vm((pairs, SIDE, SIDE, rows1, LANES), BF),
            vm((pairs, 2, SIDE - 1, SIDE, rows1, LANES), BF),
            vm((pairs, 2, SIDE, rows1, LANES), BF),
            vm((pairs, 2, SIDE - 1, rows1, LANES), BF),
            vm((pairs, 2, SIDE, 2, rows1 // 8, LANES), F32),
            vm((pairs, 2, 2, SIDE - 1, rows1 // 8, LANES), F32),
            vm((pairs, 2, rows1 // 8, LANES), F32),
            vm((SIDE - 1, views, 2, columns, width // SIDE), BF),
            vm((width // SIDE, SIDE * queries), BF),
            vm((SIDE - 1, queries, width // 2), BF),
            vm((pairs, SIDE * queries, LANES), BF),
            vm((SIDE - 1, inner // SIDE, queries), BF),
            vm((pairs, 8, 2 * queries), F32),
            vm((SIDE, rows1, half), BF),
            vm((SIDE - 1, rows1, half), BF),
            vm((SIDE, 2, rows1 // 8, half), F32),
            vm((2, SIDE - 1, rows1 // 8, half), F32),
            vm((rows1 // 8, half), F32),
            vm((SIDE, orows, width // 2), BF),
            vm((SIDE - 1, orows, width // 2), BF),
            vm((SIDE, 2, orows // 8, width // 2), F32),
            vm((2, SIDE - 1, orows // 8, width // 2), F32),
            vm((orows // 8, width // 2), F32),
            dma((4,)), dma((5,)), dma((2,)), dma((2,)),
            dma((groups,)), dma((groups,)), dma((groups,)), dma((groups,)), dma((groups,)), dma((groups,)),
            dma((pairs,)), dma((pairs,)), dma((SIDE * (pairs + 4),)), dma((SIDE * (pairs + 4),)),
            dma((6 * pairs,)), dma((6 * pairs,)), dma((9 * pairs + 6,)), dma((9 * pairs + 6,)),
            dma((21 * pairs + 14,)), dma((21 * pairs + 14,)),
        ],
        compiler_params=pltpu.CompilerParams(
            collective_id=0, has_side_effects=True, vmem_limit_bytes=VMEM_LIMIT
        ),
    )(
        latents[0, :, 0], norm_gain, cotangent[0, :, 0], kernel, partners[0],
        w_query, w_key, w_value, w_out,
    )
    return leave(*results)


def solution(mesh):
    strips = P("scene", "view", "row", None, None)
    return jax.shard_map(
        shards,
        mesh=mesh,
        in_specs=(
            strips, P(), P(), P(), P(), P(), P(),
            P("scene", "view", None), P("scene", "view"), strips,
        ),
        out_specs=(P(("scene", "view", "row"), None),) * 4,
        check_vma=False,
    )
```

```python
import functools

import jax
import jax.numpy as jnp
from jax import lax
from jax.experimental import pallas as pl
from jax.experimental.pallas import tpu as pltpu
from jax.sharding import PartitionSpec as P

HEAD_DIM = 64
LANES = 128
EPSILON = 1e-06
SIDE = 4
OFFSETS = (
    (0, 1), (1, 0), (0, 3), (3, 0), (2, 2), (1, 1), (3, 3), (0, 2),
    (2, 0), (1, 3), (3, 1), (1, 2), (2, 1), (3, 2), (2, 3),
)
BATCHES = (4, 4, 4, 3)
EARLY = 8
MESH = pl.DeviceIdType.MESH
VMEM_LIMIT = 62 * 1024 * 1024
NT = (((1,), (1,)), ((), ()))
NN = (((1,), (0,)), ((), ()))
BF = jnp.bfloat16
F32 = jnp.float32


def matmul(a, b, dims=NN):
    return lax.dot_general(a, b, dims, preferred_element_type=F32)


def kernel_body(
    lat_hbm, gain_hbm, cot_hbm, taps_hbm, partners_hbm, wq_hbm, wk_hbm, wv_hbm, wo_hbm,
    out_q, out_k, out_v, out_o,
    lat, gain, taps, partners, x, cot_all, ask, grant, outbuf, bias,
    wq, wkv, wo, xt, keys, values, qm, om, qmt, omt, up, s_all, dp_all, tops, p_buf, ds_buf, dkv, mixed,
    gk, gv, r1, p2, r2, stage, got, near,
    xn_r, xq, up_r, dq_all, mx_r, sums, q2, rq2, stage_q, got_q, near_q, o2, ro2, stage_o, got_o, near_o,
    load_sem, small_sem, own_send, own_recv, ask_send, ask_recv, out_send, out_recv, fwd_send, fwd_recv,
    mix_send, mix_recv, x_send, x_recv, s1, d1, s2, d2, s3, d3,
):
    xx, me, core = lax.axis_index("scene"), lax.axis_index("view"), lax.axis_index("row")
    yy, zz = me // SIDE, lax.rem(me, SIDE)
    groups = SIDE * SIDE
    views, columns, width = lat.shape
    half = wq.shape[1]
    pairs = half // LANES
    slots = x.shape[0]
    slot_rows = 2 * columns
    key_rows = slots * slot_rows
    queries = views * slot_rows
    scale = HEAD_DIM ** (-0.5)
    sibling = (xx, me, 1 - core)

    def group_at(step, strip, sign):
        a, b = OFFSETS[step - 1]
        a, b = a + strip * (b - a), b + strip * (a - b)
        return lax.rem(yy + SIDE + sign * a, SIDE) * SIDE + lax.rem(zz + SIDE + sign * b, SIDE)

    def peer(step):
        return group_at(step, core, 1)

    def reverse(step):
        a, b = OFFSETS[step - 1]
        return OFFSETS.index(((SIDE - a) % SIDE, (SIDE - b) % SIDE)) + 1

    def along(axis, step):
        if axis == 0:
            at = lax.rem(xx + step, SIDE)
            return at, (at, me, core)
        if axis == 1:
            at = lax.rem(yy + step, SIDE)
            return at, (xx, at * SIDE + zz, core)
        at = lax.rem(zz + step, SIDE)
        return at, (xx, yy * SIDE + at, core)

    small = [
        pltpu.make_async_copy(partners_hbm, partners, small_sem.at[0]),
        pltpu.make_async_copy(lat_hbm, lat, small_sem.at[1]),
        pltpu.make_async_copy(gain_hbm, gain, small_sem.at[2]),
        pltpu.make_async_copy(cot_hbm, cot_all.at[core], small_sem.at[3]),
        pltpu.make_async_copy(taps_hbm, taps, small_sem.at[4]),
    ]
    for copy in small:
        copy.start()
    barrier = pltpu.get_barrier_semaphore()
    for step in range(1, groups):
        pl.semaphore_signal(barrier, inc=1, device_id=(xx, peer(step), core), device_id_type=MESH)
    for step in range(1, SIDE):
        pl.semaphore_signal(barrier, inc=1, device_id=along(0, step)[1], device_id_type=MESH)
        for axis in range(3):
            there = along(axis, step)[1][:2] + (1 - core,)
            pl.semaphore_signal(barrier, inc=1, device_id=there, device_id_type=MESH)
    pl.semaphore_signal(barrier, inc=1, device_id=sibling, device_id_type=MESH)

    cols = pl.ds(pl.multiple_of(core * half, LANES), half)
    loads = [
        pltpu.make_async_copy(wq_hbm.at[:, cols], wq, load_sem.at[0]),
        pltpu.make_async_copy(wk_hbm.at[:, cols], wkv.at[:, pl.ds(0, half)], load_sem.at[1]),
        pltpu.make_async_copy(wv_hbm.at[:, cols], wkv.at[:, pl.ds(half, half)], load_sem.at[2]),
        pltpu.make_async_copy(wo_hbm.at[cols, :], wo, load_sem.at[3]),
    ]
    for copy in loads:
        copy.start()

    steps_of = lax.broadcasted_iota(jnp.int32, (groups, LANES), 0)
    first_of = jnp.full((groups, LANES), -2 * views, jnp.int32)
    for s in range(1, groups):
        first_of = jnp.where(steps_of == s, peer(s) * views, first_of)
    wanted = jnp.zeros((groups, LANES), jnp.int32)
    small[0].wait()
    for v in range(views):
        for j in range(partners.shape[1]):
            local = partners[v, j] - first_of
            wanted = jnp.maximum(wanted, jnp.where((local >= 0) & (local < views), local, 0))
    for s in range(1, groups):
        ask[s] = jnp.broadcast_to(wanted[s : s + 1], ask.shape[1:])

    pl.semaphore_wait(barrier, groups + 4 * (SIDE - 1))

    def remote(src, dst, send, recv, device):
        copy = pltpu.make_async_remote_copy(
            src_ref=src, dst_ref=dst, send_sem=send, recv_sem=recv, device_id=device, device_id_type=MESH
        )
        copy.start()
        return copy

    sent = []
    asks = [
        remote(ask.at[s], grant.at[s], ask_send.at[s], ask_recv.at[s], (xx, peer(s), core))
        for s in range(1, groups)
    ]
    own_cot = remote(cot_hbm, cot_all.at[core], own_send.at[1], own_recv.at[1], sibling)

    for copy in small[1:3]:
        copy.wait()
    for v in range(views):
        rows = lat[v].astype(F32)
        mean = jnp.mean(rows * rows, -1, keepdims=True)
        x[v, core] = (rows * lax.rsqrt(mean + EPSILON) * gain[...].reshape(1, width)).astype(BF)

    mine = x.at[pl.ds(0, views), core]
    own_x = remote(mine, mine, own_send.at[0], own_recv.at[0], sibling)

    blocks = []
    for s in range(1, groups):
        asks[reverse(s) - 1].wait_recv()
        want = grant[reverse(s)][0:1, 0:1]
        block = x[0, core]
        for v in range(1, views):
            block = jnp.where(want == v, x[v, core], block)
        outbuf[s - 1] = block
        blocks.append(
            remote(
                outbuf.at[s - 1], x.at[views - 1 + s, core], out_send.at[s], out_recv.at[s], (xx, peer(s), core)
            )
        )
    sent += asks + [own_x, own_cot] + blocks

    quarter = width // SIDE
    own_x.wait_recv()
    early = []
    for step in range(1, SIDE):
        at, device = along(0, step)
        lanes = pl.ds(pl.multiple_of(at * quarter, LANES), quarter)
        early.append(
            remote(x.at[pl.ds(0, views), :, :, lanes], xn_r.at[step - 1], x_send.at[step], x_recv.at[step], device)
        )

    row_of = lax.broadcasted_iota(jnp.int32, (bias.shape[0], LANES), 0)
    first_of = jnp.full(row_of.shape, -2 * views, jnp.int32)
    for s in range(1, groups):
        for strip in range(2):
            first_of = jnp.where(row_of == 2 * (views - 1 + s) + strip, group_at(s, strip, -1) * views, first_of)
    lane_of = lax.broadcasted_iota(jnp.int32, (bias.shape[0], LANES), 1)
    seen = []
    for v in range(views):
        hit = jnp.where(row_of // 2 == v, 1, 0)
        for j in range(partners.shape[1]):
            number = partners[v, j]
            local = number - first_of
            hit = jnp.where((local >= 0) & (local < views) & (number >= 0), 1, hit)
        seen.append(jnp.where(hit > 0, 0.0, -1e30))
    for part in range(views // 2):
        both = jnp.where(lane_of < slot_rows, seen[2 * part], seen[2 * part + 1])
        for head in range(2):
            bias[:, pl.ds(head * queries + part * LANES, LANES)] = both

    for copy in small[3:]:
        copy.wait()
    own_cot.wait_recv()
    chunk = 2 * LANES
    place = lax.broadcasted_iota(jnp.int32, (columns, chunk), 0)

    def conv_view(view, carry):
        for part in range(width // chunk):
            lanes = pl.ds(part * chunk, chunk)
            kern = taps[:, lanes].astype(F32)
            shifted = []
            for strip in range(2):
                mid = cot_all[strip, view, :, lanes].astype(F32)
                after = jnp.where(place == columns - 1, 0.0, pltpu.roll(mid, columns - 1, 0))
                before = jnp.where(place == 0, 0.0, pltpu.roll(mid, 1, 0))
                shifted.append((after, mid, before))
            for strip in range(2):
                total = shifted[strip][1]
                for a, source in ((1, strip), (2 * strip, 1 - strip)):
                    for b in range(3):
                        total = total + kern[3 * a + b : 3 * a + b + 1] * shifted[source][b]
                side = part * chunk // (width // 2)
                rows = pl.ds(pl.multiple_of(view * slot_rows + strip * columns, columns), columns)
                up[side, rows, pl.ds(part * chunk - side * (width // 2), chunk)] = total.astype(BF)
        return carry

    lax.fori_loop(0, views, conv_view, 0)
    early_up = []
    for step in range(1, SIDE):
        early_up.append(
            remote(
                up.at[core], up_r.at[step - 1], x_send.at[SIDE + step], x_recv.at[SIDE + step], along(0, step)[1]
            )
        )
    sent += early + early_up

    for copy in loads:
        copy.wait()

    lane = lax.broadcasted_iota(jnp.int32, (queries, LANES), 1)
    sublane = lax.broadcasted_iota(jnp.int32, (LANES, queries), 0)

    def split_heads(out, turned, rows_f):
        rounded = rows_f.astype(BF).astype(F32)
        for pair in range(pairs):
            block = rounded[:, pair * LANES : (pair + 1) * LANES]
            out[pair, pl.ds(0, queries)] = jnp.where(lane < HEAD_DIM, block, 0.0).astype(BF)
            out[pair, pl.ds(queries, queries)] = jnp.where(lane < HEAD_DIM, 0.0, block).astype(BF)
            block = block.T
            turned[pair, :, pl.ds(0, queries)] = jnp.where(sublane < HEAD_DIM, block, 0.0).astype(BF)
            turned[pair, :, pl.ds(queries, queries)] = jnp.where(sublane < HEAD_DIM, 0.0, block).astype(BF)

    split_heads(
        om, omt,
        matmul(up[0], wo[:, pl.ds(0, width // 2)], NT) + matmul(up[1], wo[:, pl.ds(width // 2, width // 2)], NT),
    )
    split_heads(qm, qmt, matmul(x[pl.ds(0, views)].reshape(queries, width), wq[...]))

    tile = 2 * LANES

    def fold(v, op):
        return op(v.reshape(v.shape[0] // 8, 8, v.shape[1]), axis=0)

    def batch(first, count):
        rows = pl.ds(first * slot_rows, count * slot_rows)
        flat = x[pl.ds(first, count)].reshape(count * slot_rows, width)
        out = matmul(flat, wkv[...]).astype(BF)
        for pair in range(pairs):
            keys[pair, rows] = out[:, pair * LANES : (pair + 1) * LANES]
            values[pair, rows] = out[:, half + pair * LANES : half + (pair + 1) * LANES]

        for j in range(width // tile):
            lanes = pl.ds(j * tile, tile)
            xt[lanes, rows] = flat[:, j * tile : (j + 1) * tile].T

        for pair in range(pairs):
            s = matmul(keys[pair, rows], qmt[pair]) * scale
            top = jnp.full((8, 2 * queries), -3e38, F32) if first == 0 else tops[pair]
            for i in range(2 * count):
                part = s[i * columns : (i + 1) * columns] + bias[pl.ds(2 * first + i, 1)]
                s_all[pair, pl.ds(first * slot_rows + i * columns, columns)] = part
                top = jnp.maximum(top, fold(part, jnp.max))
            tops[pair] = top
            dp_all[pair, rows] = matmul(values[pair, rows], omt[pair])

    stride = 64
    strides = key_rows // stride

    def weigh(t, top, low, high):
        def body(i, carry):
            rows = pl.ds(pl.multiple_of(i * stride, stride), stride)
            e = jnp.exp(s_all[t, rows] - top)
            s_all[t, rows] = e
            return carry[0] + fold(e, jnp.sum), carry[1] + fold(e * dp_all[t, rows], jnp.sum)

        zero = jnp.zeros((8, 2 * queries), F32)
        total, delta = lax.fori_loop(low, high, body, (zero, zero))
        return jnp.sum(total, axis=0, keepdims=True), jnp.sum(delta, axis=0, keepdims=True)

    parts = [(views + sum(BATCHES[:i]), count) for i, count in enumerate(BATCHES)]
    def turn_quarters():
        lanes = pl.ds(pl.multiple_of(xx * quarter, LANES), quarter)
        xq[:, pl.ds(0, queries)] = x[pl.ds(0, views), :, :, lanes].reshape(queries, quarter).T
        for hop in range(1, SIDE):
            early[hop - 1].wait_recv()
            xq[:, pl.ds(hop * queries, queries)] = xn_r[hop - 1].reshape(queries, quarter).T

    before = None
    batch(0, views)
    forwards = []
    for first, count in parts:
        fresh = []
        for slot in range(first, first + count):
            s = slot - views + 1
            blocks[s - 1].wait_recv()
            place_x = x.at[slot, core]
            fresh.append(remote(place_x, place_x, fwd_send.at[s], fwd_recv.at[s], sibling))
        if before:
            batch(*before)
            if sum(before) == EARLY:
                for t in range(pairs):
                    top = jnp.max(tops[t], axis=0, keepdims=True)
                    total, delta = weigh(t, top, 0, EARLY * slot_rows // stride)
                    for i, row in enumerate((top, total, delta)):
                        sums[t, pl.ds(i, 1)] = row
            if sum(before) == EARLY + BATCHES[1]:
                turn_quarters()
        for copy in fresh:
            copy.wait_recv()
        forwards += fresh
        before = (first, count)
    batch(*before)
    sent += forwards

    def send_three(axis, source, target, send, recv, base):
        copies = []
        for step in (2, 1, 3):
            at, device = along(axis, step)
            copies.append(
                remote(source(at), target.at[step - 1], send.at[base + step - 1], recv.at[base + step - 1], device)
            )
        sent.extend(copies)
        return copies

    def collect(copies):
        for copy in copies:
            copy.wait_recv()

    place_of = (xx, yy, zz)
    orders = ((1, 2, 0), (2, 0, 1))
    rows1 = gk.shape[3]
    rows2 = rows1 // SIDE

    def regroup(parts, rows):
        return [
            jnp.concatenate([part[k * rows : (k + 1) * rows] for part in parts], axis=0) for k in range(SIDE)
        ]

    def phase2(t, arrived):
        copies = []
        for m in range(2):
            collect(arrived[m])
            totals = []
            for j in range(SIDE):
                own = (gk.at[t, j, yy], gv.at[t, zz, j])[m]
                total = own[...].astype(F32)
                for i in range(SIDE - 1):
                    total = total + r1[t, m, i, j].astype(F32)
                totals.append(total)
            if m == 0:
                totals = regroup(totals, rows2)
            for j in range(SIDE):
                p2[t, m, j] = totals[j].astype(BF)
            copies.append(
                send_three(orders[m][1], lambda at, m=m: p2.at[t, m, at], r2.at[t, m], s2, d2, 9 * t + 3 * m)
            )
        return copies

    def second_sum(own, others):
        total = own[...].astype(F32)
        for i in range(SIDE - 1):
            total = total + others[i].astype(F32)
        return total

    def last_hop(total, axis, pieces, target, beside, unit):
        rows = total.shape[0] // (2 * SIDE)
        for j in range(SIDE):
            for h in range(2):
                pieces[j, h] = total[(2 * j + h) * rows : (2 * j + h + 1) * rows]
        copies = []
        for step in (2, 1, 3):
            at, device = along(axis, step)
            for cross in range(2):
                to = 1 - core if cross else core
                slot = 7 * unit + 2 * (step - 1) + cross
                copies.append(
                    remote(
                        pieces.at[at, to], target.at[cross, step - 1], s3.at[slot], d3.at[slot], device[:2] + (to,)
                    )
                )
        slot = 7 * unit + 6
        copies.append(remote(pieces.at[place_of[axis], 1 - core], beside, s3.at[slot], d3.at[slot], sibling))
        sent.extend(copies)
        return copies

    def arrive(copies, axis, pieces, target, beside, out, size, offset):
        collect(copies)
        span = out.shape[1] // 2
        total = pieces[place_of[axis], core] + target[0, 0] + target[0, 1] + target[0, 2]
        out[:, pl.ds(pl.multiple_of(core * span + offset, LANES), size)] = total
        total = beside[...] + target[1, 0] + target[1, 1] + target[1, 2]
        out[:, pl.ds(pl.multiple_of((1 - core) * span + offset, LANES), size)] = total

    def phase3(t, m, arrived):
        collect(arrived)
        total = second_sum(p2.at[t, m, place_of[orders[m][1]]], r2.at[t, m])
        return last_hop(total, orders[m][2], stage.at[t, m], got.at[t, m], near.at[t, m], 3 * t + m)

    def finish(t, m, arrived):
        arrive(
            arrived, orders[m][2], stage.at[t, m], got.at[t, m], near.at[t, m],
            (out_k, out_v)[m], LANES, t * LANES,
        )

    mixes, dqs = [], []

    early_strides = EARLY * slot_rows // stride

    def rest(t, unrolled):
        top = jnp.max(tops[t], axis=0, keepdims=True)
        factor = jnp.exp(sums[t, 0:1] - top)
        if unrolled:
            total, delta = jnp.zeros((8, 2 * queries), F32), jnp.zeros((8, 2 * queries), F32)
            for i in range(early_strides, strides):
                rows = pl.ds(i * stride, stride)
                e = jnp.exp(s_all[t, rows] - top)
                s_all[t, rows] = e
                total, delta = total + fold(e, jnp.sum), delta + fold(e * dp_all[t, rows], jnp.sum)
            total, delta = jnp.sum(total, axis=0, keepdims=True), jnp.sum(delta, axis=0, keepdims=True)
        else:
            total, delta = weigh(t, top, early_strides, strides)
        inverse = 1.0 / (total + factor * sums[t, 1:2])
        return inverse * factor, inverse, (delta + factor * sums[t, 2:3]) * inverse

    def close(t, low, high, inverse, delta, unrolled):
        scaled = inverse * scale

        def body(i, carry):
            start = i * stride if unrolled else pl.multiple_of(i * stride, stride)
            rows = pl.ds(start, stride)
            e = s_all[t, rows]
            p_buf[rows] = (e * inverse).astype(BF)
            ds_buf[rows] = (e * scaled * (dp_all[t, rows] - delta)).astype(BF)
            return carry

        if unrolled:
            for i in range(low, high):
                body(i, 0)
        else:
            lax.fori_loop(low, high, body, 0)

    def weights(t):
        first_inverse, inverse, delta = rest(t, True)
        close(t, 0, early_strides, first_inverse, delta, True)
        close(t, early_strides, strides, inverse, delta, True)

    def from_queries(t):
        both = matmul(values[t].T, p_buf[...]).astype(BF)
        top = pl.multiple_of(core * half + t * LANES, LANES)
        mixed[pl.ds(top, HEAD_DIM)] = both[:HEAD_DIM, :queries]
        mixed[pl.ds(top + HEAD_DIM, HEAD_DIM)] = both[HEAD_DIM:, queries:]
        piece = mixed.at[pl.ds(top, LANES)]
        mixes.append(remote(piece, piece, mix_send.at[t], mix_recv.at[t], sibling))
        dq = matmul(keys[t].T, ds_buf[...])
        dq = jnp.concatenate((dq[:HEAD_DIM, :queries], dq[HEAD_DIM:, queries:]), axis=0).T
        dq_all[t, pl.ds(0, queries)] = dq.astype(BF)
        copies = []
        for hop in (2, 1, 3):
            slot = SIDE * (2 + t) + hop
            copies.append(
                remote(
                    dq_all.at[t, pl.ds(0, queries)], dq_all.at[t, pl.ds(hop * queries, queries)],
                    x_send.at[slot], x_recv.at[slot], along(0, hop)[1],
                )
            )
        dqs.append(copies)
        sent.extend(copies)

    def first_hop(t):
        return [
            send_three(1, lambda at: gk.at[t, :, at], r1.at[t, 0], s1, d1, 6 * t),
            send_three(2, lambda at: gv.at[t, at], r1.at[t, 1], s1, d1, 6 * t + 3),
        ]

    def key_grads(t, between=None, follow=None):
        dkv[:, pl.ds(0, LANES)] = matmul(ds_buf[...], qm[t]).astype(BF)
        dkv[:, pl.ds(LANES, LANES)] = matmul(p_buf[...], om[t]).astype(BF)
        for i in range(SIDE):
            rows = pl.ds(i * quarter, quarter)
            kv = matmul(xt[rows], dkv[...])
            gk[t, i] = kv[:, :LANES].astype(BF).reshape(SIDE, rows1, LANES)
            v_part = kv[:, LANES:]
            parts = [v_part[y * rows1 : (y + 1) * rows1] for y in range(SIDE)]
            for z, turned in enumerate(regroup(parts, rows2)):
                gv[t, z, i] = turned.astype(BF)
            if i == 1 and between:
                between()
            if follow is not None and i == 0:
                first_inverse, inverse, delta = rest(follow, True)
            elif follow is not None:
                low = early_strides + (strides - early_strides) * (i - 2) // 2
                high = early_strides + (strides - early_strides) * (i - 1) // 2
                if i == 1:
                    close(follow, 0, early_strides, first_inverse, delta, True)
                else:
                    close(follow, low, high, inverse, delta, True)
        return first_hop(t)

    channels = 2 * half
    share = channels // SIDE
    mxs = [[], []]

    def send_mixed(part):
        low, high = ((0, share // 3), (share // 3, share))[part]
        for hop in (2, 1, 3):
            at, device = along(0, hop)
            slot = SIDE * (2 + pairs + part) + hop
            mxs[part].append(
                remote(
                    mixed.at[pl.ds(pl.multiple_of(at * share + low, 16), high - low)],
                    mx_r.at[hop - 1, pl.ds(low, high - low)], x_send.at[slot], x_recv.at[slot], device,
                )
            )
        sent.extend(mxs[part])

    def query_grad(t):
        collect(dqs[t])
        g = matmul(xq[...], dq_all[t])
        parts = [g[y * rows1 : (y + 1) * rows1] for y in range(SIDE)]
        for z, turned in enumerate(regroup(parts, rows2)):
            q2[z, :, pl.ds(t * LANES, LANES)] = turned.astype(BF)

    first, second, third = {}, {}, {}

    def hop2(t):
        second[t, 0], second[t, 1] = phase2(t, first[t])

    def hop3(t, *ms):
        for m in ms:
            third[t, m] = phase3(t, m, second[t, m])

    weights(0)
    from_queries(0)
    first[0] = key_grads(0, follow=1)
    from_queries(1)
    first[1] = key_grads(1, follow=2)
    collect(mixes[:2])
    send_mixed(0)
    query_grad(0)
    from_queries(2)

    def last_mixed():
        collect(mixes[2:])
        send_mixed(1)

    first[2] = key_grads(2, last_mixed)
    hop2(0)
    sent += mixes

    query_grad(1)
    hop2(1)
    query_grad(2)
    q_second = send_three(2, lambda at: q2.at[at], rq2, s2, d2, 9 * pairs + 3)
    hop3(0, 0, 1)

    collect(early_up)
    own = mixed[pl.ds(pl.multiple_of(xx * share, 16), share)]
    g = matmul(own, up[core])
    for part in range(2):
        collect(mxs[part])
    for hop in range(1, SIDE):
        g = g + matmul(mx_r[hop - 1], up_r[hop - 1])
    o2[...] = g.astype(BF).reshape(SIDE, share // SIDE, width // 2)
    o_second = send_three(1, lambda at: o2.at[at], ro2, s2, d2, 9 * pairs)

    hop2(2)
    hop3(1, 0, 1)
    for m in range(2):
        finish(0, m, third[0, m])
    collect(q_second)
    q_third = last_hop(second_sum(q2.at[zz], rq2), 1, stage_q, got_q, near_q, 3 * pairs + 1)
    hop3(2, 0, 1)
    collect(o_second)
    o_third = last_hop(second_sum(o2.at[yy], ro2), 2, stage_o, got_o, near_o, 3 * pairs)
    for copy in sent:
        copy.wait_send()
    for m in range(2):
        finish(1, m, third[1, m])
    arrive(q_third, 1, stage_q, got_q, near_q, out_q, half, 0)
    for m in range(2):
        finish(2, m, third[2, m])
    arrive(o_third, 2, stage_o, got_o, near_o, out_o, width // 2, 0)


def leave_kernel(*refs):
    count = len(refs) // 2
    for source, target in zip(refs[:count], refs[count:]):
        target[...] = source[...]


def leave(*results):
    return pl.pallas_call(
        leave_kernel,
        out_shape=tuple(jax.ShapeDtypeStruct(r.shape, r.dtype) for r in results),
    )(*results)


def shards(latents, norm_gain, w_query, w_key, w_value, w_out, kernel, partners, counts, cotangent):
    del counts
    views, _, columns, width = latents.shape[1:]
    inner = w_query.shape[1]
    half = inner // 2
    pairs = half // LANES
    groups = lax.axis_size("view")
    slots = groups - 1 + views
    slot_rows = 2 * columns
    key_rows = slots * slot_rows
    queries = views * slot_rows
    rows1 = width // 16
    orows = inner // 16
    vm = pltpu.VMEM
    dma = pltpu.SemaphoreType.DMA
    in_vmem = pl.BlockSpec(memory_space=pltpu.VMEM)
    in_hbm = pl.BlockSpec(memory_space=pl.ANY)
    results = pl.pallas_call(
        kernel_body,
        out_shape=(jax.ShapeDtypeStruct((rows1 // 8, inner), F32),) * 3
        + (jax.ShapeDtypeStruct((orows // 8, width), F32),),
        in_specs=[in_hbm] * 9,
        out_specs=(in_vmem,) * 4,
        scratch_shapes=[
            vm((views, columns, width), BF),
            vm((width,), F32),
            vm(kernel.shape, BF),
            pltpu.SMEM(partners.shape[1:], jnp.int32),
            vm((slots, 2, columns, width), BF),
            vm((2, views, columns, width), BF),
            vm((groups, 8, LANES), jnp.int32),
            vm((groups, 8, LANES), jnp.int32),
            vm((groups - 1, columns, width), BF),
            vm((48, 2 * queries), F32),
            vm((width, half), BF),
            vm((width, 2 * half), BF),
            vm((half, width), BF),
            vm((width, key_rows), BF),
            vm((pairs, key_rows, LANES), BF),
            vm((pairs, key_rows, LANES), BF),
            vm((pairs, 2 * queries, LANES), BF),
            vm((pairs, 2 * queries, LANES), BF),
            vm((pairs, LANES, 2 * queries), BF),
            vm((pairs, LANES, 2 * queries), BF),
            vm((2, queries, width // 2), BF),
            vm((pairs, key_rows, 2 * queries), F32),
            vm((pairs, key_rows, 2 * queries), F32),
            vm((pairs, 8, 2 * queries), F32),
            vm((key_rows, 2 * queries), BF),
            vm((key_rows, 2 * queries), BF),
            vm((key_rows, 2 * LANES), BF),
            vm((2 * half, queries), BF),
            vm((pairs, SIDE, SIDE, rows1, LANES), BF),
            vm((pairs, SIDE, SIDE, rows1, LANES), BF),
            vm((pairs, 2, SIDE - 1, SIDE, rows1, LANES), BF),
            vm((pairs, 2, SIDE, rows1, LANES), BF),
            vm((pairs, 2, SIDE - 1, rows1, LANES), BF),
            vm((pairs, 2, SIDE, 2, rows1 // 8, LANES), F32),
            vm((pairs, 2, 2, SIDE - 1, rows1 // 8, LANES), F32),
            vm((pairs, 2, rows1 // 8, LANES), F32),
            vm((SIDE - 1, views, 2, columns, width // SIDE), BF),
            vm((width // SIDE, SIDE * queries), BF),
            vm((SIDE - 1, queries, width // 2), BF),
            vm((pairs, SIDE * queries, LANES), BF),
            vm((SIDE - 1, inner // SIDE, queries), BF),
            vm((pairs, 8, 2 * queries), F32),
            vm((SIDE, rows1, half), BF),
            vm((SIDE - 1, rows1, half), BF),
            vm((SIDE, 2, rows1 // 8, half), F32),
            vm((2, SIDE - 1, rows1 // 8, half), F32),
            vm((rows1 // 8, half), F32),
            vm((SIDE, orows, width // 2), BF),
            vm((SIDE - 1, orows, width // 2), BF),
            vm((SIDE, 2, orows // 8, width // 2), F32),
            vm((2, SIDE - 1, orows // 8, width // 2), F32),
            vm((orows // 8, width // 2), F32),
            dma((4,)), dma((5,)), dma((2,)), dma((2,)),
            dma((groups,)), dma((groups,)), dma((groups,)), dma((groups,)), dma((groups,)), dma((groups,)),
            dma((pairs,)), dma((pairs,)), dma((SIDE * (pairs + 4),)), dma((SIDE * (pairs + 4),)),
            dma((6 * pairs,)), dma((6 * pairs,)), dma((9 * pairs + 6,)), dma((9 * pairs + 6,)),
            dma((21 * pairs + 14,)), dma((21 * pairs + 14,)),
        ],
        compiler_params=pltpu.CompilerParams(
            collective_id=0, has_side_effects=True, vmem_limit_bytes=VMEM_LIMIT
        ),
    )(
        latents[0, :, 0], norm_gain, cotangent[0, :, 0], kernel, partners[0],
        w_query, w_key, w_value, w_out,
    )
    return leave(*results)


def solution(mesh):
    strips = P("scene", "view", "row", None, None)
    return jax.shard_map(
        shards,
        mesh=mesh,
        in_specs=(
            strips, P(), P(), P(), P(), P(), P(),
            P("scene", "view", None), P("scene", "view"), strips,
        ),
        out_specs=(P(("scene", "view", "row"), None),) * 4,
        check_vma=False,
    )
```
